32 devices in a mesh: pos: 8 (over z, x), tile: 4 (over y, core).
Axes of the slice: x: 2, y: 2, z: 4, core: 2. Of those that a mesh axis runs over, the one named last changes fastest.
Arguments:
- probe_modes: float32 [8, 2, 256, 256], P('tile'), may hold values from -1.1 to 1.1
- object_slices: bfloat16 [2, 2, 512, 2048], P(None, None, 'tile'), may hold values from -6 to 6
- amplitudes: bfloat16 [64, 256, 256], P('pos'), may hold values from 0.5 to 3
- scan_offsets: int32 [64, 2], replicated, may hold values from 0 to 1792, as said below
- slot_counts: int32 [8], replicated, may hold values from 1 to 8, 32 in all
Outputs:
- object_grad: float32 [2, 2, 512, 2048], P(None, None, 'tile', 'pos')
- probe_grad: float32 [8, 2, 256, 256], P('tile', None, 'pos')
The draws below stay inside these ranges and needn't reach their ends.
Inputs may be any that keep to these rules, and one draw needn't show every extreme that they name: slot_counts[g] is how many leading slots of group g are live scan positions; the counts sum to 32 and the largest is exactly 8. scan_offsets[s] is (row, column); the row is at most 256 and the column at most 1792, both reached in every draw.
All inputs are finite; a program needn't handle non-finite values.
Results may differ from the reference program's by a relative error of at most 0.025.
Values may be sent and summed in bfloat16 or wider, within the bound.
No kernel may reach another device: no remote copies, remote signals or barrier semaphores. Data moves between devices by JAX's collectives and lax.ppermute only.
A program may use at most 128 MiB of HBM per device.

```python
import math
import jax
import jax.numpy as jnp
import numpy as np
from jax import lax

SIDE = 256
MODES = 8
LAYERS = 2
ROWS = 512
COLS = 2048
SLOTS = 8
GROUPS = 8
SLOT_ALL = 64
POSITIONS = 32


def draw_scan_offsets(key, part):
    first_key, second_key = jax.random.split(key)
    row_list = jax.random.randint(first_key, (SLOT_ALL,), 0, ROWS - SIDE + 1, dtype=jnp.int32)
    col_list = jax.random.randint(second_key, (SLOT_ALL,), 0, COLS - SIDE + 1, dtype=jnp.int32)
    row_list = row_list.at[1].set(ROWS - SIDE)
    col_list = col_list.at[0].set(COLS - SIDE)
    return jnp.stack([row_list, col_list], axis=1).astype(jnp.int32)


def level_of(key, shape, cuts, smallest, top_value):
    def one(position, blocks):
        draws = jax.random.uniform(jax.random.fold_in(jax.random.fold_in(key, 6), position), (blocks,), jnp.float32, smallest / len(cuts), top_value / len(cuts))
        return jnp.repeat(jnp.exp(draws), shape[position] // blocks).reshape((-1,) + (1,) * (len(shape) - position - 1))

    level = one(*cuts[0])
    for cut in cuts[1:]:
        level = level * one(*cut)
    return level


def length_profile(amount, total, most, lean):
    weights = [(1 << 20) // math.isqrt(standing ** lean) + 1 for standing in range(2, amount + 1)]
    surplus, counts = total - most - (amount - 1), [1] * (amount - 1)
    while surplus > 0:
        free = [i for i in range(amount - 1) if counts[i] < most]
        mass, left = sum([weights[i] for i in free]), surplus
        for i in free:
            more = min(most - counts[i], max(1, left * weights[i] // mass), surplus)
            counts[i] = counts[i] + more
            surplus = surplus - more
    return np.array([most] + counts)


def uneven_parts(stream_key, count, total, most, skew):
    if count == 2:
        one = jax.random.randint(stream_key, (), max(1, total - most), min(most, total - 1) + 1)
        return jnp.stack([one, total - one])
    sizes = jnp.asarray(length_profile(count, total, most, skew), jnp.int32)
    couples = (count - 1) // 2
    giver, taker = sizes[1:1 + 2 * couples:2], sizes[2:2 + 2 * couples:2]
    room = jnp.minimum(giver - 1, most - taker)
    moved = jax.random.randint(jax.random.fold_in(stream_key, 1), (couples,), 0, 1 << 20) % (room + 1)
    sizes = sizes.at[1:1 + 2 * couples:2].set(giver - moved).at[2:2 + 2 * couples:2].set(taker + moved)
    return sizes[jax.random.permutation(jax.random.fold_in(stream_key, 2), count)]


def bell_draw(stream_key, dims, deviation, most, shards=(), kind=jnp.bfloat16):
    values = deviation * jax.random.normal(stream_key, dims, jnp.float32)
    if shards:
        values = values * level_of(stream_key, dims, shards, -0.22, 0.18)
    return jnp.clip(values, -most, most).astype(kind)


def setup_inputs(seed: int = 0) -> dict:
    keys = jax.random.split(jax.random.key(seed), 6)
    return {
        "probe_modes": bell_draw(keys[0], (MODES, 2, SIDE, SIDE), 0.18, 1.1, ((0, 4),), jnp.float32),
        "object_slices": bell_draw(keys[1], (LAYERS, 2, ROWS, COLS), 1.0, 6.0, ((2, 4),)),
        "amplitudes": jnp.clip(0.5 + 2.5 * jax.random.uniform(keys[2], (SLOT_ALL, SIDE, SIDE), jnp.float32) ** level_of(keys[2], (SLOT_ALL, SIDE, SIDE), ((0, 8),), -0.2, 0.2), 0.5, 3.0).astype(jnp.bfloat16),
        "scan_offsets": draw_scan_offsets(jax.random.fold_in(keys[5], 71), 0),
        "slot_counts": uneven_parts(keys[4], GROUPS, POSITIONS, SLOTS, 2).astype(jnp.int32),
    }


FRESNEL = 0.37

def make_tables(points):
    counter = jnp.arange(points, dtype=jnp.int32)
    product = counter[:, None] * counter[None, :] % points
    angle = 2.0 * jnp.pi / points * product.astype(jnp.float32)
    factor = 1.0 / jnp.sqrt(jnp.float32(points))
    table_re = (jnp.cos(angle) * factor).astype(jnp.bfloat16)
    table_im = (-jnp.sin(angle) * factor).astype(jnp.bfloat16)
    shifted = ((counter + points // 2) % points - points // 2).astype(jnp.float32)
    phase = jnp.pi * FRESNEL / points * (shifted[:, None] * shifted[:, None] + shifted[None, :] * shifted[None, :])
    kernel = jnp.stack([jnp.cos(phase), -jnp.sin(phase)])
    return (table_re, table_im, kernel)

def times_complex(first, second):
    real_part = first[..., 0, :, :] * second[..., 0, :, :] - first[..., 1, :, :] * second[..., 1, :, :]
    imag_part = first[..., 0, :, :] * second[..., 1, :, :] + first[..., 1, :, :] * second[..., 0, :, :]
    return jnp.stack([real_part, imag_part], axis=-3)

def conjugate(values):
    return jnp.stack([values[..., 0, :, :], -values[..., 1, :, :]], axis=-3)

def transform_one(values, table_re, table_im):
    points = table_re.shape[0]
    lowered = values.astype(jnp.bfloat16)
    left_side = jnp.concatenate([table_re, table_im], axis=0)
    right_side = jnp.concatenate([lowered[0], lowered[1]], axis=1)
    first = jnp.dot(left_side, right_side, preferred_element_type=jnp.float32)
    mid_re = (first[:points, :points] - first[points:, points:]).astype(jnp.bfloat16)
    mid_im = (first[:points, points:] + first[points:, :points]).astype(jnp.bfloat16)
    second = jnp.dot(jnp.concatenate([mid_re, mid_im], axis=0), jnp.concatenate([table_re, table_im], axis=1), preferred_element_type=jnp.float32)
    out_re = second[:points, :points] - second[points:, points:]
    out_im = second[:points, points:] + second[points:, :points]
    return jnp.stack([out_re, out_im])

def propagate_one(values, table_re, table_im, kernel):
    return transform_one(times_complex(transform_one(values, table_re, table_im), kernel), table_re, -table_im)

def slot_terms(probe_modes, window, amplitude, table_re, table_im, kernel):
    layers = window.shape[0]
    kernel_conj = conjugate(kernel)

    def forward(mode_probe):
        current = times_complex(mode_probe, window[0])
        entering = []
        for layer_at in range(1, layers):
            arrived = propagate_one(current, table_re, table_im, kernel)
            entering.append(arrived)
            current = times_complex(arrived, window[layer_at])
        return (jnp.stack(entering), transform_one(current, table_re, table_im))
    entering, far_field = lax.map(forward, probe_modes)
    power = lax.optimization_barrier(jnp.sum(far_field * far_field, axis=(0, 1)))
    ratio = 1.0 - amplitude / jnp.sqrt(power + 1.0)

    def backward(packed):
        mode_probe, arrived_all, far_one = packed
        incoming = transform_one(ratio * far_one, table_re, -table_im)
        grads = [None] * layers
        for layer_at in range(layers - 1, 0, -1):
            grads[layer_at] = times_complex(conjugate(arrived_all[layer_at - 1]), incoming)
            incoming = propagate_one(times_complex(conjugate(window[layer_at]), incoming), table_re, table_im, kernel_conj)
        grads[0] = times_complex(conjugate(mode_probe), incoming)
        probe_term = times_complex(conjugate(window[0]), incoming)
        return (jnp.stack(grads), probe_term)
    object_terms, probe_terms = lax.map(backward, (probe_modes, entering, far_field))
    return (lax.optimization_barrier(jnp.sum(object_terms, axis=0)), probe_terms)

def window_anchor(place):
    zero_index = jnp.int32(0)
    return (zero_index, zero_index, place[0].astype(jnp.int32), place[1].astype(jnp.int32))

def reference(probe_modes, object_slices, amplitudes, scan_offsets, slot_counts):
    points = probe_modes.shape[-1]
    layers = object_slices.shape[0]
    table_re, table_im, kernel = make_tables(points)
    live = (jnp.arange(SLOTS, dtype=jnp.int32)[None, :] < slot_counts[:, None].astype(jnp.int32)).reshape(-1)
    canvas = jnp.zeros(object_slices.shape, jnp.float32)
    probe_sum = jnp.zeros(probe_modes.shape, jnp.float32)

    def step(carry, packed):
        canvas, probe_sum = carry
        place, amplitude, alive = packed
        anchor = window_anchor(place)
        window = lax.dynamic_slice(object_slices, anchor, (layers, 2, points, points)).astype(jnp.float32)

        def active(unused):
            return slot_terms(probe_modes, window, amplitude, table_re, table_im, kernel)

        def inactive(unused):
            return (jnp.zeros((layers, 2, points, points), jnp.float32), jnp.zeros(probe_modes.shape, jnp.float32))
        object_term, probe_term = lax.cond(alive, active, inactive, 0)
        current = lax.dynamic_slice(canvas, anchor, (layers, 2, points, points))
        canvas = lax.dynamic_update_slice(canvas, current + object_term, anchor)
        return ((canvas, probe_sum + probe_term), None)
    (canvas, probe_sum), unused = lax.scan(step, (canvas, probe_sum), (scan_offsets.astype(jnp.int32), amplitudes.astype(jnp.float32), live))
    return (canvas, probe_sum)
```

```python
import functools

import jax
import jax.numpy as jnp
import ml_dtypes
import numpy as np
from jax import lax
from jax.experimental import pallas as pl
from jax.experimental.pallas import tpu as pltpu
from jax.sharding import PartitionSpec as P

FRESNEL = 0.37
BF16 = jnp.bfloat16
F32 = jnp.float32
VMEM_LIMIT = 56 * 1024 * 1024


def split_tables(points):
    half = points // 2
    counter = np.arange(points)
    angle = (2.0 * np.pi / points * (counter[:, None] * counter[None, :] % points)).astype(np.float32)
    factor = np.float32(1.0) / np.sqrt(np.float32(points))
    table_re = np.cos(angle) * factor
    table_im = -np.sin(angle) * factor

    def stacked(rows):
        re, im = table_re[rows, :half], table_im[rows, :half]
        return np.block([[re, -im], [im, re]]).astype(ml_dtypes.bfloat16)

    even, odd = stacked(slice(0, None, 2)), stacked(slice(1, None, 2))
    tables = np.stack([even, odd, even.T, odd.T])
    order = np.concatenate([counter[0::2], counter[1::2]])
    shifted = ((order + half) % points - half).astype(np.float64)
    phase = np.pi * FRESNEL / points * (shifted[:, None] ** 2 + shifted[None, :] ** 2)
    kernel = np.stack([np.cos(phase), -np.sin(phase)]).astype(np.float32)
    mover = np.zeros((points, points), np.float32)
    mover[counter, order] = 1.0
    mover = np.stack([mover, mover.T]).astype(ml_dtypes.bfloat16)
    return tables, kernel, mover


def dot(a, b):
    return jnp.dot(a, b, preferred_element_type=F32)


def fold_rows(re, im):
    half = re.shape[0] // 2
    top = jnp.concatenate([re[:half], im[:half]], axis=0)
    bottom = jnp.concatenate([re[half:], im[half:]], axis=0)
    return (top + bottom).astype(BF16), (top - bottom).astype(BF16)


def forward_folded(even_in, odd_in, tables):
    half = even_in.shape[0] // 2
    even = dot(tables[0], even_in)
    odd = dot(tables[1], odd_in)
    re = jnp.concatenate([even[:half], odd[:half]], axis=0)
    im = jnp.concatenate([even[half:], odd[half:]], axis=0)
    left = jnp.concatenate([re[:, :half], im[:, :half]], axis=1)
    right = jnp.concatenate([re[:, half:], im[:, half:]], axis=1)
    even = dot((left + right).astype(BF16), tables[2])
    odd = dot((left - right).astype(BF16), tables[3])
    re = jnp.concatenate([even[:, :half], odd[:, :half]], axis=1)
    im = jnp.concatenate([even[:, half:], odd[:, half:]], axis=1)
    return re, im


def inverse(re, im, tables):
    half = re.shape[0] // 2
    low_re, low_im = re.astype(BF16), im.astype(BF16)
    even = dot(tables[2], jnp.concatenate([low_re[:half], low_im[:half]], axis=0))
    odd = dot(tables[3], jnp.concatenate([low_re[half:], low_im[half:]], axis=0))
    total, rest = (even + odd).astype(BF16), (even - odd).astype(BF16)
    re = jnp.concatenate([total[:half], rest[:half]], axis=0)
    im = jnp.concatenate([total[half:], rest[half:]], axis=0)
    even = dot(jnp.concatenate([re[:, :half], im[:, :half]], axis=1), tables[0])
    odd = dot(jnp.concatenate([re[:, half:], im[:, half:]], axis=1), tables[1])
    total, rest = even + odd, even - odd
    re = jnp.concatenate([total[:, :half], rest[:, :half]], axis=1)
    im = jnp.concatenate([total[:, half:], rest[:, half:]], axis=1)
    return re, im


def times(a_re, a_im, b_re, b_im):
    return a_re * b_re - a_im * b_im, a_re * b_im + a_im * b_re


def conj_times(a_re, a_im, b_re, b_im):
    return a_re * b_re + a_im * b_im, a_re * b_im - a_im * b_re


def load_complex(ref, *lead):
    return ref[(*lead, 0)].astype(F32), ref[(*lead, 1)].astype(F32)


VM = pl.BlockSpec(memory_space=pltpu.VMEM)
SM = pl.BlockSpec(memory_space=pltpu.SMEM)
ANY = pl.BlockSpec(memory_space=pl.ANY)


def call(body, inputs, specs, outs, scratch=(), out_specs=None, name=None):
    return pl.pallas_call(
        body,
        out_shape=[jax.ShapeDtypeStruct(shape, dtype) for shape, dtype in outs],
        in_specs=specs,
        out_specs=[VM] * len(outs) if out_specs is None else out_specs,
        scratch_shapes=list(scratch),
        compiler_params=pltpu.CompilerParams(vmem_limit_bytes=VMEM_LIMIT),
        name=name,
    )(*inputs)


def slot_at(plan, tiles, turn):
    place = plan[3, 0] * tiles + (plan[3, 1] ^ turn)
    return plan[1, place], plan[2, place]


def cut_kernel(tiles, points, plan, strip, *outs):
    layers = strip.shape[0]
    blocks = strip.shape[-1] // points
    lane = lax.broadcasted_iota(jnp.int32, (strip.shape[2], points), 1)
    for turn in range(tiles):
        _, col = slot_at(plan, tiles, turn)
        block = col // points
        later = jnp.minimum(block + 1, blocks - 1)
        keep = lane >= col % points
        for layer in range(layers):
            for part in range(2):
                here = strip[layer, part, :, pl.ds(pl.multiple_of(block * points, points), points)]
                there = strip[layer, part, :, pl.ds(pl.multiple_of(later * points, points), points)]
                outs[layer * tiles + turn][part] = jnp.where(
                    keep, here.astype(F32), there.astype(F32)
                ).astype(BF16)


def join_kernel(tiles, points, plan, own, one, two, three, out, whole):
    rows = own.shape[1]
    row, col = slot_at(plan, tiles, 0)
    core, up = plan[3, 1] % 2, plan[3, 1] // 2
    sub = lax.broadcasted_iota(jnp.int32, (rows, points), 0)
    for near, far, at in ((own, two, core), (one, three, 1 - core)):
        low = jnp.where(sub + at * rows >= row, 0, 1)
        for part in range(2):
            whole[part, pl.ds(pl.multiple_of(at * rows, rows), rows)] = jnp.where(
                low == up, near[part].astype(F32), far[part].astype(F32)
            )
    for part in range(2):
        value = pltpu.roll(whole[part], (points - row % points) % points, 0)
        out[part] = pltpu.roll(value, (points - col % points) % points, 1).astype(BF16)


def forward_kernel(probe, first, second, tables, kernel, phi, far, power):
    first_re, first_im = load_complex(first)
    total = None
    for mode in range(probe.shape[0]):
        re, im = times(*load_complex(probe, mode), first_re, first_im)
        re, im = forward_folded(*fold_rows(re, im), tables)
        re, im = inverse(*times(re, im, kernel[0], kernel[1]), tables)
        phi[mode, 0], phi[mode, 1] = re.astype(BF16), im.astype(BF16)
        re, im = times(re, im, *load_complex(second))
        re, im = forward_folded(*fold_rows(re, im), tables)
        far[mode, 0], far[mode, 1] = re.astype(BF16), im.astype(BF16)
        square = re * re + im * im
        total = square if total is None else total + square
    power[...] = total


def put_by_residue(plan, tiles, points, total, own, other):
    row, col = slot_at(plan, tiles, 0)
    core = plan[3, 1] % 2
    rows = points // 2
    for part in range(2):
        total[part] = pltpu.roll(pltpu.roll(total[part], row % points, 0), col % points, 1)
    for out, at in ((own, core), (other, 1 - core)):
        for part in range(2):
            out[part] = total[part, pl.ds(pl.multiple_of(at * rows, rows), rows)].astype(BF16)


def back_kernel(tiles, points, slots, plan, amplitudes, *refs):
    powers, phis, fars = refs[:tiles], refs[tiles : 2 * tiles], refs[2 * tiles : 3 * tiles]
    second, tables, mover, own, other, inner, ratio, total, held, sem = refs[3 * tiles :]
    place = plan[3, 0] * tiles + plan[3, 1]
    copy = pltpu.make_async_copy(amplitudes.at[plan[0, place] // slots], held, sem)
    copy.start()
    copy.wait()
    power = sum(ref[...] for ref in powers)
    amplitude = dot(dot(mover[0], held[...]).astype(BF16), mover[1])
    ratio[...] = 1.0 - amplitude / jnp.sqrt(power + 1.0)
    total[...] = jnp.zeros_like(total)
    modes = phis[0].shape[0]
    for turn in range(tiles):

        def one_mode(mode, unused, turn=turn):
            re, im = load_complex(fars[turn], mode)
            re, im = inverse(re * ratio[...], im * ratio[...], tables)
            grad_re, grad_im = conj_times(*load_complex(phis[turn], mode), re, im)
            total[0] += grad_re
            total[1] += grad_im
            even, odd = fold_rows(*conj_times(*load_complex(second), re, im))
            inner[turn * modes + mode, 0] = even
            inner[turn * modes + mode, 1] = odd
            return unused

        lax.fori_loop(0, modes, one_mode, 0)
    put_by_residue(plan, tiles, points, total, own, other)


def last_kernel(tiles, points, plan, inner, *refs):
    probes = refs[:tiles]
    first, tables, kernel, own, other = refs[tiles : tiles + 5]
    grads, total = refs[tiles + 5 : 2 * tiles + 5], refs[2 * tiles + 5]
    total[...] = jnp.zeros_like(total)
    modes = probes[0].shape[0]
    for turn in range(tiles):

        def one_mode(mode, unused, turn=turn):
            at = turn * modes + mode
            re, im = forward_folded(inner[at, 0], inner[at, 1], tables)
            re, im = inverse(*conj_times(kernel[0], kernel[1], re, im), tables)
            grad_re, grad_im = conj_times(*load_complex(probes[turn], mode), re, im)
            total[0] += grad_re
            total[1] += grad_im
            re, im = conj_times(*load_complex(first), re, im)
            grads[turn][mode, 0], grads[turn][mode, 1] = re.astype(BF16), im.astype(BF16)
            return unused

        lax.fori_loop(0, modes, one_mode, 0)
    put_by_residue(plan, tiles, points, total, own, other)


def place_kernel(tiles, points, plan, *refs):
    pieces, (below, same, above, canvas) = refs[:tiles], refs[tiles:]
    rows = pieces[0].shape[1]
    core, up = plan[3, 1] % 2, plan[3, 1] // 2
    base = plan[3, 0] // 2 * 2 - 2
    sub = lax.broadcasted_iota(jnp.int32, (rows, points), 0) + core * rows
    lane = lax.broadcasted_iota(jnp.int32, (rows, points), 1)
    canvas[...] = jnp.zeros_like(canvas)
    for turn in range(tiles):
        row, col = slot_at(plan, tiles, turn)
        mine = jnp.where(sub >= row, 0, 1) == up
        early = lane >= col % points
        for part in range(2):
            value = jnp.where(mine, pieces[turn][part].astype(F32), 0.0)
            for step, keep in ((0, early), (1, ~early)):
                at = col // points + step - base
                at = jnp.where((at >= 0) & (at < 6), at, 6)
                canvas[at, part] += jnp.where(keep, value, 0.0)
    below[...] = canvas[0:2].astype(BF16)
    same[...] = canvas[2:4]
    above[...] = canvas[4:6].astype(BF16)


def split_kernel(plan, *refs):
    (same, low, high, keep, send) = refs
    x_at = plan[3, 0] % 2
    keep[...] = same[x_at] + low[x_at].astype(F32) + high[x_at].astype(F32)
    send[...] = (same[1 - x_at] + low[1 - x_at].astype(F32) + high[1 - x_at].astype(F32)).astype(BF16)


def end_kernel(*refs):
    layers = (len(refs) - 2) // 2
    extra, out = refs[-2:]
    for layer in range(layers):
        out[layer] = refs[layer][...] + refs[layers + layer][...].astype(F32) + extra[layer]


def pick_kernel(tiles, slots, plan, amplitudes, out, sem):
    groups = out.shape[0]
    me, tile = plan[3, 0], plan[3, 1]
    for group in range(groups):
        slot = plan[0, group * tiles + tile]

        @pl.when(slot // slots == me)
        def _(group=group, slot=slot):
            pltpu.make_async_copy(amplitudes.at[slot % slots], out.at[group], sem).start()

    for group in range(groups):
        slot = plan[0, group * tiles + tile]

        @pl.when(slot // slots == me)
        def _(group=group, slot=slot):
            pltpu.make_async_copy(amplitudes.at[slot % slots], out.at[group], sem).wait()


def make_plan(scan_offsets, slot_counts, slots, points, tiles):
    all_slots = scan_offsets.shape[0]
    groups = slot_counts.shape[0]
    places = groups * slots // 2
    live = (jnp.arange(slots, dtype=jnp.int32)[None, :] < slot_counts[:, None]).reshape(-1)
    counter = jnp.arange(all_slots, dtype=jnp.int32)
    key = jnp.where(live, scan_offsets[:, 1], 1 << 20) * all_slots + counter
    rank = jnp.sum((key[None, :] < key[:, None]).astype(jnp.int32), axis=1)
    here = rank[None, :] == jnp.arange(places, dtype=jnp.int32)[:, None]
    table = jnp.stack([counter, scan_offsets[:, 0], scan_offsets[:, 1]])
    chosen = jnp.sum(jnp.where(here[None], table[:, None, :], 0), axis=2)
    z_at = jnp.arange(places, dtype=jnp.int32) // (2 * tiles)
    first, last = chosen[2] // (2 * points), (chosen[2] + points - 1) // (2 * points)
    distant = jnp.any((first < z_at - 1) | (last > z_at + 1))
    ids = jnp.zeros((1, places), jnp.int32)
    ids = ids.at[0, 0].set(lax.axis_index("pos")).at[0, 1].set(lax.axis_index("tile"))
    return jnp.concatenate([chosen, ids]), distant


def turned(value, turn, tiles):
    return lax.ppermute(value, "tile", [(i, i ^ turn) for i in range(tiles)])


def distant_blocks(plan, pieces, tiles, points, groups):
    rows = pieces[0][0].shape[1]
    pos, tile = plan[3, 0], plan[3, 1]
    sub = (jnp.arange(rows, dtype=jnp.int32) + tile % 2 * rows)[:, None]
    lane = jnp.arange(points, dtype=jnp.int32)[None, :]
    block = jnp.arange(groups, dtype=jnp.int32)
    outside = jnp.abs(block // 2 - pos // 2) > 1
    canvas = 0.0
    for turn in range(tiles):
        place = pos * tiles + (tile ^ turn)
        row, col = jnp.take(plan[1], place), jnp.take(plan[2], place)
        mine = jnp.where(sub >= row, 0, 1) == tile // 2
        target = col // points + jnp.where(lane >= col % points, 0, 1)
        keep = outside[:, None, None] & mine[None] & (target[None] == block[:, None, None])
        value = jnp.stack([layer[turn] for layer in pieces]).astype(F32)
        canvas = canvas + jnp.where(keep[:, None, None], value[None], 0.0)
    return lax.psum_scatter(canvas.astype(BF16), "pos", scatter_dimension=0, tiled=True)[0].astype(F32)


def on_device_by_slot(probe_modes, object_slices, amplitudes, scan_offsets, slot_counts):
    groups, tiles = lax.axis_size("pos"), lax.axis_size("tile")
    slots, points = amplitudes.shape[0], amplitudes.shape[-1]
    layers, rows = object_slices.shape[0], object_slices.shape[2]
    modes = probe_modes.shape[0]
    tables, kernel, mover = (jnp.asarray(t) for t in split_tables(points))
    plan, distant = make_plan(scan_offsets, slot_counts, slots, points, tiles)
    field = (2, points, points)

    cut = call(
        functools.partial(cut_kernel, tiles, points),
        (plan, object_slices),
        [SM, VM],
        [((2, rows, points), BF16)] * (layers * tiles),
        name="cut",
    )
    strips = [
        [cut[layer * tiles]] + [turned(cut[layer * tiles + turn], turn, tiles) for turn in range(1, tiles)]
        for layer in range(layers)
    ]
    low = probe_modes.astype(BF16)
    across = turned(low, 2, tiles)
    probes = [probe_modes, turned(low, 1, tiles), across, turned(across, 1, tiles)]
    (outgoing,) = call(
        functools.partial(pick_kernel, tiles, slots),
        (plan, amplitudes),
        [SM, ANY],
        [((groups, points, points), BF16)],
        [pltpu.SemaphoreType.DMA],
        out_specs=[ANY],
        name="pick",
    )
    arrived = lax.all_to_all(outgoing, "pos", split_axis=0, concat_axis=0, tiled=True)

    windows = [
        call(
            functools.partial(join_kernel, tiles, points),
            (plan, *strips[layer]),
            [SM] + [VM] * tiles,
            [(field, BF16)],
            [pltpu.VMEM(field, F32)],
            name="join",
        )[0]
        for layer in range(layers)
    ]
    phis, fars, powers = [], [], []
    for probe in probes:
        phi, far, power = call(
            forward_kernel,
            (probe, windows[0], windows[1], tables, kernel),
            [VM] * 5,
            [((modes, *field), BF16), ((modes, *field), BF16), ((points, points), F32)],
            name="forward",
        )
        phis.append(phi)
        fars.append(far)
        powers.append(power)

    half = ((2, points // 2, points), BF16)
    own, other, inner = call(
        functools.partial(back_kernel, tiles, points, slots),
        (plan, arrived, *powers, *phis, *fars, windows[1], tables, mover),
        [SM, ANY] + [VM] * (3 * tiles + 3),
        [half, half, ((tiles * modes, 2, points, points), BF16)],
        [
            pltpu.VMEM((points, points), F32),
            pltpu.VMEM(field, F32),
            pltpu.VMEM((points, points), BF16),
            pltpu.SemaphoreType.DMA,
        ],
        name="back",
    )
    pieces = [None] * layers
    pieces[1] = [own] + [turned(v, turn, tiles) for turn, v in ((1, other), (2, own), (3, other))]
    own, other, *grads = call(
        functools.partial(last_kernel, tiles, points),
        (plan, inner, *probes, windows[0], tables, kernel),
        [SM] + [VM] * (tiles + 4),
        [half, half] + [((modes, *field), BF16)] * tiles,
        [pltpu.VMEM(field, F32)],
        name="last",
    )
    pieces[0] = [own] + [turned(v, turn, tiles) for turn, v in ((1, other), (2, own), (3, other))]

    block = (2, rows, points)
    kept, swapped = [None] * layers, [None] * layers
    for layer in reversed(range(layers)):
        below, same, above = call(
            functools.partial(place_kernel, tiles, points),
            (plan, *pieces[layer]),
            [SM] + [VM] * tiles,
            [((2, *block), BF16), ((2, *block), F32), ((2, *block), BF16)],
            [pltpu.VMEM((7, *block), F32)],
            name="place",
        )
        low_in = lax.ppermute(above, "pos", [(i, i + 2) for i in range(groups - 2)])
        high_in = lax.ppermute(below, "pos", [(i + 2, i) for i in range(groups - 2)])
        kept[layer], send = call(
            split_kernel,
            (plan, same, low_in, high_in),
            [SM] + [VM] * 3,
            [(block, F32), (block, BF16)],
            name="split",
        )
        swapped[layer] = lax.ppermute(send, "pos", [(i, i ^ 1) for i in range(groups)])
    extra = lax.cond(
        distant,
        lambda p: distant_blocks(plan, p, tiles, points, groups),
        lambda p: jnp.zeros((layers, *block), F32),
        pieces,
    )
    (object_grad,) = call(
        end_kernel, (*kept, *swapped, extra), [VM] * (2 * layers + 1), [((layers, *block), F32)], name="end"
    )

    total = grads[0].astype(F32) + turned(grads[1], 1, tiles).astype(F32)
    beyond = grads[2].astype(F32) + turned(grads[3], 1, tiles).astype(F32)
    total = total + turned(beyond.astype(BF16), 2, tiles).astype(F32)
    split = total.astype(BF16).reshape(modes, 2, groups, points // groups, points).transpose(2, 0, 1, 3, 4)
    gathered = lax.all_to_all(split, "pos", split_axis=0, concat_axis=0, tiled=True)
    probe_grad = jnp.sum(gathered.astype(F32), axis=0)
    return object_grad, probe_grad


def make_tables(points):
    counter = jnp.arange(points, dtype=jnp.int32)
    product = counter[:, None] * counter[None, :] % points
    angle = 2.0 * jnp.pi / points * product.astype(jnp.float32)
    factor = 1.0 / jnp.sqrt(jnp.float32(points))
    table_re = (jnp.cos(angle) * factor).astype(jnp.bfloat16)
    table_im = (-jnp.sin(angle) * factor).astype(jnp.bfloat16)
    shifted = ((counter + points // 2) % points - points // 2).astype(jnp.float32)
    phase = (
        jnp.pi
        * FRESNEL
        / points
        * (shifted[:, None] * shifted[:, None] + shifted[None, :] * shifted[None, :])
    )
    kernel = jnp.stack([jnp.cos(phase), -jnp.sin(phase)])
    return (table_re, table_im, kernel)


def times_complex(first, second):
    real_part = (
        first[..., 0, :, :] * second[..., 0, :, :] - first[..., 1, :, :] * second[..., 1, :, :]
    )
    imag_part = (
        first[..., 0, :, :] * second[..., 1, :, :] + first[..., 1, :, :] * second[..., 0, :, :]
    )
    return jnp.stack([real_part, imag_part], axis=-3)


def conjugate(values):
    return jnp.stack([values[..., 0, :, :], -values[..., 1, :, :]], axis=-3)


def transform_many(values, table_re, table_im):
    tables = jnp.stack([table_re, table_im])
    lowered = values.astype(jnp.bfloat16)
    first = jnp.einsum("gab,nmtbc->nmgtac", tables, lowered, preferred_element_type=jnp.float32)
    middle = jnp.stack(
        [first[:, :, 0, 0] - first[:, :, 1, 1], first[:, :, 0, 1] + first[:, :, 1, 0]], axis=2
    ).astype(jnp.bfloat16)
    second = jnp.einsum("nmtab,gbc->nmtgac", middle, tables, preferred_element_type=jnp.float32)
    return jnp.stack(
        [second[:, :, 0, 0] - second[:, :, 1, 1], second[:, :, 0, 1] + second[:, :, 1, 0]], axis=2
    )


def propagate_many(values, table_re, table_im, kernel):
    return transform_many(
        times_complex(transform_many(values, table_re, table_im), kernel), table_re, -table_im
    )


def window_anchor(place):
    zero_index = jnp.int32(0)
    return (zero_index, zero_index, place[0], place[1])


def on_device_by_mode(probe_modes, object_slices, amplitudes, scan_offsets, slot_counts):
    group = lax.axis_index("pos")
    groups = lax.axis_size("pos")
    tile_at = lax.axis_index("tile")
    strips = lax.axis_size("tile")
    slots = amplitudes.shape[0]
    points = amplitudes.shape[-1]
    layers = object_slices.shape[0]
    strip_rows = object_slices.shape[2]
    starts = jnp.cumsum(slot_counts) - slot_counts
    share = slots // 2
    wanted = jnp.arange(groups * share, dtype=jnp.int32)
    within = wanted - starts[group]
    usable = (within >= 0) & (within < slot_counts[group])
    picked = jnp.take(amplitudes, jnp.clip(within, 0, slots - 1), axis=0)
    outgoing = jnp.where(usable[:, None, None], picked, jnp.zeros_like(picked))
    arrived_rows = lax.all_to_all(outgoing, "pos", split_axis=0, concat_axis=0, tiled=True)
    mine = group * share + jnp.arange(share, dtype=jnp.int32)
    source = jnp.sum((starts[None, :] <= mine[:, None]).astype(jnp.int32), axis=1) - 1
    amplitude = jnp.take(arrived_rows, source * share + jnp.arange(share, dtype=jnp.int32), axis=0)
    places = jnp.take(scan_offsets, source * slots + mine - starts[source], axis=0)
    alive = jnp.ones((share,), jnp.float32)
    padded = jnp.pad(object_slices, ((0, 0), (0, 0), (points, points), (0, 0)))

    def cut_piece(place):
        local_row = jnp.clip(place[0] - tile_at * strip_rows + points, 0, strip_rows + points)
        shifted_place = jnp.stack([local_row, place[1]])
        return lax.dynamic_slice(padded, window_anchor(shifted_place), (layers, 2, points, points))

    pieces = jax.vmap(cut_piece)(places).astype(jnp.float32)
    windows = lax.psum(pieces.astype(jnp.bfloat16), "tile").astype(jnp.float32)
    table_re, table_im, kernel = make_tables(points)
    kernel_conj = conjugate(kernel)
    current = times_complex(probe_modes[None], windows[:, None, 0])
    layer_at = 1
    arrived = propagate_many(current, table_re, table_im, kernel)
    entering = [arrived]
    current = times_complex(arrived, windows[:, None, layer_at])
    far_field = transform_many(current, table_re, table_im)
    partial_power = jnp.sum(far_field * far_field, axis=(1, 2))
    power = lax.psum(partial_power.astype(jnp.bfloat16), "tile").astype(jnp.float32)
    ratio = (1.0 - amplitude.astype(jnp.float32) / jnp.sqrt(power + 1.0)) * alive[:, None, None]
    incoming = transform_many(ratio[:, None, None] * far_field, table_re, -table_im)
    object_terms = [None] * layers
    layer_at = 1
    object_terms[layer_at] = jnp.sum(
        times_complex(conjugate(entering[layer_at - 1]), incoming), axis=1
    )
    incoming = propagate_many(
        times_complex(conjugate(windows[:, None, layer_at]), incoming),
        table_re,
        table_im,
        kernel_conj,
    )
    object_terms[0] = jnp.sum(times_complex(conjugate(probe_modes[None]), incoming), axis=1)
    probe_term = jnp.sum(times_complex(conjugate(windows[:, None, 0]), incoming), axis=0)
    slot_grads = jnp.stack(object_terms, axis=1)
    canvas = jnp.zeros((layers, 2, strip_rows * strips, object_slices.shape[3]), jnp.float32)

    def deposit(canvas, packed):
        place, term = packed
        anchor = window_anchor(place)
        current_part = lax.dynamic_slice(canvas, anchor, term.shape)
        return (lax.dynamic_update_slice(canvas, current_part + term, anchor), None)

    canvas, unused = lax.scan(deposit, canvas, (places, slot_grads))
    column_part = lax.psum_scatter(
        canvas.astype(jnp.bfloat16), "pos", scatter_dimension=3, tiled=True
    )
    object_grad = lax.psum_scatter(column_part, "tile", scatter_dimension=2, tiled=True).astype(
        jnp.float32
    )
    probe_grad = lax.psum_scatter(
        probe_term.astype(jnp.bfloat16), "pos", scatter_dimension=2, tiled=True
    ).astype(jnp.float32)
    return (object_grad, probe_grad)


def solution(mesh):
    in_specs = (
        P("tile", None, None, None),
        P(None, None, "tile", None),
        P("pos", None, None),
        P(),
        P(),
    )
    out_specs = (P(None, None, "tile", "pos"), P("tile", None, "pos", None))
    by_slot = mesh.shape["tile"] == 4 and mesh.shape["pos"] == 8
    return jax.shard_map(
        on_device_by_slot if by_slot else on_device_by_mode,
        mesh=mesh,
        in_specs=in_specs,
        out_specs=out_specs,
        check_vma=False,
    )
```

```python
import functools

import jax
import jax.numpy as jnp
import ml_dtypes
import numpy as np
from jax import lax
from jax.experimental import pallas as pl
from jax.experimental.pallas import tpu as pltpu
from jax.sharding import PartitionSpec as P

FRESNEL = 0.37
BF16 = jnp.bfloat16
F32 = jnp.float32


def split_tables(points):
    half = points // 2
    counter = np.arange(points)
    angle = (2.0 * np.pi / points * (counter[:, None] * counter[None, :] % points)).astype(np.float32)
    factor = np.float32(1.0) / np.sqrt(np.float32(points))
    table_re = np.cos(angle) * factor
    table_im = -np.sin(angle) * factor

    def stacked(rows):
        re, im = table_re[rows, :half], table_im[rows, :half]
        return np.block([[re, -im], [im, re]]).astype(ml_dtypes.bfloat16)

    even, odd = stacked(slice(0, None, 2)), stacked(slice(1, None, 2))
    tables = np.stack([even, odd, even.T, odd.T])
    order = np.concatenate([counter[0::2], counter[1::2]])
    shifted = ((order + half) % points - half).astype(np.float64)
    phase = np.pi * FRESNEL / points * (shifted[:, None] ** 2 + shifted[None, :] ** 2)
    kernel = np.stack([np.cos(phase), -np.sin(phase)]).astype(np.float32)
    mover = np.zeros((points, points), np.float32)
    mover[counter, order] = 1.0
    mover = np.stack([mover, mover.T]).astype(ml_dtypes.bfloat16)
    return tables, kernel, mover


def dot(a, b):
    return jnp.dot(a, b, preferred_element_type=F32)


def fold_rows(re, im):
    half = re.shape[0] // 2
    top = jnp.concatenate([re[:half], im[:half]], axis=0)
    bottom = jnp.concatenate([re[half:], im[half:]], axis=0)
    return (top + bottom).astype(BF16), (top - bottom).astype(BF16)


def join_parts(values, axis):
    return jnp.concatenate(values, axis=axis)


def forward_folded(folded, tables):
    half = folded[0][0].shape[0] // 2
    evens = [dot(tables[0], even) for even, _ in folded]
    odds = [dot(tables[1], odd) for _, odd in folded]
    lanes = []
    for even, odd in zip(evens, odds):
        re = join_parts([even[:half], odd[:half]], 0)
        im = join_parts([even[half:], odd[half:]], 0)
        left = join_parts([re[:, :half], im[:, :half]], 1)
        right = join_parts([re[:, half:], im[:, half:]], 1)
        lanes.append(((left + right).astype(BF16), (left - right).astype(BF16)))
    evens = [dot(even, tables[2]) for even, _ in lanes]
    odds = [dot(odd, tables[3]) for _, odd in lanes]
    return [
        (join_parts([even[:, :half], odd[:, :half]], 1), join_parts([even[:, half:], odd[:, half:]], 1))
        for even, odd in zip(evens, odds)
    ]


def inverse(fields, tables):
    half = fields[0][0].shape[0] // 2
    low = [(re.astype(BF16), im.astype(BF16)) for re, im in fields]
    evens = [dot(tables[2], join_parts([re[:half], im[:half]], 0)) for re, im in low]
    odds = [dot(tables[3], join_parts([re[half:], im[half:]], 0)) for re, im in low]
    lanes = []
    for even, odd in zip(evens, odds):
        total, rest = (even + odd).astype(BF16), (even - odd).astype(BF16)
        re = join_parts([total[:half], rest[:half]], 0)
        im = join_parts([total[half:], rest[half:]], 0)
        lanes.append((join_parts([re[:, :half], im[:, :half]], 1), join_parts([re[:, half:], im[:, half:]], 1)))
    evens = [dot(even, tables[0]) for even, _ in lanes]
    odds = [dot(odd, tables[1]) for _, odd in lanes]
    out = []
    for even, odd in zip(evens, odds):
        total, rest = even + odd, even - odd
        re = join_parts([total[:, :half], rest[:, :half]], 1)
        im = join_parts([total[:, half:], rest[:, half:]], 1)
        out.append((re, im))
    return out


def times(a_re, a_im, b_re, b_im):
    return a_re * b_re - a_im * b_im, a_re * b_im + a_im * b_re


def conj_times(a_re, a_im, b_re, b_im):
    return a_re * b_re + a_im * b_im, a_re * b_im - a_im * b_re


def load_complex(ref, *lead):
    return ref[(*lead, 0)].astype(F32), ref[(*lead, 1)].astype(F32)


VM = pl.BlockSpec(memory_space=pltpu.VMEM)
SM = pl.BlockSpec(memory_space=pltpu.SMEM)
HB = pl.BlockSpec(memory_space=pltpu.HBM)
VK = object()


def call(body, inputs, specs, outs, scratch=(), out_specs=None, name=None, us=0.1, mib=8, keep=()):
    return pl.pallas_call(
        body,
        out_shape=[
            pltpu.VMEM(shape, dtype) if at in keep else jax.ShapeDtypeStruct(shape, dtype)
            for at, (shape, dtype) in enumerate(outs)
        ],
        in_specs=[VM if spec is VK else spec for spec in specs],
        out_specs=[VM] * len(outs) if out_specs is None else out_specs,
        scratch_shapes=list(scratch),
        compiler_params=pltpu.CompilerParams(vmem_limit_bytes=mib * 1024 * 1024),
        cost_estimate=pl.CostEstimate(flops=int(us * 1e9), bytes_accessed=int(us * 3e6), transcendentals=0),
        name=name,
    )(
        *(
            pltpu.with_memory_space_constraint(value, pltpu.VMEM) if spec is VK else value
            for value, spec in zip(inputs, specs)
        )
    )


def fetch(sources, targets, sems):
    copies = [pltpu.make_async_copy(s, t, sems.at[at]) for at, (s, t) in enumerate(zip(sources, targets))]
    for copy in copies:
        copy.start()
    return copies


def slot_at(plan, tiles, turn):
    place = plan[3, 0] * tiles + (plan[3, 1] ^ turn)
    return plan[1, place], plan[2, place]


def first_kernel(groups, tiles, points, counts, offsets, strip_far, amplitudes_far, *refs):
    strips = refs[:tiles]
    same, remote, nearby, plan_out, plan, strip, amplitudes, sems = refs[tiles:]
    layers, rows = strip.shape[0], strip.shape[2]
    slots = amplitudes.shape[0]
    n = offsets.shape[0]
    strip_copy = pltpu.make_async_copy(strip_far, strip, sems.at[1])
    strip_copy.start()
    amplitude_copy = pltpu.make_async_copy(amplitudes_far, amplitudes, sems.at[2])
    amplitude_copy.start()
    pos, tile = lax.axis_index("pos"), lax.axis_index("tile")
    width = plan_out.shape[1]

    number = lax.broadcasted_iota(jnp.int32, (n, 1), 0)
    live = jnp.zeros((n, 1), jnp.int32)
    for group in range(groups):
        live += jnp.where((number >= group * slots) & (number < group * slots + counts[group]), 1, 0)
    row, col = offsets[:, 0:1].astype(F32), offsets[:, 1:2].astype(F32)
    number = number.astype(F32)
    key = jnp.where(live > 0, col, float(1 << 12)) * n + number
    square = (n, n)
    eye = lax.broadcasted_iota(jnp.int32, square, 0) == lax.broadcasted_iota(jnp.int32, square, 1)
    across = jnp.sum(jnp.where(eye, key, 0.0), axis=0, keepdims=True)
    rank = jnp.sum(jnp.where(across < key, 1.0, 0.0), axis=1, keepdims=True).astype(jnp.int32)
    here = lax.broadcasted_iota(jnp.int32, (n, width), 1) == rank
    chosen = [
        jnp.sum(jnp.where(here, value, 0.0), axis=0, keepdims=True).astype(jnp.int32)
        for value in (number, row, col)
    ]
    lane = lax.broadcasted_iota(jnp.int32, (1, width), 1)
    outer = 2 * points
    lowest = jnp.maximum(sum(jnp.where(lane >= i * 2 * tiles, 1, 0) for i in range(1, groups // 2)) - 1, 0)
    far = (chosen[2] < lowest * outer) | (chosen[2] + points > (lowest + jnp.where(lane < 2 * tiles, 2, 3)) * outer)
    distant = jnp.max(jnp.where(far & (lane < groups * slots // 2), 1.0, 0.0), axis=1, keepdims=True)
    for at, value in enumerate(chosen):
        plan_out[at : at + 1, :] = value
    plan_out[3:4, :] = jnp.where(
        lane == 0, pos, jnp.where(lane == 1, tile, jnp.where(lane == 2, distant.astype(jnp.int32), 0))
    )
    plan_out[4:8, :] = jnp.zeros((4, width), jnp.int32)
    copy = pltpu.make_async_copy(plan_out, plan, sems.at[0])
    copy.start()
    copy.wait()
    strip_copy.wait()

    blocks = strip.shape[-1] // points
    lane = lax.broadcasted_iota(jnp.int32, (rows, points), 1)
    for turn in range(tiles):
        _, col = slot_at(plan, tiles, turn)
        block = col // points
        later = jnp.minimum(block + 1, blocks - 1)
        keep = lane >= col % points
        for layer in range(layers):
            for part in range(2):
                here = strip[layer, part, :, pl.ds(pl.multiple_of(block * points, points), points)]
                there = strip[layer, part, :, pl.ds(pl.multiple_of(later * points, points), points)]
                strips[turn][layer, part] = jnp.where(
                    keep, here.astype(F32), there.astype(F32)
                ).astype(BF16)
    amplitude_copy.wait()
    for turn in range(groups // 2):
        across_x = (nearby, remote)[turn // 2]
        for flip, out, at in ((0, same, turn), (1, across_x, turn % 2)):
            slot = plan[0, (pos ^ (2 * turn + flip)) * tiles + tile]

            @pl.when(slot // slots == pos)
            def _(out=out, at=at, slot=slot):
                out[at] = amplitudes[slot % slots]


def merge_kernel(tiles, slots, turns, plan, same, came, *outs):
    pos, tile = plan[3, 0], plan[3, 1]
    for at, (turn, out) in enumerate(zip(turns, outs)):
        source = plan[0, (pos ^ (2 * turn)) * tiles + tile] // slots

        @pl.when(source == pos)
        def _(turn=turn, out=out):
            out[...] = same[turn]

        @pl.when(source == (pos ^ 1))
        def _(at=at, out=out):
            out[...] = came[at]


def join(tiles, points, plan, strips, layer, whole, out):
    own, one, two, three = strips
    rows = own.shape[2]
    row, col = slot_at(plan, tiles, 0)
    core, up = plan[3, 1] % 2, plan[3, 1] // 2
    sub = lax.broadcasted_iota(jnp.int32, (rows, points), 0)
    for near, far, at in ((own, two, core), (one, three, 1 - core)):
        low = jnp.where(sub + at * rows >= row, 0, 1)
        for part in range(2):
            whole[part, pl.ds(pl.multiple_of(at * rows, rows), rows)] = jnp.where(
                low == up, near[layer, part].astype(F32), far[layer, part].astype(F32)
            )
    for part in range(2):
        value = pltpu.roll(whole[part], (points - row % points) % points, 0)
        out[part] = pltpu.roll(value, (points - col % points) % points, 1).astype(BF16)


def forward(probes, first, second, tables, kernel, phi, far):
    modes = probes[0].shape[0]
    fields = []
    for probe in probes:
        for mode in range(modes):
            fields.append(fold_rows(*times(*load_complex(probe, mode), *load_complex(first))))
    fields = forward_folded(fields, tables)
    fields = inverse([times(re, im, kernel[0], kernel[1]) for re, im in fields], tables)
    folded = []
    for at, (re, im) in enumerate(fields):
        phi[at, 0], phi[at, 1] = re.astype(BF16), im.astype(BF16)
        folded.append(fold_rows(*times(re, im, *load_complex(second))))
    fields = forward_folded(folded, tables)
    power = None
    for at, (re, im) in enumerate(fields):
        far[at, 0], far[at, 1] = re.astype(BF16), im.astype(BF16)
        square = re * re + im * im
        power = square if power is None else power + square
    return power


def put_by_residue(plan, tiles, points, total, own, other):
    row, col = slot_at(plan, tiles, 0)
    core = plan[3, 1] % 2
    rows = points // 2
    for part in range(2):
        total[part] = pltpu.roll(pltpu.roll(total[part], row % points, 0), col % points, 1)
    for out, at in ((own, core), (other, 1 - core)):
        for part in range(2):
            out[part] = total[part, pl.ds(pl.multiple_of(at * rows, rows), rows)].astype(BF16)


def ahead_kernel(tiles, points, plan, *refs):
    strips, near, beside, across, diagonal, tables_far, kernel_far = refs[:4], *refs[4:10]
    first, second, phi, far, power = refs[10:15]
    mine, tables, kernel, whole, sems = refs[15:]
    copies = fetch((near, tables_far, kernel_far), (mine, tables, kernel), sems)
    join(tiles, points, plan, strips, 0, whole, first)
    join(tiles, points, plan, strips, 1, whole, second)
    for copy in copies:
        copy.wait()
    size = phi.shape[0] // 2
    power[...] = forward((mine, beside), first, second, tables, kernel, phi.at[:size], far.at[:size])
    power[...] += forward((across, diagonal), first, second, tables, kernel, phi.at[size:], far.at[size:])


def back_kernel(tiles, points, slots, plan, *refs):
    power, phi, far, second, tables_far, mover_far = refs[:6]
    arrived = refs[6:10]
    own, other, inner = refs[10:13]
    tables, mover, amplitude, total, ratio, sems = refs[13:]
    copies = fetch((mover_far, tables_far), (mover, tables), sems)
    source = plan[0, plan[3, 0] * tiles + plan[3, 1]] // slots
    for turn, ref in enumerate(arrived):

        @pl.when(((source ^ plan[3, 0]) >> 1) == turn)
        def _(ref=ref):
            amplitude[...] = ref[...]

    for copy in copies:
        copy.wait()
    measured = dot(dot(mover[0], amplitude[...]).astype(BF16), mover[1])
    ratio[...] = 1.0 - measured / jnp.sqrt(power[...] + 1.0)
    total[...] = jnp.zeros_like(total)
    size = phi.shape[0] // 2
    for start in (0, size):
        fields = []
        for at in range(start, start + size):
            re, im = load_complex(far, at)
            fields.append((re * ratio[...], im * ratio[...]))
        fields = inverse(fields, tables)
        for at, (re, im) in enumerate(fields, start):
            grad_re, grad_im = conj_times(*load_complex(phi, at), re, im)
            total[0] += grad_re
            total[1] += grad_im
            inner[at, 0], inner[at, 1] = fold_rows(*conj_times(*load_complex(second), re, im))
    put_by_residue(plan, tiles, points, total, own, other)


def last_kernel(tiles, points, plan, *refs):
    inner, near, beside, across, diagonal, first, tables_far, kernel_far = refs[:8]
    own, other, near_grad, beyond_grad, beside_grad = refs[8:13]
    mine, tables, kernel, total, sems = refs[13:]
    copies = fetch((tables_far, kernel_far, near), (tables, kernel, mine), sems)
    modes = mine.shape[0]
    probes = (mine, beside, across, diagonal)
    grads = (near_grad, beside_grad.at[0], beyond_grad, beside_grad.at[1])
    total[...] = jnp.zeros_like(total)
    for copy in copies:
        copy.wait()
    for start in range(0, tiles, 2):
        which = [(turn, mode) for turn in range(start, start + 2) for mode in range(modes)]
        fields = forward_folded([(inner[t * modes + m, 0], inner[t * modes + m, 1]) for t, m in which], tables)
        fields = inverse([conj_times(kernel[0], kernel[1], re, im) for re, im in fields], tables)
        for (turn, mode), (re, im) in zip(which, fields):
            grad_re, grad_im = conj_times(*load_complex(probes[turn], mode), re, im)
            total[0] += grad_re
            total[1] += grad_im
            re, im = conj_times(*load_complex(first), re, im)
            grads[turn][mode, 0], grads[turn][mode, 1] = re.astype(BF16), im.astype(BF16)
    put_by_residue(plan, tiles, points, total, own, other)


def place_kernel(tiles, points, plan, *refs):
    pieces, (below, same, above, canvas) = refs[:tiles], refs[tiles:]
    rows = pieces[0].shape[1]
    core, up = plan[3, 1] % 2, plan[3, 1] // 2
    base = plan[3, 0] // 2 * 2 - 2
    sub = lax.broadcasted_iota(jnp.int32, (rows, points), 0) + core * rows
    lane = lax.broadcasted_iota(jnp.int32, (rows, points), 1)
    canvas[...] = jnp.zeros_like(canvas)
    for turn in range(tiles):
        row, col = slot_at(plan, tiles, turn)
        mine = jnp.where(sub >= row, 0, 1) == up
        early = lane >= col % points
        for part in range(2):
            value = jnp.where(mine, pieces[turn][part].astype(F32), 0.0)
            for step, keep in ((0, early), (1, ~early)):
                at = col // points + step - base
                at = jnp.where((at >= 0) & (at < 6), at, 6)
                canvas[at, part] += jnp.where(keep, value, 0.0)
    below[...] = canvas[0:2].astype(BF16)
    same[...] = canvas[2:4]
    above[...] = canvas[4:6].astype(BF16)


def split_kernel(plan, same, low, high, keep, send):
    x_at = plan[3, 0] % 2
    keep[...] = same[x_at] + low[x_at].astype(F32) + high[x_at].astype(F32)
    other = same[1 - x_at] + low[1 - x_at].astype(F32) + high[1 - x_at].astype(F32)
    send[...] = other.astype(BF16)


def end_kernel(layers, *refs):
    extra, out = refs[-2:]
    for layer in range(layers):
        out[layer] = refs[layer][...] + refs[layers + layer][...].astype(F32) + extra[layer].astype(F32)


def spread_kernel(plan, mine, beyond, came, keep, send):
    pos = plan[3, 0]
    rows = keep.shape[-2]
    for which, near in enumerate((mine, beyond)):
        for turn in range(keep.shape[1]):
            for flip in range(2):
                at = pl.ds(pl.multiple_of((pos ^ (2 * turn + flip)) * rows, rows), rows)
                total = near[:, :, at].astype(F32) + came[which, :, :, at].astype(F32)
                if flip:
                    send[which, turn] = total.astype(BF16)
                else:
                    keep[which, turn] = total


def fold_kernel(near, came, keep, send):
    keep[...] = near[0] + came[0].astype(F32)
    send[...] = (near[1] + came[1].astype(F32)).astype(BF16)


def gather_kernel(near, came, own, *sends):
    own[...] = near[0] + came[0].astype(F32)
    for turn, send in enumerate(sends, 1):
        send[...] = (near[turn] + came[turn].astype(F32)).astype(BF16)


def total_kernel(*refs):
    total = refs[0][...]
    for ref in refs[1:-1]:
        total = total + ref[...].astype(F32)
    refs[-1][...] = total


def turned(value, turn, tiles):
    return lax.ppermute(value, "tile", [(i, i ^ turn) for i in range(tiles)])


def distant_blocks(plan, pieces, tiles, points, groups):
    rows = pieces[0][0].shape[1]
    pos, tile = plan[3, 0], plan[3, 1]
    sub = (jnp.arange(rows, dtype=jnp.int32) + tile % 2 * rows)[:, None]
    lane = jnp.arange(points, dtype=jnp.int32)[None, :]
    block = jnp.arange(groups, dtype=jnp.int32)
    outside = jnp.abs(block // 2 - pos // 2) > 1
    canvas = 0.0
    for turn in range(tiles):
        place = pos * tiles + (tile ^ turn)
        row, col = jnp.take(plan[1], place), jnp.take(plan[2], place)
        mine = jnp.where(sub >= row, 0, 1) == tile // 2
        target = col // points + jnp.where(lane >= col % points, 0, 1)
        keep = outside[:, None, None] & mine[None] & (target[None] == block[:, None, None])
        value = jnp.stack([layer[turn] for layer in pieces]).astype(F32)
        canvas = canvas + jnp.where(keep[:, None, None], value[None], 0.0)
    shares = lax.all_to_all(canvas.astype(BF16), "pos", split_axis=0, concat_axis=0, tiled=True)
    return jnp.sum(shares.astype(F32), axis=0).astype(BF16)


def on_device_by_slot(probe_modes, object_slices, amplitudes, scan_offsets, slot_counts):
    groups, tiles = lax.axis_size("pos"), lax.axis_size("tile")
    slots, points = amplitudes.shape[0], amplitudes.shape[-1]
    layers, rows = object_slices.shape[0], object_slices.shape[2]
    modes = probe_modes.shape[0]
    tables, kernel, mover = (jnp.asarray(t) for t in split_tables(points))
    field = (2, points, points)

    low = probe_modes.astype(BF16)
    low, scan_offsets = lax.optimization_barrier((low, scan_offsets))
    across = turned(low, 2, tiles)
    beside = turned(low, 1, tiles)
    shot = (points, points)
    outs = call(
        functools.partial(first_kernel, groups, tiles, points),
        (slot_counts, scan_offsets, object_slices, amplitudes),
        [SM, VM, HB, HB],
        [((layers, 2, rows, points), BF16)] * tiles
        + [((groups // 2, *shot), BF16)]
        + [((groups // 4, *shot), BF16)] * 2
        + [((8, 128), jnp.int32)],
        [
            pltpu.SMEM((8, 128), jnp.int32),
            pltpu.VMEM(object_slices.shape, BF16),
            pltpu.VMEM(amplitudes.shape, BF16),
            pltpu.SemaphoreType.DMA((3,)),
        ],
        name="first",
        us=5.0,
        mib=16,
    )
    (*cut, same, far, near, plan) = outs
    across, cut = lax.optimization_barrier((across, cut))
    aside = [(i, i ^ 1) for i in range(groups)]
    merged = [None] * (groups // 2)
    for turns, value in (((2, 3), far), ((0, 1), near)):
        merged[turns[0]], merged[turns[1]] = call(
            functools.partial(merge_kernel, tiles, slots, turns),
            (plan, same, lax.ppermute(value, "pos", aside)),
            [SM, VM, VM],
            [(shot, BF16)] * 2,
            name="merge",
        )
    arrived = [merged[0]] + [
        lax.ppermute(merged[turn], "pos", [(i, i ^ (2 * turn)) for i in range(groups)])
        for turn in range(1, groups // 2)
    ]
    strips = [cut[0]] + [turned(cut[turn], turn, tiles) for turn in range(1, tiles)]
    probes = [probe_modes, beside, across, turned(across, 1, tiles)]
    half = ((2, points // 2, points), BF16)
    stack = (tiles * modes, *field)
    first, second, phi, far, power = call(
        functools.partial(ahead_kernel, tiles, points),
        (plan, *strips, *probes, tables, kernel),
        [SM] + [VK] * tiles + [HB] + [VK] * 3 + [HB] * 2,
        [(field, BF16), (field, BF16), (stack, BF16), (stack, BF16), ((points, points), F32)],
        [
            pltpu.VMEM(probe_modes.shape, F32),
            pltpu.VMEM(tables.shape, BF16),
            pltpu.VMEM(kernel.shape, F32),
            pltpu.VMEM(field, F32),
            pltpu.SemaphoreType.DMA((3,)),
        ],
        name="ahead",
        us=12.0,
        mib=24,
        keep=range(5),
    )
    own, other, inner = call(
        functools.partial(back_kernel, tiles, points, slots),
        (plan, power, phi, far, second, tables, mover, *arrived),
        [SM] + [VK] * 4 + [HB] * 2 + [VM] * len(arrived),
        [half, half, (stack, BF16)],
        [
            pltpu.VMEM(tables.shape, BF16),
            pltpu.VMEM(mover.shape, BF16),
            pltpu.VMEM((points, points), BF16),
            pltpu.VMEM(field, F32),
            pltpu.VMEM((points, points), F32),
            pltpu.SemaphoreType.DMA((2,)),
        ],
        name="back",
        us=5.0,
        mib=24,
        keep=(2,),
    )
    pieces = [None] * layers
    pieces[1] = [own] + [turned(v, turn, tiles) for turn, v in ((1, other), (2, own), (3, other))]
    own, other, mine, beyond, beside = call(
        functools.partial(last_kernel, tiles, points),
        (plan, inner, *probes, first, tables, kernel),
        [SM, VK, HB] + [VK] * 4 + [HB] * 2,
        [half, half] + [((modes, *field), BF16)] * 2 + [((2, modes, *field), BF16)],
        [
            pltpu.VMEM(probe_modes.shape, F32),
            pltpu.VMEM(tables.shape, BF16),
            pltpu.VMEM(kernel.shape, F32),
            pltpu.VMEM(field, F32),
            pltpu.SemaphoreType.DMA((3,)),
        ],
        name="last",
        us=6.0,
        mib=24,
    )
    pieces[1], own, other, beside = lax.optimization_barrier((pieces[1], own, other, beside))
    pieces[0] = [own] + [turned(v, turn, tiles) for turn, v in ((1, other), (2, own), (3, other))]
    share = (groups // 2, modes, 2, points // groups, points)
    keep, send = call(
        spread_kernel,
        (plan, mine, beyond, turned(beside, 1, tiles)),
        [SM] + [VM] * 3,
        [((2, *share), F32), ((2, *share), BF16)],
        name="spread",
    )
    keep, send = call(
        fold_kernel,
        (keep, lax.ppermute(send, "pos", aside)),
        [VM] * 2,
        [(share, F32), (share, BF16)],
        name="fold",
    )
    own, *sends = call(
        gather_kernel,
        (keep, turned(send, 2, tiles)),
        [VM] * 2,
        [(share[1:], F32)] + [(share[1:], BF16)] * (groups // 2 - 1),
        name="gather",
    )
    came = [
        lax.ppermute(send, "pos", [(i, i ^ (2 * turn)) for i in range(groups)]) for turn, send in enumerate(sends, 1)
    ]
    (probe_grad,) = call(total_kernel, (own, *came), [VM] * (1 + len(came)), [(share[1:], F32)], name="total")

    block = (2, rows, points)
    keeps, swapped = [None] * layers, [None] * layers
    for layer in reversed(range(layers)):
        below, same, above = call(
            functools.partial(place_kernel, tiles, points),
            (plan, *pieces[layer]),
            [SM] + [VM] * tiles,
            [((2, *block), BF16), ((2, *block), F32), ((2, *block), BF16)],
            [pltpu.VMEM((7, *block), F32)],
            name="place",
        )
        if layer:
            pieces[0], above, below = lax.optimization_barrier((pieces[0], above, below))
        low_in = lax.ppermute(above, "pos", [(i, i + 2) for i in range(groups - 2)])
        high_in = lax.ppermute(below, "pos", [(i + 2, i) for i in range(groups - 2)])
        if layer == 0:
            pieces, low_in = lax.optimization_barrier((pieces, low_in))
        keeps[layer], send = call(
            split_kernel,
            (plan, same, low_in, high_in),
            [SM] + [VM] * 3,
            [(block, F32), (block, BF16)],
            name="split",
        )
        swapped[layer] = lax.ppermute(send, "pos", [(i, i ^ 1) for i in range(groups)])
    extra = lax.cond(
        plan[3, 2] > 0,
        lambda p: distant_blocks(plan, p, tiles, points, groups),
        lambda p: jnp.zeros((layers, *block), BF16),
        pieces,
    )
    (object_grad,) = call(
        functools.partial(end_kernel, layers),
        (*keeps, *swapped, extra),
        [VM] * (2 * layers + 1),
        [((layers, *block), F32)],
        name="end",
    )
    return object_grad, probe_grad


def make_tables(points):
    counter = jnp.arange(points, dtype=jnp.int32)
    product = counter[:, None] * counter[None, :] % points
    angle = 2.0 * jnp.pi / points * product.astype(jnp.float32)
    factor = 1.0 / jnp.sqrt(jnp.float32(points))
    table_re = (jnp.cos(angle) * factor).astype(jnp.bfloat16)
    table_im = (-jnp.sin(angle) * factor).astype(jnp.bfloat16)
    shifted = ((counter + points // 2) % points - points // 2).astype(jnp.float32)
    phase = (
        jnp.pi
        * FRESNEL
        / points
        * (shifted[:, None] * shifted[:, None] + shifted[None, :] * shifted[None, :])
    )
    kernel = jnp.stack([jnp.cos(phase), -jnp.sin(phase)])
    return (table_re, table_im, kernel)


def times_complex(first, second):
    real_part = (
        first[..., 0, :, :] * second[..., 0, :, :] - first[..., 1, :, :] * second[..., 1, :, :]
    )
    imag_part = (
        first[..., 0, :, :] * second[..., 1, :, :] + first[..., 1, :, :] * second[..., 0, :, :]
    )
    return jnp.stack([real_part, imag_part], axis=-3)


def conjugate(values):
    return jnp.stack([values[..., 0, :, :], -values[..., 1, :, :]], axis=-3)


def transform_many(values, table_re, table_im):
    tables = jnp.stack([table_re, table_im])
    lowered = values.astype(jnp.bfloat16)
    first = jnp.einsum("gab,nmtbc->nmgtac", tables, lowered, preferred_element_type=jnp.float32)
    middle = jnp.stack(
        [first[:, :, 0, 0] - first[:, :, 1, 1], first[:, :, 0, 1] + first[:, :, 1, 0]], axis=2
    ).astype(jnp.bfloat16)
    second = jnp.einsum("nmtab,gbc->nmtgac", middle, tables, preferred_element_type=jnp.float32)
    return jnp.stack(
        [second[:, :, 0, 0] - second[:, :, 1, 1], second[:, :, 0, 1] + second[:, :, 1, 0]], axis=2
    )


def propagate_many(values, table_re, table_im, kernel):
    return transform_many(
        times_complex(transform_many(values, table_re, table_im), kernel), table_re, -table_im
    )


def window_anchor(place):
    zero_index = jnp.int32(0)
    return (zero_index, zero_index, place[0], place[1])


def on_device_by_mode(probe_modes, object_slices, amplitudes, scan_offsets, slot_counts):
    group = lax.axis_index("pos")
    groups = lax.axis_size("pos")
    tile_at = lax.axis_index("tile")
    strips = lax.axis_size("tile")
    slots = amplitudes.shape[0]
    points = amplitudes.shape[-1]
    layers = object_slices.shape[0]
    strip_rows = object_slices.shape[2]
    starts = jnp.cumsum(slot_counts) - slot_counts
    share = slots // 2
    wanted = jnp.arange(groups * share, dtype=jnp.int32)
    within = wanted - starts[group]
    usable = (within >= 0) & (within < slot_counts[group])
    picked = jnp.take(amplitudes, jnp.clip(within, 0, slots - 1), axis=0)
    outgoing = jnp.where(usable[:, None, None], picked, jnp.zeros_like(picked))
    arrived_rows = lax.all_to_all(outgoing, "pos", split_axis=0, concat_axis=0, tiled=True)
    mine = group * share + jnp.arange(share, dtype=jnp.int32)
    source = jnp.sum((starts[None, :] <= mine[:, None]).astype(jnp.int32), axis=1) - 1
    amplitude = jnp.take(arrived_rows, source * share + jnp.arange(share, dtype=jnp.int32), axis=0)
    places = jnp.take(scan_offsets, source * slots + mine - starts[source], axis=0)
    alive = jnp.ones((share,), jnp.float32)
    padded = jnp.pad(object_slices, ((0, 0), (0, 0), (points, points), (0, 0)))

    def cut_piece(place):
        local_row = jnp.clip(place[0] - tile_at * strip_rows + points, 0, strip_rows + points)
        shifted_place = jnp.stack([local_row, place[1]])
        return lax.dynamic_slice(padded, window_anchor(shifted_place), (layers, 2, points, points))

    pieces = jax.vmap(cut_piece)(places).astype(jnp.float32)
    windows = lax.psum(pieces.astype(jnp.bfloat16), "tile").astype(jnp.float32)
    table_re, table_im, kernel = make_tables(points)
    kernel_conj = conjugate(kernel)
    current = times_complex(probe_modes[None], windows[:, None, 0])
    layer_at = 1
    arrived = propagate_many(current, table_re, table_im, kernel)
    entering = [arrived]
    current = times_complex(arrived, windows[:, None, layer_at])
    far_field = transform_many(current, table_re, table_im)
    partial_power = jnp.sum(far_field * far_field, axis=(1, 2))
    power = lax.psum(partial_power.astype(jnp.bfloat16), "tile").astype(jnp.float32)
    ratio = (1.0 - amplitude.astype(jnp.float32) / jnp.sqrt(power + 1.0)) * alive[:, None, None]
    incoming = transform_many(ratio[:, None, None] * far_field, table_re, -table_im)
    object_terms = [None] * layers
    layer_at = 1
    object_terms[layer_at] = jnp.sum(
        times_complex(conjugate(entering[layer_at - 1]), incoming), axis=1
    )
    incoming = propagate_many(
        times_complex(conjugate(windows[:, None, layer_at]), incoming),
        table_re,
        table_im,
        kernel_conj,
    )
    object_terms[0] = jnp.sum(times_complex(conjugate(probe_modes[None]), incoming), axis=1)
    probe_term = jnp.sum(times_complex(conjugate(windows[:, None, 0]), incoming), axis=0)
    slot_grads = jnp.stack(object_terms, axis=1)
    canvas = jnp.zeros((layers, 2, strip_rows * strips, object_slices.shape[3]), jnp.float32)

    def deposit(canvas, packed):
        place, term = packed
        anchor = window_anchor(place)
        current_part = lax.dynamic_slice(canvas, anchor, term.shape)
        return (lax.dynamic_update_slice(canvas, current_part + term, anchor), None)

    canvas, unused = lax.scan(deposit, canvas, (places, slot_grads))
    column_part = lax.psum_scatter(
        canvas.astype(jnp.bfloat16), "pos", scatter_dimension=3, tiled=True
    )
    object_grad = lax.psum_scatter(column_part, "tile", scatter_dimension=2, tiled=True).astype(
        jnp.float32
    )
    probe_grad = lax.psum_scatter(
        probe_term.astype(jnp.bfloat16), "pos", scatter_dimension=2, tiled=True
    ).astype(jnp.float32)
    return (object_grad, probe_grad)


def solution(mesh):
    in_specs = (
        P("tile", None, None, None),
        P(None, None, "tile", None),
        P("pos", None, None),
        P(),
        P(),
    )
    out_specs = (P(None, None, "tile", "pos"), P("tile", None, "pos", None))
    by_slot = mesh.shape["tile"] == 4 and mesh.shape["pos"] == 8
    return jax.shard_map(
        on_device_by_slot if by_slot else on_device_by_mode,
        mesh=mesh,
        in_specs=in_specs,
        out_specs=out_specs,
        check_vma=False,
    )
```

```python
import functools

import jax
import jax.numpy as jnp
import ml_dtypes
import numpy as np
from jax import lax
from jax.experimental import pallas as pl
from jax.experimental.pallas import tpu as pltpu
from jax.sharding import PartitionSpec as P

FRESNEL = 0.37
BF16 = jnp.bfloat16
F32 = jnp.float32


def split_tables(points):
    half = points // 2
    counter = np.arange(points)
    angle = (2.0 * np.pi / points * (counter[:, None] * counter[None, :] % points)).astype(np.float32)
    factor = np.float32(1.0) / np.sqrt(np.float32(points))
    table_re = np.cos(angle) * factor
    table_im = -np.sin(angle) * factor

    def stacked(rows):
        re, im = table_re[rows, :half], table_im[rows, :half]
        return np.block([[re, -im], [im, re]]).astype(ml_dtypes.bfloat16)

    even, odd = stacked(slice(0, None, 2)), stacked(slice(1, None, 2))
    tables = np.stack([even, odd, even.T, odd.T])
    order = np.concatenate([counter[0::2], counter[1::2]])
    shifted = ((order + half) % points - half).astype(np.float64)
    phase = np.pi * FRESNEL / points * (shifted[:, None] ** 2 + shifted[None, :] ** 2)
    kernel = np.stack([np.cos(phase), -np.sin(phase)]).astype(np.float32)
    mover = np.zeros((points, points), np.float32)
    mover[counter, order] = 1.0
    mover = np.stack([mover, mover.T]).astype(ml_dtypes.bfloat16)
    return tables, kernel, mover


def dot(a, b):
    return jnp.dot(a, b, preferred_element_type=F32)


def fold_rows(re, im):
    half = re.shape[0] // 2
    top = jnp.concatenate([re[:half], im[:half]], axis=0)
    bottom = jnp.concatenate([re[half:], im[half:]], axis=0)
    return (top + bottom).astype(BF16), (top - bottom).astype(BF16)


def join_parts(values, axis):
    return jnp.concatenate(values, axis=axis)


def forward_folded(folded, tables):
    half = folded[0][0].shape[0] // 2
    evens = [dot(tables[0], even) for even, _ in folded]
    odds = [dot(tables[1], odd) for _, odd in folded]
    lanes = []
    for even, odd in zip(evens, odds):
        re = join_parts([even[:half], odd[:half]], 0)
        im = join_parts([even[half:], odd[half:]], 0)
        left = join_parts([re[:, :half], im[:, :half]], 1)
        right = join_parts([re[:, half:], im[:, half:]], 1)
        lanes.append(((left + right).astype(BF16), (left - right).astype(BF16)))
    evens = [dot(even, tables[2]) for even, _ in lanes]
    odds = [dot(odd, tables[3]) for _, odd in lanes]
    return [
        (join_parts([even[:, :half], odd[:, :half]], 1), join_parts([even[:, half:], odd[:, half:]], 1))
        for even, odd in zip(evens, odds)
    ]


def inverse(fields, tables):
    half = fields[0][0].shape[0] // 2
    low = [(re.astype(BF16), im.astype(BF16)) for re, im in fields]
    evens = [dot(tables[2], join_parts([re[:half], im[:half]], 0)) for re, im in low]
    odds = [dot(tables[3], join_parts([re[half:], im[half:]], 0)) for re, im in low]
    lanes = []
    for even, odd in zip(evens, odds):
        total, rest = (even + odd).astype(BF16), (even - odd).astype(BF16)
        re = join_parts([total[:half], rest[:half]], 0)
        im = join_parts([total[half:], rest[half:]], 0)
        lanes.append((join_parts([re[:, :half], im[:, :half]], 1), join_parts([re[:, half:], im[:, half:]], 1)))
    evens = [dot(even, tables[0]) for even, _ in lanes]
    odds = [dot(odd, tables[1]) for _, odd in lanes]
    out = []
    for even, odd in zip(evens, odds):
        total, rest = even + odd, even - odd
        re = join_parts([total[:, :half], rest[:, :half]], 1)
        im = join_parts([total[:, half:], rest[:, half:]], 1)
        out.append((re, im))
    return out


def times(a_re, a_im, b_re, b_im):
    return a_re * b_re - a_im * b_im, a_re * b_im + a_im * b_re


def conj_times(a_re, a_im, b_re, b_im):
    return a_re * b_re + a_im * b_im, a_re * b_im - a_im * b_re


def load_complex(ref, *lead):
    return ref[(*lead, 0)].astype(F32), ref[(*lead, 1)].astype(F32)


VM = pl.BlockSpec(memory_space=pltpu.VMEM)
SM = pl.BlockSpec(memory_space=pltpu.SMEM)
HB = pl.BlockSpec(memory_space=pltpu.HBM)
VK = object()


def call(body, inputs, specs, outs, scratch=(), out_specs=None, name=None, us=0.1, mib=8, keep=()):
    return pl.pallas_call(
        body,
        out_shape=[
            pltpu.VMEM(shape, dtype) if at in keep else jax.ShapeDtypeStruct(shape, dtype)
            for at, (shape, dtype) in enumerate(outs)
        ],
        in_specs=[VM if spec is VK else spec for spec in specs],
        out_specs=[VM] * len(outs) if out_specs is None else out_specs,
        scratch_shapes=list(scratch),
        compiler_params=pltpu.CompilerParams(vmem_limit_bytes=mib * 1024 * 1024),
        cost_estimate=pl.CostEstimate(flops=int(us * 1e9), bytes_accessed=int(us * 3e6), transcendentals=0),
        name=name,
    )(
        *(
            pltpu.with_memory_space_constraint(value, pltpu.VMEM) if spec is VK else value
            for value, spec in zip(inputs, specs)
        )
    )


def fetch(sources, targets, sems):
    copies = [pltpu.make_async_copy(s, t, sems.at[at]) for at, (s, t) in enumerate(zip(sources, targets))]
    for copy in copies:
        copy.start()
    return copies


def slot_at(plan, tiles, turn):
    place = plan[3, 0] * tiles + (plan[3, 1] ^ turn)
    return plan[1, place], plan[2, place]


def first_kernel(groups, tiles, points, counts, offsets, strip_far, amplitudes_far, *refs):
    strips = refs[:tiles]
    same, other_x, plan_out, plan, strip, amplitudes, sems = refs[tiles:]
    layers, rows = strip.shape[0], strip.shape[2]
    slots = amplitudes.shape[0]
    n = offsets.shape[1]
    strip_copy = pltpu.make_async_copy(strip_far, strip, sems.at[1])
    strip_copy.start()
    amplitude_copy = pltpu.make_async_copy(amplitudes_far, amplitudes, sems.at[2])
    amplitude_copy.start()
    pos, tile = lax.axis_index("pos"), lax.axis_index("tile")
    width = plan_out.shape[1]

    number = lax.broadcasted_iota(jnp.int32, (1, n), 1)
    live = jnp.zeros((1, n), jnp.int32)
    for group in range(groups):
        live += jnp.where((number >= group * slots) & (number < group * slots + counts[group]), 1, 0)
    row, col = offsets[0:1, :].astype(F32), offsets[1:2, :].astype(F32)
    number = number.astype(F32)
    across = jnp.where(live > 0, col, float(1 << 12)) * n + number
    square = (n, n)
    eye = lax.broadcasted_iota(jnp.int32, square, 0) == lax.broadcasted_iota(jnp.int32, square, 1)
    key, number, row, col = (
        jnp.sum(jnp.where(eye, value, 0.0), axis=1, keepdims=True) for value in (across, number, row, col)
    )
    rank = jnp.sum(jnp.where(across < key, 1.0, 0.0), axis=1, keepdims=True).astype(jnp.int32)
    here = lax.broadcasted_iota(jnp.int32, (n, width), 1) == rank
    chosen = [
        jnp.sum(jnp.where(here, value, 0.0), axis=0, keepdims=True).astype(jnp.int32)
        for value in (number, row, col)
    ]
    lane = lax.broadcasted_iota(jnp.int32, (1, width), 1)
    outer = 2 * points
    lowest = jnp.maximum(sum(jnp.where(lane >= i * 2 * tiles, 1, 0) for i in range(1, groups // 2)) - 1, 0)
    far = (chosen[2] < lowest * outer) | (chosen[2] + points > (lowest + jnp.where(lane < 2 * tiles, 2, 3)) * outer)
    distant = jnp.max(jnp.where(far & (lane < groups * slots // 2), 1.0, 0.0), axis=1, keepdims=True)
    for at, value in enumerate(chosen):
        plan_out[at : at + 1, :] = value
    plan_out[3:4, :] = jnp.where(
        lane == 0, pos, jnp.where(lane == 1, tile, jnp.where(lane == 2, distant.astype(jnp.int32), 0))
    )
    plan_out[4:8, :] = jnp.zeros((4, width), jnp.int32)
    copy = pltpu.make_async_copy(plan_out, plan, sems.at[0])
    copy.start()
    copy.wait()
    strip_copy.wait()

    blocks = strip.shape[-1] // points
    lane = lax.broadcasted_iota(jnp.int32, (rows, points), 1)
    for turn in range(tiles):
        _, col = slot_at(plan, tiles, turn)
        block = col // points
        later = jnp.minimum(block + 1, blocks - 1)
        keep = lane >= col % points
        for layer in range(layers):
            for part in range(2):
                here = strip[layer, part, :, pl.ds(pl.multiple_of(block * points, points), points)]
                there = strip[layer, part, :, pl.ds(pl.multiple_of(later * points, points), points)]
                strips[turn][layer, part] = jnp.where(
                    keep, here.astype(F32), there.astype(F32)
                ).astype(BF16)
    amplitude_copy.wait()
    for turn in range(groups // 2):
        for flip, out, at in ((0, same, turn), (1, other_x, turn)):
            slot = plan[0, (pos ^ (2 * turn + flip)) * tiles + tile]

            @pl.when(slot // slots == pos)
            def _(out=out, at=at, slot=slot):
                out[at] = amplitudes[slot % slots]


def merge_kernel(tiles, slots, turns, plan, same, came, *outs):
    pos, tile = plan[3, 0], plan[3, 1]
    for at, (turn, out) in enumerate(zip(turns, outs)):
        source = plan[0, (pos ^ (2 * turn)) * tiles + tile] // slots

        @pl.when(source == pos)
        def _(turn=turn, out=out):
            out[...] = same[turn]

        @pl.when(source == (pos ^ 1))
        def _(at=at, out=out):
            out[...] = came[at]


def join(tiles, points, plan, strips, layer, whole, out):
    own, one, two, three = strips
    rows = own.shape[2]
    row, col = slot_at(plan, tiles, 0)
    core, up = plan[3, 1] % 2, plan[3, 1] // 2
    sub = lax.broadcasted_iota(jnp.int32, (rows, points), 0)
    for near, far, at in ((own, two, core), (one, three, 1 - core)):
        low = jnp.where(sub + at * rows >= row, 0, 1)
        for part in range(2):
            whole[part, pl.ds(pl.multiple_of(at * rows, rows), rows)] = jnp.where(
                low == up, near[layer, part].astype(F32), far[layer, part].astype(F32)
            )
    for part in range(2):
        value = pltpu.roll(whole[part], (points - row % points) % points, 0)
        out[part] = pltpu.roll(value, (points - col % points) % points, 1).astype(BF16)


def forward(probes, first, second, tables, kernel, phi, far):
    modes = probes[0].shape[0]
    fields = []
    for probe in probes:
        for mode in range(modes):
            fields.append(fold_rows(*times(*load_complex(probe, mode), *load_complex(first))))
    fields = forward_folded(fields, tables)
    fields = inverse([times(re, im, kernel[0], kernel[1]) for re, im in fields], tables)
    folded = []
    for at, (re, im) in enumerate(fields):
        phi[at, 0], phi[at, 1] = re.astype(BF16), im.astype(BF16)
        folded.append(fold_rows(*times(re, im, *load_complex(second))))
    fields = forward_folded(folded, tables)
    power = None
    for at, (re, im) in enumerate(fields):
        far[at, 0], far[at, 1] = re.astype(BF16), im.astype(BF16)
        square = re * re + im * im
        power = square if power is None else power + square
    return power


def put_by_residue(plan, tiles, points, total, own, other):
    row, col = slot_at(plan, tiles, 0)
    core = plan[3, 1] % 2
    rows = points // 2
    for part in range(2):
        total[part] = pltpu.roll(pltpu.roll(total[part], row % points, 0), col % points, 1)
    for out, at in ((own, core), (other, 1 - core)):
        for part in range(2):
            out[part] = total[part, pl.ds(pl.multiple_of(at * rows, rows), rows)].astype(BF16)


def ahead_kernel(tiles, points, plan, *refs):
    strips, near, beside, across, diagonal, tables_far, kernel_far = refs[:4], *refs[4:10]
    first, second, phi, far, power = refs[10:15]
    mine, tables, kernel, whole, sems = refs[15:]
    copies = fetch((near, tables_far, kernel_far), (mine, tables, kernel), sems)
    join(tiles, points, plan, strips, 0, whole, first)
    join(tiles, points, plan, strips, 1, whole, second)
    for copy in copies:
        copy.wait()
    size = phi.shape[0] // 2
    power[...] = forward((mine, beside), first, second, tables, kernel, phi.at[:size], far.at[:size])
    power[...] += forward((across, diagonal), first, second, tables, kernel, phi.at[size:], far.at[size:])


def back_kernel(tiles, points, slots, plan, *refs):
    power, phi, far, second, tables_far, mover_far = refs[:6]
    arrived = refs[6:10]
    own, other, inner = refs[10:13]
    tables, mover, amplitude, total, ratio, sems = refs[13:]
    copies = fetch((mover_far, tables_far), (mover, tables), sems)
    source = plan[0, plan[3, 0] * tiles + plan[3, 1]] // slots
    for turn, ref in enumerate(arrived):

        @pl.when(((source ^ plan[3, 0]) >> 1) == turn)
        def _(ref=ref):
            amplitude[...] = ref[...]

    for copy in copies:
        copy.wait()
    measured = dot(dot(mover[0], amplitude[...]).astype(BF16), mover[1])
    ratio[...] = 1.0 - measured / jnp.sqrt(power[...] + 1.0)
    total[...] = jnp.zeros_like(total)
    size = phi.shape[0] // 2
    for start in (0, size):
        fields = []
        for at in range(start, start + size):
            re, im = load_complex(far, at)
            fields.append((re * ratio[...], im * ratio[...]))
        fields = inverse(fields, tables)
        for at, (re, im) in enumerate(fields, start):
            grad_re, grad_im = conj_times(*load_complex(phi, at), re, im)
            total[0] += grad_re
            total[1] += grad_im
            inner[at, 0], inner[at, 1] = fold_rows(*conj_times(*load_complex(second), re, im))
    put_by_residue(plan, tiles, points, total, own, other)


def last_kernel(tiles, points, plan, *refs):
    inner, near, beside, across, diagonal, first, tables_far, kernel_far = refs[:8]
    own, other, near_grad, beyond_grad, beside_grad = refs[8:13]
    mine, tables, kernel, total, sems = refs[13:]
    copies = fetch((tables_far, kernel_far, near), (tables, kernel, mine), sems)
    modes = mine.shape[0]
    probes = (mine, beside, across, diagonal)
    grads = (near_grad, beside_grad.at[0], beyond_grad, beside_grad.at[1])
    total[...] = jnp.zeros_like(total)
    for copy in copies:
        copy.wait()
    for start in range(0, tiles, 2):
        which = [(turn, mode) for turn in range(start, start + 2) for mode in range(modes)]
        fields = forward_folded([(inner[t * modes + m, 0], inner[t * modes + m, 1]) for t, m in which], tables)
        fields = inverse([conj_times(kernel[0], kernel[1], re, im) for re, im in fields], tables)
        for (turn, mode), (re, im) in zip(which, fields):
            grad_re, grad_im = conj_times(*load_complex(probes[turn], mode), re, im)
            total[0] += grad_re
            total[1] += grad_im
            re, im = conj_times(*load_complex(first), re, im)
            grads[turn][mode, 0], grads[turn][mode, 1] = re.astype(BF16), im.astype(BF16)
    put_by_residue(plan, tiles, points, total, own, other)


def place_kernel(tiles, points, plan, *refs):
    pieces, (even, same, odd, canvas) = refs[:-4], refs[-4:]
    rows = pieces[0].shape[1]
    core, up = plan[3, 1] % 2, plan[3, 1] // 2
    base = plan[3, 0] // 2 * 2 - 2
    sub = lax.broadcasted_iota(jnp.int32, (rows, points), 0) + core * rows
    lane = lax.broadcasted_iota(jnp.int32, (rows, points), 1)
    canvas[...] = jnp.zeros_like(canvas)
    for turn in range(tiles):
        row, col = slot_at(plan, tiles, turn)
        mine = jnp.where(sub >= row, 0, 1) == up
        early = lane >= col % points
        for layer in range(len(pieces) // tiles):
            for part in range(2):
                value = jnp.where(mine, pieces[layer * tiles + turn][part].astype(F32), 0.0)
                for step, keep in ((0, early), (1, ~early)):
                    at = col // points + step - base
                    at = jnp.where((at >= 0) & (at < 6), at, 6)
                    canvas[layer, at, part] += jnp.where(keep, value, 0.0)
    same[...] = canvas[:, 2:4]
    up_first = plan[3, 0] // 2 % 2 == 0
    for out, at in ((even, jnp.where(up_first, 4, 0)), (odd, jnp.where(up_first, 0, 4))):
        out[...] = canvas[:, pl.ds(at, 2)].astype(BF16)


def split_kernel(plan, same, low, high, keep, send):
    x_at = plan[3, 0] % 2
    for layer in range(same.shape[0]):
        mine = same[layer, x_at] + low[layer, x_at].astype(F32) + high[layer, x_at].astype(F32)
        other = same[layer, 1 - x_at] + low[layer, 1 - x_at].astype(F32) + high[layer, 1 - x_at].astype(F32)
        keep[layer] = mine
        send[layer] = other.astype(BF16)


def end_kernel(keep, came, extra, out):
    out[...] = keep[...] + came[...].astype(F32) + extra[...].astype(F32)


def spread_kernel(plan, mine, beyond, came, keep, send):
    pos = plan[3, 0]
    rows = keep.shape[-2]
    for which, near in enumerate((mine, beyond)):
        for turn in range(keep.shape[1]):
            for flip in range(2):
                at = pl.ds(pl.multiple_of((pos ^ (2 * turn + flip)) * rows, rows), rows)
                total = near[:, :, at].astype(F32) + came[which, :, :, at].astype(F32)
                if flip:
                    send[which, turn] = total.astype(BF16)
                else:
                    keep[which, turn] = total


def fold_kernel(near, came, keep, send):
    keep[...] = near[0] + came[0].astype(F32)
    send[...] = (near[1] + came[1].astype(F32)).astype(BF16)


def gather_kernel(near, came, own, *sends):
    own[...] = near[0] + came[0].astype(F32)
    for turn, send in enumerate(sends, 1):
        send[...] = (near[turn] + came[turn].astype(F32)).astype(BF16)


def total_kernel(*refs):
    total = refs[0][...]
    for ref in refs[1:-1]:
        total = total + ref[...].astype(F32)
    refs[-1][...] = total


def turned(value, turn, tiles):
    return lax.ppermute(value, "tile", [(i, i ^ turn) for i in range(tiles)])


def distant_blocks(plan, pieces, tiles, points, groups):
    rows = pieces[0][0].shape[1]
    pos, tile = plan[3, 0], plan[3, 1]
    sub = (jnp.arange(rows, dtype=jnp.int32) + tile % 2 * rows)[:, None]
    lane = jnp.arange(points, dtype=jnp.int32)[None, :]
    block = jnp.arange(groups, dtype=jnp.int32)
    outside = jnp.abs(block // 2 - pos // 2) > 1
    canvas = 0.0
    for turn in range(tiles):
        place = pos * tiles + (tile ^ turn)
        row, col = jnp.take(plan[1], place), jnp.take(plan[2], place)
        mine = jnp.where(sub >= row, 0, 1) == tile // 2
        target = col // points + jnp.where(lane >= col % points, 0, 1)
        keep = outside[:, None, None] & mine[None] & (target[None] == block[:, None, None])
        value = jnp.stack([layer[turn] for layer in pieces]).astype(F32)
        canvas = canvas + jnp.where(keep[:, None, None], value[None], 0.0)
    shares = lax.all_to_all(canvas.astype(BF16), "pos", split_axis=0, concat_axis=0, tiled=True)
    return jnp.sum(shares.astype(F32), axis=0).astype(BF16)


def on_device_by_slot(probe_modes, object_slices, amplitudes, scan_offsets, slot_counts):
    groups, tiles = lax.axis_size("pos"), lax.axis_size("tile")
    slots, points = amplitudes.shape[0], amplitudes.shape[-1]
    layers, rows = object_slices.shape[0], object_slices.shape[2]
    modes = probe_modes.shape[0]
    tables, kernel, mover = (jnp.asarray(t) for t in split_tables(points))
    field = (2, points, points)

    low = probe_modes.astype(BF16)
    low, scan_offsets = lax.optimization_barrier((low, scan_offsets))
    across = turned(low, 2, tiles)
    beside = turned(low, 1, tiles)
    shot = (points, points)
    outs = call(
        functools.partial(first_kernel, groups, tiles, points),
        (slot_counts, scan_offsets.T, object_slices, amplitudes),
        [SM, VM, HB, HB],
        [((layers, 2, rows, points), BF16)] * tiles
        + [((groups // 2, *shot), BF16)] * 2
        + [((8, 128), jnp.int32)],
        [
            pltpu.SMEM((8, 128), jnp.int32),
            pltpu.VMEM(object_slices.shape, BF16),
            pltpu.VMEM(amplitudes.shape, BF16),
            pltpu.SemaphoreType.DMA((3,)),
        ],
        name="first",
        us=0.1,
        mib=16,
    )
    (*cut, same, far, plan) = outs
    across, cut = lax.optimization_barrier((across, cut))
    aside = [(i, i ^ 1) for i in range(groups)]
    merged = call(
        functools.partial(merge_kernel, tiles, slots, range(groups // 2)),
        (plan, same, lax.ppermute(far, "pos", aside)),
        [SM, VM, VM],
        [(shot, BF16)] * (groups // 2),
        name="merge",
    )
    arrived = [merged[0]] + [
        lax.ppermute(merged[turn], "pos", [(i, i ^ (2 * turn)) for i in range(groups)])
        for turn in range(1, groups // 2)
    ]
    strips = [cut[0]] + [turned(cut[turn], turn, tiles) for turn in range(1, tiles)]
    probes = [probe_modes, beside, across, turned(across, 1, tiles)]
    half = ((2, points // 2, points), BF16)
    stack = (tiles * modes, *field)
    first, second, phi, far, power = call(
        functools.partial(ahead_kernel, tiles, points),
        (plan, *strips, *probes, tables, kernel),
        [SM] + [VK] * tiles + [HB] + [VK] * 3 + [HB] * 2,
        [(field, BF16), (field, BF16), (stack, BF16), (stack, BF16), ((points, points), F32)],
        [
            pltpu.VMEM(probe_modes.shape, F32),
            pltpu.VMEM(tables.shape, BF16),
            pltpu.VMEM(kernel.shape, F32),
            pltpu.VMEM(field, F32),
            pltpu.SemaphoreType.DMA((3,)),
        ],
        name="ahead",
        us=0.1,
        mib=24,
        keep=range(5),
    )
    own, other, inner = call(
        functools.partial(back_kernel, tiles, points, slots),
        (plan, power, phi, far, second, tables, mover, *arrived),
        [SM] + [VK] * 4 + [HB] * 2 + [VM] * len(arrived),
        [half, half, (stack, BF16)],
        [
            pltpu.VMEM(tables.shape, BF16),
            pltpu.VMEM(mover.shape, BF16),
            pltpu.VMEM((points, points), BF16),
            pltpu.VMEM(field, F32),
            pltpu.VMEM((points, points), F32),
            pltpu.SemaphoreType.DMA((2,)),
        ],
        name="back",
        us=0.1,
        mib=24,
        keep=(2,),
    )
    pieces = [None] * layers
    pieces[1] = [own] + [turned(v, turn, tiles) for turn, v in ((1, other), (2, own), (3, other))]
    own, other, mine, beyond, beside = call(
        functools.partial(last_kernel, tiles, points),
        (plan, inner, *probes, first, tables, kernel),
        [SM, VK, HB] + [VK] * 4 + [HB] * 2,
        [half, half] + [((modes, *field), BF16)] * 2 + [((2, modes, *field), BF16)],
        [
            pltpu.VMEM(probe_modes.shape, F32),
            pltpu.VMEM(tables.shape, BF16),
            pltpu.VMEM(kernel.shape, F32),
            pltpu.VMEM(field, F32),
            pltpu.SemaphoreType.DMA((3,)),
        ],
        name="last",
        us=0.1,
        mib=24,
    )
    pieces[1], own, other, beside = lax.optimization_barrier((pieces[1], own, other, beside))
    pieces[0] = [own] + [turned(v, turn, tiles) for turn, v in ((1, other), (2, own), (3, other))]
    share = (groups // 2, modes, 2, points // groups, points)
    keep, send = call(
        spread_kernel,
        (plan, mine, beyond, turned(beside, 1, tiles)),
        [SM] + [VM] * 3,
        [((2, *share), F32), ((2, *share), BF16)],
        name="spread",
    )
    keep, send = call(
        fold_kernel,
        (keep, lax.ppermute(send, "pos", aside)),
        [VM] * 2,
        [(share, F32), (share, BF16)],
        name="fold",
    )
    own, *sends = call(
        gather_kernel,
        (keep, turned(send, 2, tiles)),
        [VM] * 2,
        [(share[1:], F32)] + [(share[1:], BF16)] * (groups // 2 - 1),
        name="gather",
    )
    came = [
        lax.ppermute(send, "pos", [(i, i ^ (2 * turn)) for i in range(groups)]) for turn, send in enumerate(sends, 1)
    ]
    (probe_grad,) = call(total_kernel, (own, *came), [VM] * (1 + len(came)), [(share[1:], F32)], name="total")

    block = (2, rows, points)
    even, same, odd = call(
        functools.partial(place_kernel, tiles, points),
        (plan, *pieces[0], *pieces[1]),
        [SM] + [VM] * (2 * tiles),
        [((layers, 2, *block), BF16), ((layers, 2, *block), F32), ((layers, 2, *block), BF16)],
        [pltpu.VMEM((layers, 7, *block), F32)],
        name="place",
        mib=16,
    )
    pairs = [(i, i ^ 2) for i in range(groups)]
    low_in = lax.ppermute(even, "pos", pairs)
    pairs = [(i, i + 2 if i // 2 % 2 else i - 2) for i in range(2, groups - 2)]
    high_in = lax.ppermute(odd, "pos", pairs)
    pieces, low_in = lax.optimization_barrier((pieces, low_in))
    keep, send = call(
        split_kernel,
        (plan, same, low_in, high_in),
        [SM] + [VM] * 3,
        [((layers, *block), F32), ((layers, *block), BF16)],
        name="split",
        mib=16,
    )
    swapped = lax.ppermute(send, "pos", aside)
    extra = lax.cond(
        plan[3, 2] > 0,
        lambda p: distant_blocks(plan, p, tiles, points, groups),
        lambda p: jnp.zeros((layers, *block), BF16),
        pieces,
    )
    (object_grad,) = call(
        end_kernel,
        (keep, swapped, extra),
        [VM] * 3,
        [((layers, *block), F32)],
        name="end",
    )
    return object_grad, probe_grad


def make_tables(points):
    counter = jnp.arange(points, dtype=jnp.int32)
    product = counter[:, None] * counter[None, :] % points
    angle = 2.0 * jnp.pi / points * product.astype(jnp.float32)
    factor = 1.0 / jnp.sqrt(jnp.float32(points))
    table_re = (jnp.cos(angle) * factor).astype(jnp.bfloat16)
    table_im = (-jnp.sin(angle) * factor).astype(jnp.bfloat16)
    shifted = ((counter + points // 2) % points - points // 2).astype(jnp.float32)
    phase = (
        jnp.pi
        * FRESNEL
        / points
        * (shifted[:, None] * shifted[:, None] + shifted[None, :] * shifted[None, :])
    )
    kernel = jnp.stack([jnp.cos(phase), -jnp.sin(phase)])
    return (table_re, table_im, kernel)


def times_complex(first, second):
    real_part = (
        first[..., 0, :, :] * second[..., 0, :, :] - first[..., 1, :, :] * second[..., 1, :, :]
    )
    imag_part = (
        first[..., 0, :, :] * second[..., 1, :, :] + first[..., 1, :, :] * second[..., 0, :, :]
    )
    return jnp.stack([real_part, imag_part], axis=-3)


def conjugate(values):
    return jnp.stack([values[..., 0, :, :], -values[..., 1, :, :]], axis=-3)


def transform_many(values, table_re, table_im):
    tables = jnp.stack([table_re, table_im])
    lowered = values.astype(jnp.bfloat16)
    first = jnp.einsum("gab,nmtbc->nmgtac", tables, lowered, preferred_element_type=jnp.float32)
    middle = jnp.stack(
        [first[:, :, 0, 0] - first[:, :, 1, 1], first[:, :, 0, 1] + first[:, :, 1, 0]], axis=2
    ).astype(jnp.bfloat16)
    second = jnp.einsum("nmtab,gbc->nmtgac", middle, tables, preferred_element_type=jnp.float32)
    return jnp.stack(
        [second[:, :, 0, 0] - second[:, :, 1, 1], second[:, :, 0, 1] + second[:, :, 1, 0]], axis=2
    )


def propagate_many(values, table_re, table_im, kernel):
    return transform_many(
        times_complex(transform_many(values, table_re, table_im), kernel), table_re, -table_im
    )


def window_anchor(place):
    zero_index = jnp.int32(0)
    return (zero_index, zero_index, place[0], place[1])


def on_device_by_mode(probe_modes, object_slices, amplitudes, scan_offsets, slot_counts):
    group = lax.axis_index("pos")
    groups = lax.axis_size("pos")
    tile_at = lax.axis_index("tile")
    strips = lax.axis_size("tile")
    slots = amplitudes.shape[0]
    points = amplitudes.shape[-1]
    layers = object_slices.shape[0]
    strip_rows = object_slices.shape[2]
    starts = jnp.cumsum(slot_counts) - slot_counts
    share = slots // 2
    wanted = jnp.arange(groups * share, dtype=jnp.int32)
    within = wanted - starts[group]
    usable = (within >= 0) & (within < slot_counts[group])
    picked = jnp.take(amplitudes, jnp.clip(within, 0, slots - 1), axis=0)
    outgoing = jnp.where(usable[:, None, None], picked, jnp.zeros_like(picked))
    arrived_rows = lax.all_to_all(outgoing, "pos", split_axis=0, concat_axis=0, tiled=True)
    mine = group * share + jnp.arange(share, dtype=jnp.int32)
    source = jnp.sum((starts[None, :] <= mine[:, None]).astype(jnp.int32), axis=1) - 1
    amplitude = jnp.take(arrived_rows, source * share + jnp.arange(share, dtype=jnp.int32), axis=0)
    places = jnp.take(scan_offsets, source * slots + mine - starts[source], axis=0)
    alive = jnp.ones((share,), jnp.float32)
    padded = jnp.pad(object_slices, ((0, 0), (0, 0), (points, points), (0, 0)))

    def cut_piece(place):
        local_row = jnp.clip(place[0] - tile_at * strip_rows + points, 0, strip_rows + points)
        shifted_place = jnp.stack([local_row, place[1]])
        return lax.dynamic_slice(padded, window_anchor(shifted_place), (layers, 2, points, points))

    pieces = jax.vmap(cut_piece)(places).astype(jnp.float32)
    windows = lax.psum(pieces.astype(jnp.bfloat16), "tile").astype(jnp.float32)
    table_re, table_im, kernel = make_tables(points)
    kernel_conj = conjugate(kernel)
    current = times_complex(probe_modes[None], windows[:, None, 0])
    layer_at = 1
    arrived = propagate_many(current, table_re, table_im, kernel)
    entering = [arrived]
    current = times_complex(arrived, windows[:, None, layer_at])
    far_field = transform_many(current, table_re, table_im)
    partial_power = jnp.sum(far_field * far_field, axis=(1, 2))
    power = lax.psum(partial_power.astype(jnp.bfloat16), "tile").astype(jnp.float32)
    ratio = (1.0 - amplitude.astype(jnp.float32) / jnp.sqrt(power + 1.0)) * alive[:, None, None]
    incoming = transform_many(ratio[:, None, None] * far_field, table_re, -table_im)
    object_terms = [None] * layers
    layer_at = 1
    object_terms[layer_at] = jnp.sum(
        times_complex(conjugate(entering[layer_at - 1]), incoming), axis=1
    )
    incoming = propagate_many(
        times_complex(conjugate(windows[:, None, layer_at]), incoming),
        table_re,
        table_im,
        kernel_conj,
    )
    object_terms[0] = jnp.sum(times_complex(conjugate(probe_modes[None]), incoming), axis=1)
    probe_term = jnp.sum(times_complex(conjugate(windows[:, None, 0]), incoming), axis=0)
    slot_grads = jnp.stack(object_terms, axis=1)
    canvas = jnp.zeros((layers, 2, strip_rows * strips, object_slices.shape[3]), jnp.float32)

    def deposit(canvas, packed):
        place, term = packed
        anchor = window_anchor(place)
        current_part = lax.dynamic_slice(canvas, anchor, term.shape)
        return (lax.dynamic_update_slice(canvas, current_part + term, anchor), None)

    canvas, unused = lax.scan(deposit, canvas, (places, slot_grads))
    column_part = lax.psum_scatter(
        canvas.astype(jnp.bfloat16), "pos", scatter_dimension=3, tiled=True
    )
    object_grad = lax.psum_scatter(column_part, "tile", scatter_dimension=2, tiled=True).astype(
        jnp.float32
    )
    probe_grad = lax.psum_scatter(
        probe_term.astype(jnp.bfloat16), "pos", scatter_dimension=2, tiled=True
    ).astype(jnp.float32)
    return (object_grad, probe_grad)


def solution(mesh):
    in_specs = (
        P("tile", None, None, None),
        P(None, None, "tile", None),
        P("pos", None, None),
        P(),
        P(),
    )
    out_specs = (P(None, None, "tile", "pos"), P("tile", None, "pos", None))
    by_slot = mesh.shape["tile"] == 4 and mesh.shape["pos"] == 8
    return jax.shard_map(
        on_device_by_slot if by_slot else on_device_by_mode,
        mesh=mesh,
        in_specs=in_specs,
        out_specs=out_specs,
        check_vma=False,
    )
```

```python
import functools

import jax
import jax.numpy as jnp
import ml_dtypes
import numpy as np
from jax import lax
from jax.experimental import pallas as pl
from jax.experimental.pallas import tpu as pltpu
from jax.sharding import PartitionSpec as P

FRESNEL = 0.37
BF16 = jnp.bfloat16
F32 = jnp.float32


def split_tables(points):
    half = points // 2
    counter = np.arange(points)
    angle = (2.0 * np.pi / points * (counter[:, None] * counter[None, :] % points)).astype(np.float32)
    factor = np.float32(1.0) / np.sqrt(np.float32(points))
    table_re = np.cos(angle) * factor
    table_im = -np.sin(angle) * factor

    def stacked(rows):
        re, im = table_re[rows, :half], table_im[rows, :half]
        return np.block([[re, -im], [im, re]]).astype(ml_dtypes.bfloat16)

    even, odd = stacked(slice(0, None, 2)), stacked(slice(1, None, 2))
    tables = np.stack([even, odd, even.T, odd.T])
    order = np.concatenate([counter[0::2], counter[1::2]])
    shifted = ((order + half) % points - half).astype(np.float64)
    phase = np.pi * FRESNEL / points * (shifted[:, None] ** 2 + shifted[None, :] ** 2)
    kernel = np.stack([np.cos(phase), -np.sin(phase)]).astype(np.float32)
    mover = np.zeros((points, points), np.float32)
    mover[counter, order] = 1.0
    mover = np.stack([mover, mover.T]).astype(ml_dtypes.bfloat16)
    return tables, kernel, mover


def dot(a, b):
    return jnp.dot(a, b, preferred_element_type=F32)


def fold_rows(re, im):
    half = re.shape[0] // 2
    top = jnp.concatenate([re[:half], im[:half]], axis=0)
    bottom = jnp.concatenate([re[half:], im[half:]], axis=0)
    return (top + bottom).astype(BF16), (top - bottom).astype(BF16)


def join_parts(values, axis):
    return jnp.concatenate(values, axis=axis)


def forward_folded(folded, tables):
    half = folded[0][0].shape[0] // 2
    evens = [dot(tables[0], even) for even, _ in folded]
    odds = [dot(tables[1], odd) for _, odd in folded]
    lanes = []
    for even, odd in zip(evens, odds):
        re = join_parts([even[:half], odd[:half]], 0)
        im = join_parts([even[half:], odd[half:]], 0)
        left = join_parts([re[:, :half], im[:, :half]], 1)
        right = join_parts([re[:, half:], im[:, half:]], 1)
        lanes.append(((left + right).astype(BF16), (left - right).astype(BF16)))
    evens = [dot(even, tables[2]) for even, _ in lanes]
    odds = [dot(odd, tables[3]) for _, odd in lanes]
    return [
        (join_parts([even[:, :half], odd[:, :half]], 1), join_parts([even[:, half:], odd[:, half:]], 1))
        for even, odd in zip(evens, odds)
    ]


def inverse(fields, tables):
    half = fields[0][0].shape[0] // 2
    low = [(re.astype(BF16), im.astype(BF16)) for re, im in fields]
    evens = [dot(tables[2], join_parts([re[:half], im[:half]], 0)) for re, im in low]
    odds = [dot(tables[3], join_parts([re[half:], im[half:]], 0)) for re, im in low]
    lanes = []
    for even, odd in zip(evens, odds):
        total, rest = (even + odd).astype(BF16), (even - odd).astype(BF16)
        re = join_parts([total[:half], rest[:half]], 0)
        im = join_parts([total[half:], rest[half:]], 0)
        lanes.append((join_parts([re[:, :half], im[:, :half]], 1), join_parts([re[:, half:], im[:, half:]], 1)))
    evens = [dot(even, tables[0]) for even, _ in lanes]
    odds = [dot(odd, tables[1]) for _, odd in lanes]
    out = []
    for even, odd in zip(evens, odds):
        total, rest = even + odd, even - odd
        re = join_parts([total[:, :half], rest[:, :half]], 1)
        im = join_parts([total[:, half:], rest[:, half:]], 1)
        out.append((re, im))
    return out


def times(a_re, a_im, b_re, b_im):
    return a_re * b_re - a_im * b_im, a_re * b_im + a_im * b_re


def conj_times(a_re, a_im, b_re, b_im):
    return a_re * b_re + a_im * b_im, a_re * b_im - a_im * b_re


def load_complex(ref, *lead):
    return ref[(*lead, 0)].astype(F32), ref[(*lead, 1)].astype(F32)


VM = pl.BlockSpec(memory_space=pltpu.VMEM)
SM = pl.BlockSpec(memory_space=pltpu.SMEM)
HB = pl.BlockSpec(memory_space=pltpu.HBM)
VK = object()


def call(body, inputs, specs, outs, scratch=(), out_specs=None, name=None, us=0.1, mib=8, keep=()):
    return pl.pallas_call(
        body,
        out_shape=[
            pltpu.VMEM(shape, dtype) if at in keep else jax.ShapeDtypeStruct(shape, dtype)
            for at, (shape, dtype) in enumerate(outs)
        ],
        in_specs=[VM if spec is VK else spec for spec in specs],
        out_specs=[VM] * len(outs) if out_specs is None else out_specs,
        scratch_shapes=list(scratch),
        compiler_params=pltpu.CompilerParams(vmem_limit_bytes=mib * 1024 * 1024),
        cost_estimate=pl.CostEstimate(flops=int(us * 1e9), bytes_accessed=int(us * 3e6), transcendentals=0),
        name=name,
    )(
        *(
            pltpu.with_memory_space_constraint(value, pltpu.VMEM) if spec is VK else value
            for value, spec in zip(inputs, specs)
        )
    )


def fetch(sources, targets, sems):
    copies = [pltpu.make_async_copy(s, t, sems.at[at]) for at, (s, t) in enumerate(zip(sources, targets))]
    for copy in copies:
        copy.start()
    return copies


def slot_at(plan, tiles, turn):
    place = plan[3, 0] * tiles + (plan[3, 1] ^ turn)
    return plan[1, place], plan[2, place]


def first_kernel(groups, tiles, points, counts, offsets, strip_far, amplitudes_far, *refs):
    strips = refs[:tiles]
    same, other_x, plan_out, plan, strip, amplitudes, sems = refs[tiles:]
    layers, rows = strip.shape[0], strip.shape[2]
    slots = amplitudes.shape[0]
    n = offsets.shape[0]
    strip_copy = pltpu.make_async_copy(strip_far, strip, sems.at[1])
    strip_copy.start()
    amplitude_copy = pltpu.make_async_copy(amplitudes_far, amplitudes, sems.at[2])
    amplitude_copy.start()
    pos, tile = lax.axis_index("pos"), lax.axis_index("tile")
    width = plan_out.shape[1]

    number = lax.broadcasted_iota(jnp.int32, (n, 1), 0)
    live = jnp.zeros((n, 1), jnp.int32)
    for group in range(groups):
        live += jnp.where((number >= group * slots) & (number < group * slots + counts[group]), 1, 0)
    row, col = offsets[:, 0:1].astype(F32), offsets[:, 1:2].astype(F32)
    number = number.astype(F32)
    key = jnp.where(live > 0, col, float(1 << 12)) * n + number
    square = (n, n)
    eye = lax.broadcasted_iota(jnp.int32, square, 0) == lax.broadcasted_iota(jnp.int32, square, 1)
    across = jnp.sum(jnp.where(eye, key, 0.0), axis=0, keepdims=True)
    rank = jnp.sum(jnp.where(across < key, 1.0, 0.0), axis=1, keepdims=True).astype(jnp.int32)
    here = lax.broadcasted_iota(jnp.int32, (n, width), 1) == rank
    chosen = [
        jnp.sum(jnp.where(here, value, 0.0), axis=0, keepdims=True).astype(jnp.int32)
        for value in (number, row, col)
    ]
    lane = lax.broadcasted_iota(jnp.int32, (1, width), 1)
    outer = 2 * points
    lowest = jnp.maximum(sum(jnp.where(lane >= i * 2 * tiles, 1, 0) for i in range(1, groups // 2)) - 1, 0)
    far = (chosen[2] < lowest * outer) | (chosen[2] + points > (lowest + jnp.where(lane < 2 * tiles, 2, 3)) * outer)
    distant = jnp.max(jnp.where(far & (lane < groups * slots // 2), 1.0, 0.0), axis=1, keepdims=True)
    for at, value in enumerate(chosen):
        plan_out[at : at + 1, :] = value
    plan_out[3:4, :] = jnp.where(
        lane == 0, pos, jnp.where(lane == 1, tile, jnp.where(lane == 2, distant.astype(jnp.int32), 0))
    )
    plan_out[4:8, :] = jnp.zeros((4, width), jnp.int32)
    copy = pltpu.make_async_copy(plan_out, plan, sems.at[0])
    copy.start()
    copy.wait()
    strip_copy.wait()

    blocks = strip.shape[-1] // points
    lane = lax.broadcasted_iota(jnp.int32, (rows, points), 1)
    for turn in range(tiles):
        _, col = slot_at(plan, tiles, turn)
        block = col // points
        later = jnp.minimum(block + 1, blocks - 1)
        keep = lane >= col % points
        for layer in range(layers):
            for part in range(2):
                here = strip[layer, part, :, pl.ds(pl.multiple_of(block * points, points), points)]
                there = strip[layer, part, :, pl.ds(pl.multiple_of(later * points, points), points)]
                strips[turn][layer, part] = jnp.where(
                    keep, here.astype(F32), there.astype(F32)
                ).astype(BF16)
    amplitude_copy.wait()
    for turn in range(groups // 2):
        for flip, out, at in ((0, same, turn), (1, other_x, turn)):
            slot = plan[0, (pos ^ (2 * turn + flip)) * tiles + tile]

            @pl.when(slot // slots == pos)
            def _(out=out, at=at, slot=slot):
                out[at] = amplitudes[slot % slots]


def merge_kernel(tiles, slots, turns, plan, same, came, *outs):
    pos, tile = plan[3, 0], plan[3, 1]
    for at, (turn, out) in enumerate(zip(turns, outs)):
        source = plan[0, (pos ^ (2 * turn)) * tiles + tile] // slots

        @pl.when(source == pos)
        def _(turn=turn, out=out):
            out[...] = same[turn]

        @pl.when(source == (pos ^ 1))
        def _(at=at, out=out):
            out[...] = came[at]


def join(tiles, points, plan, strips, layer, whole, out):
    own, one, two, three = strips
    rows = own.shape[2]
    row, col = slot_at(plan, tiles, 0)
    core, up = plan[3, 1] % 2, plan[3, 1] // 2
    sub = lax.broadcasted_iota(jnp.int32, (rows, points), 0)
    for near, far, at in ((own, two, core), (one, three, 1 - core)):
        low = jnp.where(sub + at * rows >= row, 0, 1)
        for part in range(2):
            whole[part, pl.ds(pl.multiple_of(at * rows, rows), rows)] = jnp.where(
                low == up, near[layer, part].astype(F32), far[layer, part].astype(F32)
            )
    for part in range(2):
        value = pltpu.roll(whole[part], (points - row % points) % points, 0)
        out[part] = pltpu.roll(value, (points - col % points) % points, 1).astype(BF16)


def forward(probes, first, second, tables, kernel, phi, far):
    modes = probes[0].shape[0]
    fields = []
    for probe in probes:
        for mode in range(modes):
            fields.append(fold_rows(*times(*load_complex(probe, mode), *load_complex(first))))
    fields = forward_folded(fields, tables)
    fields = inverse([times(re, im, kernel[0], kernel[1]) for re, im in fields], tables)
    folded = []
    for at, (re, im) in enumerate(fields):
        phi[at, 0], phi[at, 1] = re.astype(BF16), im.astype(BF16)
        folded.append(fold_rows(*times(re, im, *load_complex(second))))
    fields = forward_folded(folded, tables)
    power = None
    for at, (re, im) in enumerate(fields):
        far[at, 0], far[at, 1] = re.astype(BF16), im.astype(BF16)
        square = re * re + im * im
        power = square if power is None else power + square
    return power


def put_by_residue(plan, tiles, points, total, own, other):
    row, col = slot_at(plan, tiles, 0)
    core = plan[3, 1] % 2
    rows = points // 2
    for part in range(2):
        total[part] = pltpu.roll(pltpu.roll(total[part], row % points, 0), col % points, 1)
    for out, at in ((own, core), (other, 1 - core)):
        for part in range(2):
            out[part] = total[part, pl.ds(pl.multiple_of(at * rows, rows), rows)].astype(BF16)


def ahead_kernel(tiles, points, plan, *refs):
    strips, near, beside, across, diagonal, tables_far, kernel_far = refs[:4], *refs[4:10]
    first, second, phi, far, power = refs[10:15]
    mine, tables, kernel, whole, sems = refs[15:]
    copies = fetch((near, tables_far, kernel_far), (mine, tables, kernel), sems)
    join(tiles, points, plan, strips, 0, whole, first)
    join(tiles, points, plan, strips, 1, whole, second)
    for copy in copies:
        copy.wait()
    size = phi.shape[0] // 2
    power[...] = forward((mine, beside), first, second, tables, kernel, phi.at[:size], far.at[:size])
    power[...] += forward((across, diagonal), first, second, tables, kernel, phi.at[size:], far.at[size:])


def back_kernel(tiles, points, slots, plan, *refs):
    power, phi, far, second, tables_far, mover_far = refs[:6]
    arrived = refs[6:10]
    own, other, inner = refs[10:13]
    tables, mover, amplitude, total, ratio, sems = refs[13:]
    copies = fetch((mover_far, tables_far), (mover, tables), sems)
    source = plan[0, plan[3, 0] * tiles + plan[3, 1]] // slots
    for turn, ref in enumerate(arrived):

        @pl.when(((source ^ plan[3, 0]) >> 1) == turn)
        def _(ref=ref):
            amplitude[...] = ref[...]

    for copy in copies:
        copy.wait()
    measured = dot(dot(mover[0], amplitude[...]).astype(BF16), mover[1])
    ratio[...] = 1.0 - measured / jnp.sqrt(power[...] + 1.0)
    total[...] = jnp.zeros_like(total)
    size = phi.shape[0] // 2
    for start in (0, size):
        fields = []
        for at in range(start, start + size):
            re, im = load_complex(far, at)
            fields.append((re * ratio[...], im * ratio[...]))
        fields = inverse(fields, tables)
        for at, (re, im) in enumerate(fields, start):
            grad_re, grad_im = conj_times(*load_complex(phi, at), re, im)
            total[0] += grad_re
            total[1] += grad_im
            inner[at, 0], inner[at, 1] = fold_rows(*conj_times(*load_complex(second), re, im))
    put_by_residue(plan, tiles, points, total, own, other)


def last_kernel(tiles, points, plan, *refs):
    inner, near, beside, across, diagonal, first, tables_far, kernel_far = refs[:8]
    own, other, pair, near_grad, beyond_grad, beside_grad = refs[8:14]
    mine, tables, kernel, total, sems = refs[14:]
    copies = fetch((tables_far, kernel_far, near), (tables, kernel, mine), sems)
    modes = mine.shape[0]
    probes = (mine, beside, across, diagonal)
    grads = (near_grad, beside_grad.at[0], beyond_grad, beside_grad.at[1])
    total[...] = jnp.zeros_like(total)
    for copy in copies:
        copy.wait()
    for start in range(0, tiles, 2):
        which = [(turn, mode) for turn in range(start, start + 2) for mode in range(modes)]
        fields = forward_folded([(inner[t * modes + m, 0], inner[t * modes + m, 1]) for t, m in which], tables)
        fields = inverse([conj_times(kernel[0], kernel[1], re, im) for re, im in fields], tables)
        for (turn, mode), (re, im) in zip(which, fields):
            grad_re, grad_im = conj_times(*load_complex(probes[turn], mode), re, im)
            total[0] += grad_re
            total[1] += grad_im
            re, im = conj_times(*load_complex(first), re, im)
            grads[turn][mode, 0], grads[turn][mode, 1] = re.astype(BF16), im.astype(BF16)
    put_by_residue(plan, tiles, points, total, own, other)
    pair[0] = own[...]
    pair[1] = other[...]


def piece_of(pieces, turn):
    piece = pieces[turn]
    if len(piece.shape) == 3:
        return piece
    return piece[turn - 2]


def place_kernel(tiles, points, plan, *refs):
    pieces, (even, same, odd, canvas) = refs[:tiles], refs[tiles:]
    rows = pieces[0].shape[1]
    core, up = plan[3, 1] % 2, plan[3, 1] // 2
    base = plan[3, 0] // 2 * 2 - 2
    sub = lax.broadcasted_iota(jnp.int32, (rows, points), 0) + core * rows
    lane = lax.broadcasted_iota(jnp.int32, (rows, points), 1)
    canvas[...] = jnp.zeros_like(canvas)
    for turn in range(tiles):
        row, col = slot_at(plan, tiles, turn)
        mine = jnp.where(sub >= row, 0, 1) == up
        early = lane >= col % points
        for part in range(2):
            value = jnp.where(mine, piece_of(pieces, turn)[part].astype(F32), 0.0)
            for step, keep in ((0, early), (1, ~early)):
                at = col // points + step - base
                at = jnp.where((at >= 0) & (at < 6), at, 6)
                canvas[at, part] += jnp.where(keep, value, 0.0)
    same[...] = canvas[2:4]
    up_first = plan[3, 0] // 2 % 2 == 0
    for out, at in ((even, jnp.where(up_first, 4, 0)), (odd, jnp.where(up_first, 0, 4))):
        out[...] = canvas[pl.ds(at, 2)].astype(BF16)


def split_kernel(plan, same, low, high, keep, send):
    x_at = plan[3, 0] % 2
    keep[...] = same[x_at] + low[x_at].astype(F32) + high[x_at].astype(F32)
    other = same[1 - x_at] + low[1 - x_at].astype(F32) + high[1 - x_at].astype(F32)
    send[...] = other.astype(BF16)


def end_kernel(layers, *refs):
    extra, out = refs[-2:]
    for layer in range(layers):
        out[layer] = refs[layer][...] + refs[layers + layer][...].astype(F32) + extra[layer].astype(F32)


def spread_kernel(plan, mine, beyond, came, keep, send):
    pos = plan[3, 0]
    rows = keep.shape[-2]
    for which, near in enumerate((mine, beyond)):
        for turn in range(keep.shape[1]):
            for flip in range(2):
                at = pl.ds(pl.multiple_of((pos ^ (2 * turn + flip)) * rows, rows), rows)
                total = near[:, :, at].astype(F32) + came[which, :, :, at].astype(F32)
                if flip:
                    send[which, turn] = total.astype(BF16)
                else:
                    keep[which, turn] = total


def fold_kernel(near, came, keep, send):
    keep[...] = near[0] + came[0].astype(F32)
    send[...] = (near[1] + came[1].astype(F32)).astype(BF16)


def gather_kernel(near, came, own, *sends):
    own[...] = near[0] + came[0].astype(F32)
    for turn, send in enumerate(sends, 1):
        send[...] = (near[turn] + came[turn].astype(F32)).astype(BF16)


def total_kernel(*refs):
    total = refs[0][...]
    for ref in refs[1:-1]:
        total = total + ref[...].astype(F32)
    refs[-1][...] = total


def turned(value, turn, tiles):
    return lax.ppermute(value, "tile", [(i, i ^ turn) for i in range(tiles)])


def distant_blocks(plan, pieces, tiles, points, groups):
    rows = pieces[0][0].shape[1]
    pos, tile = plan[3, 0], plan[3, 1]
    sub = (jnp.arange(rows, dtype=jnp.int32) + tile % 2 * rows)[:, None]
    lane = jnp.arange(points, dtype=jnp.int32)[None, :]
    block = jnp.arange(groups, dtype=jnp.int32)
    outside = jnp.abs(block // 2 - pos // 2) > 1
    canvas = 0.0
    for turn in range(tiles):
        place = pos * tiles + (tile ^ turn)
        row, col = jnp.take(plan[1], place), jnp.take(plan[2], place)
        mine = jnp.where(sub >= row, 0, 1) == tile // 2
        target = col // points + jnp.where(lane >= col % points, 0, 1)
        keep = outside[:, None, None] & mine[None] & (target[None] == block[:, None, None])
        value = jnp.stack([piece_of(layer, turn) for layer in pieces]).astype(F32)
        canvas = canvas + jnp.where(keep[:, None, None], value[None], 0.0)
    shares = lax.all_to_all(canvas.astype(BF16), "pos", split_axis=0, concat_axis=0, tiled=True)
    return jnp.sum(shares.astype(F32), axis=0).astype(BF16)


def on_device_by_slot(probe_modes, object_slices, amplitudes, scan_offsets, slot_counts):
    groups, tiles = lax.axis_size("pos"), lax.axis_size("tile")
    slots, points = amplitudes.shape[0], amplitudes.shape[-1]
    layers, rows = object_slices.shape[0], object_slices.shape[2]
    modes = probe_modes.shape[0]
    tables, kernel, mover = (jnp.asarray(t) for t in split_tables(points))
    field = (2, points, points)

    low = probe_modes.astype(BF16)
    low, scan_offsets = lax.optimization_barrier((low, scan_offsets))
    across = turned(low, 2, tiles)
    beside = turned(low, 1, tiles)
    shot = (points, points)
    outs = call(
        functools.partial(first_kernel, groups, tiles, points),
        (slot_counts, scan_offsets, object_slices, amplitudes),
        [SM, VM, HB, HB],
        [((layers, 2, rows, points), BF16)] * tiles
        + [((groups // 2, *shot), BF16)] * 2
        + [((8, 128), jnp.int32)],
        [
            pltpu.SMEM((8, 128), jnp.int32),
            pltpu.VMEM(object_slices.shape, BF16),
            pltpu.VMEM(amplitudes.shape, BF16),
            pltpu.SemaphoreType.DMA((3,)),
        ],
        name="first",
        us=0.1,
        mib=16,
    )
    (*cut, same, far, plan) = outs
    across, cut = lax.optimization_barrier((across, cut))
    aside = [(i, i ^ 1) for i in range(groups)]
    merged = call(
        functools.partial(merge_kernel, tiles, slots, range(groups // 2)),
        (plan, same, lax.ppermute(far, "pos", aside)),
        [SM, VM, VM],
        [(shot, BF16)] * (groups // 2),
        name="merge",
    )
    arrived = [merged[0]] + [
        lax.ppermute(merged[turn], "pos", [(i, i ^ (2 * turn)) for i in range(groups)])
        for turn in range(1, groups // 2)
    ]
    strips = [cut[0]] + [turned(cut[turn], turn, tiles) for turn in range(1, tiles)]
    probes = [probe_modes, beside, across, turned(across, 1, tiles)]
    half = ((2, points // 2, points), BF16)
    stack = (tiles * modes, *field)
    first, second, phi, far, power = call(
        functools.partial(ahead_kernel, tiles, points),
        (plan, *strips, *probes, tables, kernel),
        [SM] + [VK] * tiles + [HB] + [VK] * 3 + [HB] * 2,
        [(field, BF16), (field, BF16), (stack, BF16), (stack, BF16), ((points, points), F32)],
        [
            pltpu.VMEM(probe_modes.shape, F32),
            pltpu.VMEM(tables.shape, BF16),
            pltpu.VMEM(kernel.shape, F32),
            pltpu.VMEM(field, F32),
            pltpu.SemaphoreType.DMA((3,)),
        ],
        name="ahead",
        us=0.1,
        mib=24,
        keep=range(5),
    )
    own, other, inner = call(
        functools.partial(back_kernel, tiles, points, slots),
        (plan, power, phi, far, second, tables, mover, *arrived),
        [SM] + [VK] * 4 + [HB] * 2 + [VM] * len(arrived),
        [half, half, (stack, BF16)],
        [
            pltpu.VMEM(tables.shape, BF16),
            pltpu.VMEM(mover.shape, BF16),
            pltpu.VMEM((points, points), BF16),
            pltpu.VMEM(field, F32),
            pltpu.VMEM((points, points), F32),
            pltpu.SemaphoreType.DMA((2,)),
        ],
        name="back",
        us=0.1,
        mib=24,
        keep=(2,),
    )
    pieces = [None] * layers
    pieces[1] = [own] + [turned(v, turn, tiles) for turn, v in ((1, other), (2, own), (3, other))]
    own, other, pair, mine, beyond, beside = call(
        functools.partial(last_kernel, tiles, points),
        (plan, inner, *probes, first, tables, kernel),
        [SM, VK, HB] + [VK] * 4 + [HB] * 2,
        [half, half, ((2, *half[0]), BF16)] + [((modes, *field), BF16)] * 2 + [((2, modes, *field), BF16)],
        [
            pltpu.VMEM(probe_modes.shape, F32),
            pltpu.VMEM(tables.shape, BF16),
            pltpu.VMEM(kernel.shape, F32),
            pltpu.VMEM(field, F32),
            pltpu.SemaphoreType.DMA((3,)),
        ],
        name="last",
        us=0.1,
        mib=24,
    )
    pieces[1], own, other, pair, beside = lax.optimization_barrier((pieces[1], own, other, pair, beside))
    pair = turned(pair, 2, tiles)
    pieces[0] = [own, turned(other, 1, tiles), pair, turned(pair, 1, tiles)]
    share = (groups // 2, modes, 2, points // groups, points)
    keep, send = call(
        spread_kernel,
        (plan, mine, beyond, turned(beside, 1, tiles)),
        [SM] + [VM] * 3,
        [((2, *share), F32), ((2, *share), BF16)],
        name="spread",
    )
    keep, send = call(
        fold_kernel,
        (keep, lax.ppermute(send, "pos", aside)),
        [VM] * 2,
        [(share, F32), (share, BF16)],
        name="fold",
    )
    own, *sends = call(
        gather_kernel,
        (keep, turned(send, 2, tiles)),
        [VM] * 2,
        [(share[1:], F32)] + [(share[1:], BF16)] * (groups // 2 - 1),
        name="gather",
    )
    came = [
        lax.ppermute(send, "pos", [(i, i ^ (2 * turn)) for i in range(groups)]) for turn, send in enumerate(sends, 1)
    ]
    (probe_grad,) = call(total_kernel, (own, *came), [VM] * (1 + len(came)), [(share[1:], F32)], name="total")

    block = (2, rows, points)
    keeps, swapped = [None] * layers, [None] * layers
    for layer in reversed(range(layers)):
        even, same, odd = call(
            functools.partial(place_kernel, tiles, points),
            (plan, *pieces[layer]),
            [SM] + [VM] * tiles,
            [((2, *block), BF16), ((2, *block), F32), ((2, *block), BF16)],
            [pltpu.VMEM((7, *block), F32)],
            name="place",
        )
        if layer:
            pass
        pairs = [(i, i ^ 2) for i in range(groups)]
        low_in = lax.ppermute(even, "pos", pairs)
        pairs = [(i, i + 2 if i // 2 % 2 else i - 2) for i in range(2, groups - 2)]
        high_in = lax.ppermute(odd, "pos", pairs)
        if layer == 0:
            pieces, low_in = lax.optimization_barrier((pieces, low_in))
        if layer:
            pieces[0], low_in = lax.optimization_barrier((pieces[0], low_in))
        keeps[layer], send = call(
            split_kernel,
            (plan, same, low_in, high_in),
            [SM] + [VM] * 3,
            [(block, F32), (block, BF16)],
            name="split",
        )
        swapped[layer] = lax.ppermute(send, "pos", [(i, i ^ 1) for i in range(groups)])
    extra = lax.cond(
        plan[3, 2] > 0,
        lambda p: distant_blocks(plan, p, tiles, points, groups),
        lambda p: jnp.zeros((layers, *block), BF16),
        pieces,
    )
    (object_grad,) = call(
        functools.partial(end_kernel, layers),
        (*keeps, *swapped, extra),
        [VM] * (2 * layers + 1),
        [((layers, *block), F32)],
        name="end",
    )
    return object_grad, probe_grad


def make_tables(points):
    counter = jnp.arange(points, dtype=jnp.int32)
    product = counter[:, None] * counter[None, :] % points
    angle = 2.0 * jnp.pi / points * product.astype(jnp.float32)
    factor = 1.0 / jnp.sqrt(jnp.float32(points))
    table_re = (jnp.cos(angle) * factor).astype(jnp.bfloat16)
    table_im = (-jnp.sin(angle) * factor).astype(jnp.bfloat16)
    shifted = ((counter + points // 2) % points - points // 2).astype(jnp.float32)
    phase = (
        jnp.pi
        * FRESNEL
        / points
        * (shifted[:, None] * shifted[:, None] + shifted[None, :] * shifted[None, :])
    )
    kernel = jnp.stack([jnp.cos(phase), -jnp.sin(phase)])
    return (table_re, table_im, kernel)


def times_complex(first, second):
    real_part = (
        first[..., 0, :, :] * second[..., 0, :, :] - first[..., 1, :, :] * second[..., 1, :, :]
    )
    imag_part = (
        first[..., 0, :, :] * second[..., 1, :, :] + first[..., 1, :, :] * second[..., 0, :, :]
    )
    return jnp.stack([real_part, imag_part], axis=-3)


def conjugate(values):
    return jnp.stack([values[..., 0, :, :], -values[..., 1, :, :]], axis=-3)


def transform_many(values, table_re, table_im):
    tables = jnp.stack([table_re, table_im])
    lowered = values.astype(jnp.bfloat16)
    first = jnp.einsum("gab,nmtbc->nmgtac", tables, lowered, preferred_element_type=jnp.float32)
    middle = jnp.stack(
        [first[:, :, 0, 0] - first[:, :, 1, 1], first[:, :, 0, 1] + first[:, :, 1, 0]], axis=2
    ).astype(jnp.bfloat16)
    second = jnp.einsum("nmtab,gbc->nmtgac", middle, tables, preferred_element_type=jnp.float32)
    return jnp.stack(
        [second[:, :, 0, 0] - second[:, :, 1, 1], second[:, :, 0, 1] + second[:, :, 1, 0]], axis=2
    )


def propagate_many(values, table_re, table_im, kernel):
    return transform_many(
        times_complex(transform_many(values, table_re, table_im), kernel), table_re, -table_im
    )


def window_anchor(place):
    zero_index = jnp.int32(0)
    return (zero_index, zero_index, place[0], place[1])


def on_device_by_mode(probe_modes, object_slices, amplitudes, scan_offsets, slot_counts):
    group = lax.axis_index("pos")
    groups = lax.axis_size("pos")
    tile_at = lax.axis_index("tile")
    strips = lax.axis_size("tile")
    slots = amplitudes.shape[0]
    points = amplitudes.shape[-1]
    layers = object_slices.shape[0]
    strip_rows = object_slices.shape[2]
    starts = jnp.cumsum(slot_counts) - slot_counts
    share = slots // 2
    wanted = jnp.arange(groups * share, dtype=jnp.int32)
    within = wanted - starts[group]
    usable = (within >= 0) & (within < slot_counts[group])
    picked = jnp.take(amplitudes, jnp.clip(within, 0, slots - 1), axis=0)
    outgoing = jnp.where(usable[:, None, None], picked, jnp.zeros_like(picked))
    arrived_rows = lax.all_to_all(outgoing, "pos", split_axis=0, concat_axis=0, tiled=True)
    mine = group * share + jnp.arange(share, dtype=jnp.int32)
    source = jnp.sum((starts[None, :] <= mine[:, None]).astype(jnp.int32), axis=1) - 1
    amplitude = jnp.take(arrived_rows, source * share + jnp.arange(share, dtype=jnp.int32), axis=0)
    places = jnp.take(scan_offsets, source * slots + mine - starts[source], axis=0)
    alive = jnp.ones((share,), jnp.float32)
    padded = jnp.pad(object_slices, ((0, 0), (0, 0), (points, points), (0, 0)))

    def cut_piece(place):
        local_row = jnp.clip(place[0] - tile_at * strip_rows + points, 0, strip_rows + points)
        shifted_place = jnp.stack([local_row, place[1]])
        return lax.dynamic_slice(padded, window_anchor(shifted_place), (layers, 2, points, points))

    pieces = jax.vmap(cut_piece)(places).astype(jnp.float32)
    windows = lax.psum(pieces.astype(jnp.bfloat16), "tile").astype(jnp.float32)
    table_re, table_im, kernel = make_tables(points)
    kernel_conj = conjugate(kernel)
    current = times_complex(probe_modes[None], windows[:, None, 0])
    layer_at = 1
    arrived = propagate_many(current, table_re, table_im, kernel)
    entering = [arrived]
    current = times_complex(arrived, windows[:, None, layer_at])
    far_field = transform_many(current, table_re, table_im)
    partial_power = jnp.sum(far_field * far_field, axis=(1, 2))
    power = lax.psum(partial_power.astype(jnp.bfloat16), "tile").astype(jnp.float32)
    ratio = (1.0 - amplitude.astype(jnp.float32) / jnp.sqrt(power + 1.0)) * alive[:, None, None]
    incoming = transform_many(ratio[:, None, None] * far_field, table_re, -table_im)
    object_terms = [None] * layers
    layer_at = 1
    object_terms[layer_at] = jnp.sum(
        times_complex(conjugate(entering[layer_at - 1]), incoming), axis=1
    )
    incoming = propagate_many(
        times_complex(conjugate(windows[:, None, layer_at]), incoming),
        table_re,
        table_im,
        kernel_conj,
    )
    object_terms[0] = jnp.sum(times_complex(conjugate(probe_modes[None]), incoming), axis=1)
    probe_term = jnp.sum(times_complex(conjugate(windows[:, None, 0]), incoming), axis=0)
    slot_grads = jnp.stack(object_terms, axis=1)
    canvas = jnp.zeros((layers, 2, strip_rows * strips, object_slices.shape[3]), jnp.float32)

    def deposit(canvas, packed):
        place, term = packed
        anchor = window_anchor(place)
        current_part = lax.dynamic_slice(canvas, anchor, term.shape)
        return (lax.dynamic_update_slice(canvas, current_part + term, anchor), None)

    canvas, unused = lax.scan(deposit, canvas, (places, slot_grads))
    column_part = lax.psum_scatter(
        canvas.astype(jnp.bfloat16), "pos", scatter_dimension=3, tiled=True
    )
    object_grad = lax.psum_scatter(column_part, "tile", scatter_dimension=2, tiled=True).astype(
        jnp.float32
    )
    probe_grad = lax.psum_scatter(
        probe_term.astype(jnp.bfloat16), "pos", scatter_dimension=2, tiled=True
    ).astype(jnp.float32)
    return (object_grad, probe_grad)


def solution(mesh):
    in_specs = (
        P("tile", None, None, None),
        P(None, None, "tile", None),
        P("pos", None, None),
        P(),
        P(),
    )
    out_specs = (P(None, None, "tile", "pos"), P("tile", None, "pos", None))
    by_slot = mesh.shape["tile"] == 4 and mesh.shape["pos"] == 8
    return jax.shard_map(
        on_device_by_slot if by_slot else on_device_by_mode,
        mesh=mesh,
        in_specs=in_specs,
        out_specs=out_specs,
        check_vma=False,
    )
```

```python
import functools

import jax
import jax.numpy as jnp
import ml_dtypes
import numpy as np
from jax import lax
from jax.experimental import pallas as pl
from jax.experimental.pallas import tpu as pltpu
from jax.sharding import PartitionSpec as P

FRESNEL = 0.37
BF16 = jnp.bfloat16
F32 = jnp.float32


def split_tables(points):
    half = points // 2
    counter = np.arange(points)
    angle = (2.0 * np.pi / points * (counter[:, None] * counter[None, :] % points)).astype(np.float32)
    factor = np.float32(1.0) / np.sqrt(np.float32(points))
    table_re = np.cos(angle) * factor
    table_im = -np.sin(angle) * factor

    def stacked(rows):
        re, im = table_re[rows, :half], table_im[rows, :half]
        return np.block([[re, -im], [im, re]]).astype(ml_dtypes.bfloat16)

    even, odd = stacked(slice(0, None, 2)), stacked(slice(1, None, 2))
    tables = np.stack([even, odd, even.T, odd.T])
    order = np.concatenate([counter[0::2], counter[1::2]])
    shifted = ((order + half) % points - half).astype(np.float64)
    phase = np.pi * FRESNEL / points * (shifted[:, None] ** 2 + shifted[None, :] ** 2)
    kernel = np.stack([np.cos(phase), -np.sin(phase)]).astype(np.float32)
    mover = np.zeros((points, points), np.float32)
    mover[counter, order] = 1.0
    mover = np.stack([mover, mover.T]).astype(ml_dtypes.bfloat16)
    return tables, kernel, mover


def dot(a, b):
    return jnp.dot(a, b, preferred_element_type=F32)


def fold_rows(re, im):
    half = re.shape[0] // 2
    top = jnp.concatenate([re[:half], im[:half]], axis=0)
    bottom = jnp.concatenate([re[half:], im[half:]], axis=0)
    return (top + bottom).astype(BF16), (top - bottom).astype(BF16)


def join_parts(values, axis):
    return jnp.concatenate(values, axis=axis)


def forward_folded(folded, tables):
    half = folded[0][0].shape[0] // 2
    evens = [dot(tables[0], even) for even, _ in folded]
    odds = [dot(tables[1], odd) for _, odd in folded]
    lanes = []
    for even, odd in zip(evens, odds):
        re = join_parts([even[:half], odd[:half]], 0)
        im = join_parts([even[half:], odd[half:]], 0)
        left = join_parts([re[:, :half], im[:, :half]], 1)
        right = join_parts([re[:, half:], im[:, half:]], 1)
        lanes.append(((left + right).astype(BF16), (left - right).astype(BF16)))
    evens = [dot(even, tables[2]) for even, _ in lanes]
    odds = [dot(odd, tables[3]) for _, odd in lanes]
    return [
        (join_parts([even[:, :half], odd[:, :half]], 1), join_parts([even[:, half:], odd[:, half:]], 1))
        for even, odd in zip(evens, odds)
    ]


def inverse(fields, tables):
    half = fields[0][0].shape[0] // 2
    low = [(re.astype(BF16), im.astype(BF16)) for re, im in fields]
    evens = [dot(tables[2], join_parts([re[:half], im[:half]], 0)) for re, im in low]
    odds = [dot(tables[3], join_parts([re[half:], im[half:]], 0)) for re, im in low]
    lanes = []
    for even, odd in zip(evens, odds):
        total, rest = (even + odd).astype(BF16), (even - odd).astype(BF16)
        re = join_parts([total[:half], rest[:half]], 0)
        im = join_parts([total[half:], rest[half:]], 0)
        lanes.append((join_parts([re[:, :half], im[:, :half]], 1), join_parts([re[:, half:], im[:, half:]], 1)))
    evens = [dot(even, tables[0]) for even, _ in lanes]
    odds = [dot(odd, tables[1]) for _, odd in lanes]
    out = []
    for even, odd in zip(evens, odds):
        total, rest = even + odd, even - odd
        re = join_parts([total[:, :half], rest[:, :half]], 1)
        im = join_parts([total[:, half:], rest[:, half:]], 1)
        out.append((re, im))
    return out


def times(a_re, a_im, b_re, b_im):
    return a_re * b_re - a_im * b_im, a_re * b_im + a_im * b_re


def conj_times(a_re, a_im, b_re, b_im):
    return a_re * b_re + a_im * b_im, a_re * b_im - a_im * b_re


def load_complex(ref, *lead):
    return ref[(*lead, 0)].astype(F32), ref[(*lead, 1)].astype(F32)


VM = pl.BlockSpec(memory_space=pltpu.VMEM)
SM = pl.BlockSpec(memory_space=pltpu.SMEM)
HB = pl.BlockSpec(memory_space=pltpu.HBM)
VK = object()


def call(body, inputs, specs, outs, scratch=(), out_specs=None, name=None, us=0.1, mib=8, keep=()):
    return pl.pallas_call(
        body,
        out_shape=[
            pltpu.VMEM(shape, dtype) if at in keep else jax.ShapeDtypeStruct(shape, dtype)
            for at, (shape, dtype) in enumerate(outs)
        ],
        in_specs=[VM if spec is VK else spec for spec in specs],
        out_specs=[VM] * len(outs) if out_specs is None else out_specs,
        scratch_shapes=list(scratch),
        compiler_params=pltpu.CompilerParams(vmem_limit_bytes=mib * 1024 * 1024),
        cost_estimate=pl.CostEstimate(flops=int(us * 1e9), bytes_accessed=int(us * 3e6), transcendentals=0),
        name=name,
    )(
        *(
            pltpu.with_memory_space_constraint(value, pltpu.VMEM) if spec is VK else value
            for value, spec in zip(inputs, specs)
        )
    )


def fetch(sources, targets, sems):
    copies = [pltpu.make_async_copy(s, t, sems.at[at]) for at, (s, t) in enumerate(zip(sources, targets))]
    for copy in copies:
        copy.start()
    return copies


def slot_at(plan, tiles, turn):
    place = plan[3, 0] * tiles + (plan[3, 1] ^ turn)
    return plan[1, place], plan[2, place]


def first_kernel(groups, tiles, points, counts, offsets, strip_far, amplitudes_far, *refs):
    strips = refs[:tiles]
    same, other_x, plan_out, plan, strip, amplitudes, sems = refs[tiles:]
    layers, rows = strip.shape[0], strip.shape[2]
    slots = amplitudes.shape[0]
    n = offsets.shape[0]
    strip_copy = pltpu.make_async_copy(strip_far, strip, sems.at[1])
    strip_copy.start()
    amplitude_copy = pltpu.make_async_copy(amplitudes_far, amplitudes, sems.at[2])
    amplitude_copy.start()
    pos, tile = lax.axis_index("pos"), lax.axis_index("tile")
    width = plan_out.shape[1]

    number = lax.broadcasted_iota(jnp.int32, (n, 1), 0)
    live = jnp.zeros((n, 1), jnp.int32)
    for group in range(groups):
        live += jnp.where((number >= group * slots) & (number < group * slots + counts[group]), 1, 0)
    row, col = offsets[:, 0:1].astype(F32), offsets[:, 1:2].astype(F32)
    number = number.astype(F32)
    key = jnp.where(live > 0, col, float(1 << 12)) * n + number
    square = (n, n)
    eye = lax.broadcasted_iota(jnp.int32, square, 0) == lax.broadcasted_iota(jnp.int32, square, 1)
    across = jnp.sum(jnp.where(eye, key, 0.0), axis=0, keepdims=True)
    rank = jnp.sum(jnp.where(across < key, 1.0, 0.0), axis=1, keepdims=True).astype(jnp.int32)
    here = lax.broadcasted_iota(jnp.int32, (n, width), 1) == rank
    chosen = [
        jnp.sum(jnp.where(here, value, 0.0), axis=0, keepdims=True).astype(jnp.int32)
        for value in (number, row, col)
    ]
    lane = lax.broadcasted_iota(jnp.int32, (1, width), 1)
    outer = 2 * points
    lowest = jnp.maximum(sum(jnp.where(lane >= i * 2 * tiles, 1, 0) for i in range(1, groups // 2)) - 1, 0)
    far = (chosen[2] < lowest * outer) | (chosen[2] + points > (lowest + jnp.where(lane < 2 * tiles, 2, 3)) * outer)
    distant = jnp.max(jnp.where(far & (lane < groups * slots // 2), 1.0, 0.0), axis=1, keepdims=True)
    for at, value in enumerate(chosen):
        plan_out[at : at + 1, :] = value
    plan_out[3:4, :] = jnp.where(
        lane == 0, pos, jnp.where(lane == 1, tile, jnp.where(lane == 2, distant.astype(jnp.int32), 0))
    )
    plan_out[4:8, :] = jnp.zeros((4, width), jnp.int32)
    copy = pltpu.make_async_copy(plan_out, plan, sems.at[0])
    copy.start()
    copy.wait()
    strip_copy.wait()

    blocks = strip.shape[-1] // points
    lane = lax.broadcasted_iota(jnp.int32, (rows, points), 1)
    for turn in range(tiles):
        _, col = slot_at(plan, tiles, turn)
        block = col // points
        later = jnp.minimum(block + 1, blocks - 1)
        keep = lane >= col % points
        for layer in range(layers):
            for part in range(2):
                here = strip[layer, part, :, pl.ds(pl.multiple_of(block * points, points), points)]
                there = strip[layer, part, :, pl.ds(pl.multiple_of(later * points, points), points)]
                strips[turn][layer, part] = jnp.where(
                    keep, here.astype(F32), there.astype(F32)
                ).astype(BF16)
    amplitude_copy.wait()
    for turn in range(groups // 2):
        for flip, out, at in ((0, same, turn), (1, other_x, turn)):
            slot = plan[0, (pos ^ (2 * turn + flip)) * tiles + tile]

            @pl.when(slot // slots == pos)
            def _(out=out, at=at, slot=slot):
                out[at] = amplitudes[slot % slots]


def merge_kernel(tiles, slots, turns, plan, same, came, *outs):
    pos, tile = plan[3, 0], plan[3, 1]
    for at, (turn, out) in enumerate(zip(turns, outs)):
        source = plan[0, (pos ^ (2 * turn)) * tiles + tile] // slots

        @pl.when(source == pos)
        def _(turn=turn, out=out):
            out[...] = same[turn]

        @pl.when(source == (pos ^ 1))
        def _(at=at, out=out):
            out[...] = came[at]


def join(tiles, points, plan, strips, layer, whole, out):
    own, one, two, three = strips
    rows = own.shape[2]
    row, col = slot_at(plan, tiles, 0)
    core, up = plan[3, 1] % 2, plan[3, 1] // 2
    sub = lax.broadcasted_iota(jnp.int32, (rows, points), 0)
    for near, far, at in ((own, two, core), (one, three, 1 - core)):
        low = jnp.where(sub + at * rows >= row, 0, 1)
        for part in range(2):
            whole[part, pl.ds(pl.multiple_of(at * rows, rows), rows)] = jnp.where(
                low == up, near[layer, part].astype(F32), far[layer, part].astype(F32)
            )
    for part in range(2):
        value = pltpu.roll(whole[part], (points - row % points) % points, 0)
        out[part] = pltpu.roll(value, (points - col % points) % points, 1).astype(BF16)


def forward(probes, first, second, tables, kernel, phi, far):
    modes = probes[0].shape[0]
    fields = []
    for probe in probes:
        for mode in range(modes):
            fields.append(fold_rows(*times(*load_complex(probe, mode), *load_complex(first))))
    fields = forward_folded(fields, tables)
    fields = inverse([times(re, im, kernel[0], kernel[1]) for re, im in fields], tables)
    folded = []
    for at, (re, im) in enumerate(fields):
        phi[at, 0], phi[at, 1] = re.astype(BF16), im.astype(BF16)
        folded.append(fold_rows(*times(re, im, *load_complex(second))))
    fields = forward_folded(folded, tables)
    power = None
    for at, (re, im) in enumerate(fields):
        far[at, 0], far[at, 1] = re.astype(BF16), im.astype(BF16)
        square = re * re + im * im
        power = square if power is None else power + square
    return power


def put_by_residue(plan, tiles, points, total, own, other):
    row, col = slot_at(plan, tiles, 0)
    core = plan[3, 1] % 2
    rows = points // 2
    for part in range(2):
        total[part] = pltpu.roll(pltpu.roll(total[part], row % points, 0), col % points, 1)
    for out, at in ((own, core), (other, 1 - core)):
        for part in range(2):
            out[part] = total[part, pl.ds(pl.multiple_of(at * rows, rows), rows)].astype(BF16)


def ahead_kernel(tiles, points, plan, *refs):
    strips, near, beside, across, diagonal, tables_far, kernel_far = refs[:4], *refs[4:10]
    first, second, phi, far, power = refs[10:15]
    mine, tables, kernel, whole, sems = refs[15:]
    copies = fetch((near, tables_far, kernel_far), (mine, tables, kernel), sems)
    join(tiles, points, plan, strips, 0, whole, first)
    join(tiles, points, plan, strips, 1, whole, second)
    for copy in copies:
        copy.wait()
    size = phi.shape[0] // 2
    power[...] = forward((mine, beside), first, second, tables, kernel, phi.at[:size], far.at[:size])
    power[...] += forward((across, diagonal), first, second, tables, kernel, phi.at[size:], far.at[size:])


def back_kernel(tiles, points, slots, plan, *refs):
    power, phi, far, second, tables_far, mover_far = refs[:6]
    arrived = refs[6:10]
    own, other, inner = refs[10:13]
    tables, mover, amplitude, total, ratio, sems = refs[13:]
    copies = fetch((mover_far, tables_far), (mover, tables), sems)
    source = plan[0, plan[3, 0] * tiles + plan[3, 1]] // slots
    for turn, ref in enumerate(arrived):

        @pl.when(((source ^ plan[3, 0]) >> 1) == turn)
        def _(ref=ref):
            amplitude[...] = ref[...]

    for copy in copies:
        copy.wait()
    measured = dot(dot(mover[0], amplitude[...]).astype(BF16), mover[1])
    ratio[...] = 1.0 - measured / jnp.sqrt(power[...] + 1.0)
    total[...] = jnp.zeros_like(total)
    size = phi.shape[0]
    for start in (0,):
        fields = []
        for at in range(start, start + size):
            re, im = load_complex(far, at)
            fields.append((re * ratio[...], im * ratio[...]))
        fields = inverse(fields, tables)
        for at, (re, im) in enumerate(fields, start):
            grad_re, grad_im = conj_times(*load_complex(phi, at), re, im)
            total[0] += grad_re
            total[1] += grad_im
            inner[at, 0], inner[at, 1] = fold_rows(*conj_times(*load_complex(second), re, im))
    put_by_residue(plan, tiles, points, total, own, other)


def last_kernel(tiles, points, plan, *refs):
    inner, near, beside, across, diagonal, first, tables_far, kernel_far = refs[:8]
    own, other, pair, near_grad, beyond_grad, beside_grad = refs[8:14]
    mine, tables, kernel, total, sems = refs[14:]
    copies = fetch((tables_far, kernel_far, near), (tables, kernel, mine), sems)
    modes = mine.shape[0]
    probes = (mine, beside, across, diagonal)
    grads = (near_grad, beside_grad.at[0], beyond_grad, beside_grad.at[1])
    total[...] = jnp.zeros_like(total)
    for copy in copies:
        copy.wait()
    for start in range(0, tiles, tiles):
        which = [(turn, mode) for turn in range(start, start + tiles) for mode in range(modes)]
        fields = forward_folded([(inner[t * modes + m, 0], inner[t * modes + m, 1]) for t, m in which], tables)
        fields = inverse([conj_times(kernel[0], kernel[1], re, im) for re, im in fields], tables)
        for (turn, mode), (re, im) in zip(which, fields):
            grad_re, grad_im = conj_times(*load_complex(probes[turn], mode), re, im)
            total[0] += grad_re
            total[1] += grad_im
            re, im = conj_times(*load_complex(first), re, im)
            grads[turn][mode, 0], grads[turn][mode, 1] = re.astype(BF16), im.astype(BF16)
    put_by_residue(plan, tiles, points, total, own, other)
    pair[0] = own[...]
    pair[1] = other[...]


def piece_of(pieces, turn):
    piece = pieces[turn]
    if len(piece.shape) == 3:
        return piece
    return piece[turn - 2]


def place_kernel(tiles, points, plan, *refs):
    pieces, (even, same, odd, canvas) = refs[:tiles], refs[tiles:]
    rows = pieces[0].shape[1]
    core, up = plan[3, 1] % 2, plan[3, 1] // 2
    base = plan[3, 0] // 2 * 2 - 2
    sub = lax.broadcasted_iota(jnp.int32, (rows, points), 0) + core * rows
    lane = lax.broadcasted_iota(jnp.int32, (rows, points), 1)
    canvas[...] = jnp.zeros_like(canvas)
    for turn in range(tiles):
        row, col = slot_at(plan, tiles, turn)
        mine = jnp.where(sub >= row, 0, 1) == up
        early = lane >= col % points
        for part in range(2):
            value = jnp.where(mine, piece_of(pieces, turn)[part].astype(F32), 0.0)
            for step, keep in ((0, early), (1, ~early)):
                at = col // points + step - base
                at = jnp.where((at >= 0) & (at < 6), at, 6)
                canvas[at, part] += jnp.where(keep, value, 0.0)
    same[...] = canvas[2:4]
    up_first = plan[3, 0] // 2 % 2 == 0
    for out, at in ((even, jnp.where(up_first, 4, 0)), (odd, jnp.where(up_first, 0, 4))):
        out[...] = canvas[pl.ds(at, 2)].astype(BF16)


def split_kernel(plan, same, low, high, keep, send):
    x_at = plan[3, 0] % 2
    keep[...] = same[x_at] + low[x_at].astype(F32) + high[x_at].astype(F32)
    other = same[1 - x_at] + low[1 - x_at].astype(F32) + high[1 - x_at].astype(F32)
    send[...] = other.astype(BF16)


def end_kernel(layers, *refs):
    extra, out = refs[-2:]
    for layer in range(layers):
        out[layer] = refs[layer][...] + refs[layers + layer][...].astype(F32) + extra[layer].astype(F32)


def spread_kernel(plan, mine, beyond, came, keep, send):
    pos = plan[3, 0]
    rows = keep.shape[-2]
    for which, near in enumerate((mine, beyond)):
        for turn in range(keep.shape[1]):
            for flip in range(2):
                at = pl.ds(pl.multiple_of((pos ^ (2 * turn + flip)) * rows, rows), rows)
                total = near[:, :, at].astype(F32) + came[which, :, :, at].astype(F32)
                if flip:
                    send[which, turn] = total.astype(BF16)
                else:
                    keep[which, turn] = total


def fold_kernel(near, came, keep, send):
    keep[...] = near[0] + came[0].astype(F32)
    send[...] = (near[1] + came[1].astype(F32)).astype(BF16)


def gather_kernel(near, came, own, *sends):
    own[...] = near[0] + came[0].astype(F32)
    for turn, send in enumerate(sends, 1):
        send[...] = (near[turn] + came[turn].astype(F32)).astype(BF16)


def total_kernel(*refs):
    total = refs[0][...]
    for ref in refs[1:-1]:
        total = total + ref[...].astype(F32)
    refs[-1][...] = total


def turned(value, turn, tiles):
    return lax.ppermute(value, "tile", [(i, i ^ turn) for i in range(tiles)])


def distant_blocks(plan, pieces, tiles, points, groups):
    rows = pieces[0][0].shape[1]
    pos, tile = plan[3, 0], plan[3, 1]
    sub = (jnp.arange(rows, dtype=jnp.int32) + tile % 2 * rows)[:, None]
    lane = jnp.arange(points, dtype=jnp.int32)[None, :]
    block = jnp.arange(groups, dtype=jnp.int32)
    outside = jnp.abs(block // 2 - pos // 2) > 1
    canvas = 0.0
    for turn in range(tiles):
        place = pos * tiles + (tile ^ turn)
        row, col = jnp.take(plan[1], place), jnp.take(plan[2], place)
        mine = jnp.where(sub >= row, 0, 1) == tile // 2
        target = col // points + jnp.where(lane >= col % points, 0, 1)
        keep = outside[:, None, None] & mine[None] & (target[None] == block[:, None, None])
        value = jnp.stack([piece_of(layer, turn) for layer in pieces]).astype(F32)
        canvas = canvas + jnp.where(keep[:, None, None], value[None], 0.0)
    shares = lax.all_to_all(canvas.astype(BF16), "pos", split_axis=0, concat_axis=0, tiled=True)
    return jnp.sum(shares.astype(F32), axis=0).astype(BF16)


def on_device_by_slot(probe_modes, object_slices, amplitudes, scan_offsets, slot_counts):
    groups, tiles = lax.axis_size("pos"), lax.axis_size("tile")
    slots, points = amplitudes.shape[0], amplitudes.shape[-1]
    layers, rows = object_slices.shape[0], object_slices.shape[2]
    modes = probe_modes.shape[0]
    tables, kernel, mover = (jnp.asarray(t) for t in split_tables(points))
    field = (2, points, points)

    low = probe_modes.astype(BF16)
    low, scan_offsets = lax.optimization_barrier((low, scan_offsets))
    across = turned(low, 2, tiles)
    beside = turned(low, 1, tiles)
    shot = (points, points)
    outs = call(
        functools.partial(first_kernel, groups, tiles, points),
        (slot_counts, scan_offsets, object_slices, amplitudes),
        [SM, VM, HB, HB],
        [((layers, 2, rows, points), BF16)] * tiles
        + [((groups // 2, *shot), BF16)] * 2
        + [((8, 128), jnp.int32)],
        [
            pltpu.SMEM((8, 128), jnp.int32),
            pltpu.VMEM(object_slices.shape, BF16),
            pltpu.VMEM(amplitudes.shape, BF16),
            pltpu.SemaphoreType.DMA((3,)),
        ],
        name="first",
        us=0.1,
        mib=16,
    )
    (*cut, same, far, plan) = outs
    across, cut = lax.optimization_barrier((across, cut))
    aside = [(i, i ^ 1) for i in range(groups)]
    merged = call(
        functools.partial(merge_kernel, tiles, slots, range(groups // 2)),
        (plan, same, lax.ppermute(far, "pos", aside)),
        [SM, VM, VM],
        [(shot, BF16)] * (groups // 2),
        name="merge",
    )
    arrived = [merged[0]] + [
        lax.ppermute(merged[turn], "pos", [(i, i ^ (2 * turn)) for i in range(groups)])
        for turn in range(1, groups // 2)
    ]
    strips = [cut[0]] + [turned(cut[turn], turn, tiles) for turn in range(1, tiles)]
    probes = [probe_modes, beside, across, turned(across, 1, tiles)]
    half = ((2, points // 2, points), BF16)
    stack = (tiles * modes, *field)
    first, second, phi, far, power = call(
        functools.partial(ahead_kernel, tiles, points),
        (plan, *strips, *probes, tables, kernel),
        [SM] + [VK] * tiles + [HB] + [VK] * 3 + [HB] * 2,
        [(field, BF16), (field, BF16), (stack, BF16), (stack, BF16), ((points, points), F32)],
        [
            pltpu.VMEM(probe_modes.shape, F32),
            pltpu.VMEM(tables.shape, BF16),
            pltpu.VMEM(kernel.shape, F32),
            pltpu.VMEM(field, F32),
            pltpu.SemaphoreType.DMA((3,)),
        ],
        name="ahead",
        us=0.1,
        mib=24,
        keep=range(5),
    )
    own, other, inner = call(
        functools.partial(back_kernel, tiles, points, slots),
        (plan, power, phi, far, second, tables, mover, *arrived),
        [SM] + [VK] * 4 + [HB] * 2 + [VM] * len(arrived),
        [half, half, (stack, BF16)],
        [
            pltpu.VMEM(tables.shape, BF16),
            pltpu.VMEM(mover.shape, BF16),
            pltpu.VMEM((points, points), BF16),
            pltpu.VMEM(field, F32),
            pltpu.VMEM((points, points), F32),
            pltpu.SemaphoreType.DMA((2,)),
        ],
        name="back",
        us=0.1,
        mib=24,
        keep=(2,),
    )
    pieces = [None] * layers
    pieces[1] = [own] + [turned(v, turn, tiles) for turn, v in ((1, other), (2, own), (3, other))]
    own, other, pair, mine, beyond, beside = call(
        functools.partial(last_kernel, tiles, points),
        (plan, inner, *probes, first, tables, kernel),
        [SM, VK, HB] + [VK] * 4 + [HB] * 2,
        [half, half, ((2, *half[0]), BF16)] + [((modes, *field), BF16)] * 2 + [((2, modes, *field), BF16)],
        [
            pltpu.VMEM(probe_modes.shape, F32),
            pltpu.VMEM(tables.shape, BF16),
            pltpu.VMEM(kernel.shape, F32),
            pltpu.VMEM(field, F32),
            pltpu.SemaphoreType.DMA((3,)),
        ],
        name="last",
        us=0.1,
        mib=24,
    )
    pieces[1], own, other, pair, beside = lax.optimization_barrier((pieces[1], own, other, pair, beside))
    pair = turned(pair, 2, tiles)
    pieces[0] = [own, turned(other, 1, tiles), pair, turned(pair, 1, tiles)]
    share = (groups // 2, modes, 2, points // groups, points)
    keep, send = call(
        spread_kernel,
        (plan, mine, beyond, turned(beside, 1, tiles)),
        [SM] + [VM] * 3,
        [((2, *share), F32), ((2, *share), BF16)],
        name="spread",
    )
    keep, send = call(
        fold_kernel,
        (keep, lax.ppermute(send, "pos", aside)),
        [VM] * 2,
        [(share, F32), (share, BF16)],
        name="fold",
    )
    own, *sends = call(
        gather_kernel,
        (keep, turned(send, 2, tiles)),
        [VM] * 2,
        [(share[1:], F32)] + [(share[1:], BF16)] * (groups // 2 - 1),
        name="gather",
    )
    came = [
        lax.ppermute(send, "pos", [(i, i ^ (2 * turn)) for i in range(groups)]) for turn, send in enumerate(sends, 1)
    ]
    (probe_grad,) = call(total_kernel, (own, *came), [VM] * (1 + len(came)), [(share[1:], F32)], name="total")

    block = (2, rows, points)
    keeps, swapped = [None] * layers, [None] * layers
    for layer in reversed(range(layers)):
        even, same, odd = call(
            functools.partial(place_kernel, tiles, points),
            (plan, *pieces[layer]),
            [SM] + [VM] * tiles,
            [((2, *block), BF16), ((2, *block), F32), ((2, *block), BF16)],
            [pltpu.VMEM((7, *block), F32)],
            name="place",
        )
        if layer:
            pass
        pairs = [(i, i ^ 2) for i in range(groups)]
        low_in = lax.ppermute(even, "pos", pairs)
        pairs = [(i, i + 2 if i // 2 % 2 else i - 2) for i in range(2, groups - 2)]
        high_in = lax.ppermute(odd, "pos", pairs)
        if layer:
            pieces[0], low_in = lax.optimization_barrier((pieces[0], low_in))
        keeps[layer], send = call(
            split_kernel,
            (plan, same, low_in, high_in),
            [SM] + [VM] * 3,
            [(block, F32), (block, BF16)],
            name="split",
        )
        swapped[layer] = lax.ppermute(send, "pos", [(i, i ^ 1) for i in range(groups)])
    extra = lax.cond(
        plan[3, 2] > 0,
        lambda p: distant_blocks(plan, p, tiles, points, groups),
        lambda p: jnp.zeros((layers, *block), BF16),
        pieces,
    )
    (object_grad,) = call(
        functools.partial(end_kernel, layers),
        (*keeps, *swapped, extra),
        [VM] * (2 * layers + 1),
        [((layers, *block), F32)],
        name="end",
    )
    return object_grad, probe_grad


def make_tables(points):
    counter = jnp.arange(points, dtype=jnp.int32)
    product = counter[:, None] * counter[None, :] % points
    angle = 2.0 * jnp.pi / points * product.astype(jnp.float32)
    factor = 1.0 / jnp.sqrt(jnp.float32(points))
    table_re = (jnp.cos(angle) * factor).astype(jnp.bfloat16)
    table_im = (-jnp.sin(angle) * factor).astype(jnp.bfloat16)
    shifted = ((counter + points // 2) % points - points // 2).astype(jnp.float32)
    phase = (
        jnp.pi
        * FRESNEL
        / points
        * (shifted[:, None] * shifted[:, None] + shifted[None, :] * shifted[None, :])
    )
    kernel = jnp.stack([jnp.cos(phase), -jnp.sin(phase)])
    return (table_re, table_im, kernel)


def times_complex(first, second):
    real_part = (
        first[..., 0, :, :] * second[..., 0, :, :] - first[..., 1, :, :] * second[..., 1, :, :]
    )
    imag_part = (
        first[..., 0, :, :] * second[..., 1, :, :] + first[..., 1, :, :] * second[..., 0, :, :]
    )
    return jnp.stack([real_part, imag_part], axis=-3)


def conjugate(values):
    return jnp.stack([values[..., 0, :, :], -values[..., 1, :, :]], axis=-3)


def transform_many(values, table_re, table_im):
    tables = jnp.stack([table_re, table_im])
    lowered = values.astype(jnp.bfloat16)
    first = jnp.einsum("gab,nmtbc->nmgtac", tables, lowered, preferred_element_type=jnp.float32)
    middle = jnp.stack(
        [first[:, :, 0, 0] - first[:, :, 1, 1], first[:, :, 0, 1] + first[:, :, 1, 0]], axis=2
    ).astype(jnp.bfloat16)
    second = jnp.einsum("nmtab,gbc->nmtgac", middle, tables, preferred_element_type=jnp.float32)
    return jnp.stack(
        [second[:, :, 0, 0] - second[:, :, 1, 1], second[:, :, 0, 1] + second[:, :, 1, 0]], axis=2
    )


def propagate_many(values, table_re, table_im, kernel):
    return transform_many(
        times_complex(transform_many(values, table_re, table_im), kernel), table_re, -table_im
    )


def window_anchor(place):
    zero_index = jnp.int32(0)
    return (zero_index, zero_index, place[0], place[1])


def on_device_by_mode(probe_modes, object_slices, amplitudes, scan_offsets, slot_counts):
    group = lax.axis_index("pos")
    groups = lax.axis_size("pos")
    tile_at = lax.axis_index("tile")
    strips = lax.axis_size("tile")
    slots = amplitudes.shape[0]
    points = amplitudes.shape[-1]
    layers = object_slices.shape[0]
    strip_rows = object_slices.shape[2]
    starts = jnp.cumsum(slot_counts) - slot_counts
    share = slots // 2
    wanted = jnp.arange(groups * share, dtype=jnp.int32)
    within = wanted - starts[group]
    usable = (within >= 0) & (within < slot_counts[group])
    picked = jnp.take(amplitudes, jnp.clip(within, 0, slots - 1), axis=0)
    outgoing = jnp.where(usable[:, None, None], picked, jnp.zeros_like(picked))
    arrived_rows = lax.all_to_all(outgoing, "pos", split_axis=0, concat_axis=0, tiled=True)
    mine = group * share + jnp.arange(share, dtype=jnp.int32)
    source = jnp.sum((starts[None, :] <= mine[:, None]).astype(jnp.int32), axis=1) - 1
    amplitude = jnp.take(arrived_rows, source * share + jnp.arange(share, dtype=jnp.int32), axis=0)
    places = jnp.take(scan_offsets, source * slots + mine - starts[source], axis=0)
    alive = jnp.ones((share,), jnp.float32)
    padded = jnp.pad(object_slices, ((0, 0), (0, 0), (points, points), (0, 0)))

    def cut_piece(place):
        local_row = jnp.clip(place[0] - tile_at * strip_rows + points, 0, strip_rows + points)
        shifted_place = jnp.stack([local_row, place[1]])
        return lax.dynamic_slice(padded, window_anchor(shifted_place), (layers, 2, points, points))

    pieces = jax.vmap(cut_piece)(places).astype(jnp.float32)
    windows = lax.psum(pieces.astype(jnp.bfloat16), "tile").astype(jnp.float32)
    table_re, table_im, kernel = make_tables(points)
    kernel_conj = conjugate(kernel)
    current = times_complex(probe_modes[None], windows[:, None, 0])
    layer_at = 1
    arrived = propagate_many(current, table_re, table_im, kernel)
    entering = [arrived]
    current = times_complex(arrived, windows[:, None, layer_at])
    far_field = transform_many(current, table_re, table_im)
    partial_power = jnp.sum(far_field * far_field, axis=(1, 2))
    power = lax.psum(partial_power.astype(jnp.bfloat16), "tile").astype(jnp.float32)
    ratio = (1.0 - amplitude.astype(jnp.float32) / jnp.sqrt(power + 1.0)) * alive[:, None, None]
    incoming = transform_many(ratio[:, None, None] * far_field, table_re, -table_im)
    object_terms = [None] * layers
    layer_at = 1
    object_terms[layer_at] = jnp.sum(
        times_complex(conjugate(entering[layer_at - 1]), incoming), axis=1
    )
    incoming = propagate_many(
        times_complex(conjugate(windows[:, None, layer_at]), incoming),
        table_re,
        table_im,
        kernel_conj,
    )
    object_terms[0] = jnp.sum(times_complex(conjugate(probe_modes[None]), incoming), axis=1)
    probe_term = jnp.sum(times_complex(conjugate(windows[:, None, 0]), incoming), axis=0)
    slot_grads = jnp.stack(object_terms, axis=1)
    canvas = jnp.zeros((layers, 2, strip_rows * strips, object_slices.shape[3]), jnp.float32)

    def deposit(canvas, packed):
        place, term = packed
        anchor = window_anchor(place)
        current_part = lax.dynamic_slice(canvas, anchor, term.shape)
        return (lax.dynamic_update_slice(canvas, current_part + term, anchor), None)

    canvas, unused = lax.scan(deposit, canvas, (places, slot_grads))
    column_part = lax.psum_scatter(
        canvas.astype(jnp.bfloat16), "pos", scatter_dimension=3, tiled=True
    )
    object_grad = lax.psum_scatter(column_part, "tile", scatter_dimension=2, tiled=True).astype(
        jnp.float32
    )
    probe_grad = lax.psum_scatter(
        probe_term.astype(jnp.bfloat16), "pos", scatter_dimension=2, tiled=True
    ).astype(jnp.float32)
    return (object_grad, probe_grad)


def solution(mesh):
    in_specs = (
        P("tile", None, None, None),
        P(None, None, "tile", None),
        P("pos", None, None),
        P(),
        P(),
    )
    out_specs = (P(None, None, "tile", "pos"), P("tile", None, "pos", None))
    by_slot = mesh.shape["tile"] == 4 and mesh.shape["pos"] == 8
    return jax.shard_map(
        on_device_by_slot if by_slot else on_device_by_mode,
        mesh=mesh,
        in_specs=in_specs,
        out_specs=out_specs,
        check_vma=False,
    )
```

```python
import functools

import jax
import jax.numpy as jnp
import ml_dtypes
import numpy as np
from jax import lax
from jax.experimental import pallas as pl
from jax.experimental.pallas import tpu as pltpu
from jax.sharding import PartitionSpec as P

FRESNEL = 0.37
BF16 = jnp.bfloat16
F32 = jnp.float32


def split_tables(points):
    half = points // 2
    counter = np.arange(points)
    angle = (2.0 * np.pi / points * (counter[:, None] * counter[None, :] % points)).astype(np.float32)
    factor = np.float32(1.0) / np.sqrt(np.float32(points))
    table_re = np.cos(angle) * factor
    table_im = -np.sin(angle) * factor

    def stacked(rows):
        re, im = table_re[rows, :half], table_im[rows, :half]
        return np.block([[re, -im], [im, re]]).astype(ml_dtypes.bfloat16)

    even, odd = stacked(slice(0, None, 2)), stacked(slice(1, None, 2))
    tables = np.stack([even, odd, even.T, odd.T])
    order = np.concatenate([counter[0::2], counter[1::2]])
    shifted = ((order + half) % points - half).astype(np.float64)
    phase = np.pi * FRESNEL / points * (shifted[:, None] ** 2 + shifted[None, :] ** 2)
    kernel = np.stack([np.cos(phase), -np.sin(phase)]).astype(np.float32)
    mover = np.zeros((points, points), np.float32)
    mover[counter, order] = 1.0
    mover = np.stack([mover, mover.T]).astype(ml_dtypes.bfloat16)
    return tables, kernel, mover


def dot(a, b):
    return jnp.dot(a, b, preferred_element_type=F32)


def fold_rows(re, im):
    half = re.shape[0] // 2
    top = jnp.concatenate([re[:half], im[:half]], axis=0)
    bottom = jnp.concatenate([re[half:], im[half:]], axis=0)
    return (top + bottom).astype(BF16), (top - bottom).astype(BF16)


def join_parts(values, axis):
    return jnp.concatenate(values, axis=axis)


def forward_folded(folded, tables):
    half = folded[0][0].shape[0] // 2
    evens = [dot(tables[0], even) for even, _ in folded]
    odds = [dot(tables[1], odd) for _, odd in folded]
    lanes = []
    for even, odd in zip(evens, odds):
        re = join_parts([even[:half], odd[:half]], 0)
        im = join_parts([even[half:], odd[half:]], 0)
        left = join_parts([re[:, :half], im[:, :half]], 1)
        right = join_parts([re[:, half:], im[:, half:]], 1)
        lanes.append(((left + right).astype(BF16), (left - right).astype(BF16)))
    evens = [dot(even, tables[2]) for even, _ in lanes]
    odds = [dot(odd, tables[3]) for _, odd in lanes]
    return [
        (join_parts([even[:, :half], odd[:, :half]], 1), join_parts([even[:, half:], odd[:, half:]], 1))
        for even, odd in zip(evens, odds)
    ]


def inverse(fields, tables):
    half = fields[0][0].shape[0] // 2
    low = [(re.astype(BF16), im.astype(BF16)) for re, im in fields]
    evens = [dot(tables[2], join_parts([re[:half], im[:half]], 0)) for re, im in low]
    odds = [dot(tables[3], join_parts([re[half:], im[half:]], 0)) for re, im in low]
    lanes = []
    for even, odd in zip(evens, odds):
        total, rest = (even + odd).astype(BF16), (even - odd).astype(BF16)
        re = join_parts([total[:half], rest[:half]], 0)
        im = join_parts([total[half:], rest[half:]], 0)
        lanes.append((join_parts([re[:, :half], im[:, :half]], 1), join_parts([re[:, half:], im[:, half:]], 1)))
    evens = [dot(even, tables[0]) for even, _ in lanes]
    odds = [dot(odd, tables[1]) for _, odd in lanes]
    out = []
    for even, odd in zip(evens, odds):
        total, rest = even + odd, even - odd
        re = join_parts([total[:, :half], rest[:, :half]], 1)
        im = join_parts([total[:, half:], rest[:, half:]], 1)
        out.append((re, im))
    return out


def times(a_re, a_im, b_re, b_im):
    return a_re * b_re - a_im * b_im, a_re * b_im + a_im * b_re


def conj_times(a_re, a_im, b_re, b_im):
    return a_re * b_re + a_im * b_im, a_re * b_im - a_im * b_re


def load_complex(ref, *lead):
    return ref[(*lead, 0)].astype(F32), ref[(*lead, 1)].astype(F32)


VM = pl.BlockSpec(memory_space=pltpu.VMEM)
SM = pl.BlockSpec(memory_space=pltpu.SMEM)
HB = pl.BlockSpec(memory_space=pltpu.HBM)
VK = object()


def call(body, inputs, specs, outs, scratch=(), out_specs=None, name=None, us=0.1, mib=8, keep=()):
    return pl.pallas_call(
        body,
        out_shape=[
            pltpu.VMEM(shape, dtype) if at in keep else jax.ShapeDtypeStruct(shape, dtype)
            for at, (shape, dtype) in enumerate(outs)
        ],
        in_specs=[VM if spec is VK else spec for spec in specs],
        out_specs=[VM] * len(outs) if out_specs is None else out_specs,
        scratch_shapes=list(scratch),
        compiler_params=pltpu.CompilerParams(vmem_limit_bytes=mib * 1024 * 1024),
        cost_estimate=pl.CostEstimate(flops=int(us * 1e9), bytes_accessed=int(us * 3e6), transcendentals=0),
        name=name,
    )(
        *(
            pltpu.with_memory_space_constraint(value, pltpu.VMEM) if spec is VK else value
            for value, spec in zip(inputs, specs)
        )
    )


def fetch(sources, targets, sems):
    copies = [pltpu.make_async_copy(s, t, sems.at[at]) for at, (s, t) in enumerate(zip(sources, targets))]
    for copy in copies:
        copy.start()
    return copies


def slot_at(plan, tiles, turn):
    place = plan[3, 0] * tiles + (plan[3, 1] ^ turn)
    return plan[1, place], plan[2, place]


def first_kernel(groups, tiles, points, counts, offsets, strip_far, amplitudes_far, *refs):
    strips = refs[:tiles]
    same, other_x, plan_out, plan, strip, amplitudes, sems = refs[tiles:]
    layers, rows = strip.shape[0], strip.shape[2]
    slots = amplitudes.shape[0]
    n = offsets.shape[0]
    strip_copy = pltpu.make_async_copy(strip_far, strip, sems.at[1])
    strip_copy.start()
    amplitude_copy = pltpu.make_async_copy(amplitudes_far, amplitudes, sems.at[2])
    amplitude_copy.start()
    pos, tile = lax.axis_index("pos"), lax.axis_index("tile")
    width = plan_out.shape[1]

    number = lax.broadcasted_iota(jnp.int32, (n, 1), 0)
    live = jnp.zeros((n, 1), jnp.int32)
    for group in range(groups):
        live += jnp.where((number >= group * slots) & (number < group * slots + counts[group]), 1, 0)
    row, col = offsets[:, 0:1].astype(F32), offsets[:, 1:2].astype(F32)
    number = number.astype(F32)
    key = jnp.where(live > 0, col, float(1 << 12)) * n + number
    square = (n, n)
    eye = lax.broadcasted_iota(jnp.int32, square, 0) == lax.broadcasted_iota(jnp.int32, square, 1)
    across = jnp.sum(jnp.where(eye, key, 0.0), axis=0, keepdims=True)
    rank = jnp.sum(jnp.where(across < key, 1.0, 0.0), axis=1, keepdims=True).astype(jnp.int32)
    here = lax.broadcasted_iota(jnp.int32, (n, width), 1) == rank
    chosen = [
        jnp.sum(jnp.where(here, value, 0.0), axis=0, keepdims=True).astype(jnp.int32)
        for value in (number, row, col)
    ]
    lane = lax.broadcasted_iota(jnp.int32, (1, width), 1)
    outer = 2 * points
    lowest = jnp.maximum(sum(jnp.where(lane >= i * 2 * tiles, 1, 0) for i in range(1, groups // 2)) - 1, 0)
    far = (chosen[2] < lowest * outer) | (chosen[2] + points > (lowest + jnp.where(lane < 2 * tiles, 2, 3)) * outer)
    distant = jnp.max(jnp.where(far & (lane < groups * slots // 2), 1.0, 0.0), axis=1, keepdims=True)
    for at, value in enumerate(chosen):
        plan_out[at : at + 1, :] = value
    plan_out[3:4, :] = jnp.where(
        lane == 0, pos, jnp.where(lane == 1, tile, jnp.where(lane == 2, distant.astype(jnp.int32), 0))
    )
    plan_out[4:8, :] = jnp.zeros((4, width), jnp.int32)
    copy = pltpu.make_async_copy(plan_out, plan, sems.at[0])
    copy.start()
    copy.wait()
    strip_copy.wait()

    blocks = strip.shape[-1] // points
    lane = lax.broadcasted_iota(jnp.int32, (rows, points), 1)
    for turn in range(tiles):
        _, col = slot_at(plan, tiles, turn)
        block = col // points
        later = jnp.minimum(block + 1, blocks - 1)
        keep = lane >= col % points
        for layer in range(layers):
            for part in range(2):
                here = strip[layer, part, :, pl.ds(pl.multiple_of(block * points, points), points)]
                there = strip[layer, part, :, pl.ds(pl.multiple_of(later * points, points), points)]
                strips[turn][layer, part] = jnp.where(
                    keep, here.astype(F32), there.astype(F32)
                ).astype(BF16)
    amplitude_copy.wait()
    for turn in range(groups // 2):
        for flip, out, at in ((0, same, turn), (1, other_x, turn)):
            slot = plan[0, (pos ^ (2 * turn + flip)) * tiles + tile]

            @pl.when(slot // slots == pos)
            def _(out=out, at=at, slot=slot):
                out[at] = amplitudes[slot % slots]


def merge_kernel(tiles, slots, turns, plan, same, came, *outs):
    pos, tile = plan[3, 0], plan[3, 1]
    for at, (turn, out) in enumerate(zip(turns, outs)):
        source = plan[0, (pos ^ (2 * turn)) * tiles + tile] // slots

        @pl.when(source == pos)
        def _(turn=turn, out=out):
            out[...] = same[turn]

        @pl.when(source == (pos ^ 1))
        def _(at=at, out=out):
            out[...] = came[at]


def join(tiles, points, plan, strips, layer, whole, out):
    own, one, two, three = strips
    rows = own.shape[2]
    row, col = slot_at(plan, tiles, 0)
    core, up = plan[3, 1] % 2, plan[3, 1] // 2
    sub = lax.broadcasted_iota(jnp.int32, (rows, points), 0)
    for near, far, at in ((own, two, core), (one, three, 1 - core)):
        low = jnp.where(sub + at * rows >= row, 0, 1)
        for part in range(2):
            whole[part, pl.ds(pl.multiple_of(at * rows, rows), rows)] = jnp.where(
                low == up, near[layer, part].astype(F32), far[layer, part].astype(F32)
            )
    for part in range(2):
        value = pltpu.roll(whole[part], (points - row % points) % points, 0)
        out[part] = pltpu.roll(value, (points - col % points) % points, 1).astype(BF16)


def forward(probes, first, second, tables, kernel, phi, far):
    modes = probes[0].shape[0]
    fields = []
    for probe in probes:
        for mode in range(modes):
            fields.append(fold_rows(*times(*load_complex(probe, mode), *load_complex(first))))
    fields = forward_folded(fields, tables)
    fields = inverse([times(re, im, kernel[0], kernel[1]) for re, im in fields], tables)
    folded = []
    for at, (re, im) in enumerate(fields):
        phi[at, 0], phi[at, 1] = re.astype(BF16), im.astype(BF16)
        folded.append(fold_rows(*times(re, im, *load_complex(second))))
    fields = forward_folded(folded, tables)
    power = None
    for at, (re, im) in enumerate(fields):
        far[at, 0], far[at, 1] = re.astype(BF16), im.astype(BF16)
        square = re * re + im * im
        power = square if power is None else power + square
    return power


def put_by_residue(plan, tiles, points, total, own, other):
    row, col = slot_at(plan, tiles, 0)
    core = plan[3, 1] % 2
    rows = points // 2
    for part in range(2):
        total[part] = pltpu.roll(pltpu.roll(total[part], row % points, 0), col % points, 1)
    for out, at in ((own, core), (other, 1 - core)):
        for part in range(2):
            out[part] = total[part, pl.ds(pl.multiple_of(at * rows, rows), rows)].astype(BF16)


def ahead_kernel(tiles, points, plan, *refs):
    strips, near, beside, across, diagonal, tables_far, kernel_far = refs[:4], *refs[4:10]
    first, second, phi, far, power = refs[10:15]
    mine, tables, kernel, whole, sems = refs[15:]
    copies = fetch((near, tables_far, kernel_far), (mine, tables, kernel), sems)
    join(tiles, points, plan, strips, 0, whole, first)
    join(tiles, points, plan, strips, 1, whole, second)
    for copy in copies:
        copy.wait()
    size = phi.shape[0] // 2
    power[...] = forward((mine, beside), first, second, tables, kernel, phi.at[:size], far.at[:size])
    power[...] += forward((across, diagonal), first, second, tables, kernel, phi.at[size:], far.at[size:])


def back_kernel(tiles, points, slots, plan, *refs):
    power, phi, far, second, tables_far, mover_far = refs[:6]
    arrived = refs[6:10]
    own, other, inner = refs[10:13]
    tables, mover, amplitude, total, ratio, sems = refs[13:]
    copies = fetch((mover_far, tables_far), (mover, tables), sems)
    source = plan[0, plan[3, 0] * tiles + plan[3, 1]] // slots
    for turn, ref in enumerate(arrived):

        @pl.when(((source ^ plan[3, 0]) >> 1) == turn)
        def _(ref=ref):
            amplitude[...] = ref[...]

    for copy in copies:
        copy.wait()
    measured = dot(dot(mover[0], amplitude[...]).astype(BF16), mover[1])
    ratio[...] = 1.0 - measured / jnp.sqrt(power[...] + 1.0)
    total[...] = jnp.zeros_like(total)
    size = phi.shape[0]
    for start in (0,):
        fields = []
        for at in range(start, start + size):
            re, im = load_complex(far, at)
            fields.append((re * ratio[...], im * ratio[...]))
        fields = inverse(fields, tables)
        for at, (re, im) in enumerate(fields, start):
            grad_re, grad_im = conj_times(*load_complex(phi, at), re, im)
            total[0] += grad_re
            total[1] += grad_im
            inner[at, 0], inner[at, 1] = fold_rows(*conj_times(*load_complex(second), re, im))
    put_by_residue(plan, tiles, points, total, own, other)


def last_kernel(tiles, points, plan, *refs):
    inner, near, beside, across, diagonal, first, tables_far, kernel_far = refs[:8]
    own, other, pair, near_grad, beyond_grad, beside_grad = refs[8:14]
    mine, tables, kernel, total, sems = refs[14:]
    copies = fetch((tables_far, kernel_far, near), (tables, kernel, mine), sems)
    modes = mine.shape[0]
    probes = (mine, beside, across, diagonal)
    grads = (near_grad, beside_grad.at[0], beyond_grad, beside_grad.at[1])
    total[...] = jnp.zeros_like(total)
    for copy in copies:
        copy.wait()
    for start in range(0, tiles, tiles):
        which = [(turn, mode) for turn in range(start, start + tiles) for mode in range(modes)]
        fields = forward_folded([(inner[t * modes + m, 0], inner[t * modes + m, 1]) for t, m in which], tables)
        fields = inverse([conj_times(kernel[0], kernel[1], re, im) for re, im in fields], tables)
        for (turn, mode), (re, im) in zip(which, fields):
            grad_re, grad_im = conj_times(*load_complex(probes[turn], mode), re, im)
            total[0] += grad_re
            total[1] += grad_im
            re, im = conj_times(*load_complex(first), re, im)
            grads[turn][mode, 0], grads[turn][mode, 1] = re.astype(BF16), im.astype(BF16)
    put_by_residue(plan, tiles, points, total, own, other)
    pair[0] = own[...]
    pair[1] = other[...]


def piece_of(pieces, turn):
    piece = pieces[turn]
    if len(piece.shape) == 3:
        return piece
    return piece[turn - 2]


def place_kernel(tiles, points, plan, *refs):
    pieces, (even, same, odd, canvas) = refs[:tiles], refs[tiles:]
    rows = pieces[0].shape[1]
    core, up = plan[3, 1] % 2, plan[3, 1] // 2
    base = plan[3, 0] // 2 * 2 - 2
    sub = lax.broadcasted_iota(jnp.int32, (rows, points), 0) + core * rows
    lane = lax.broadcasted_iota(jnp.int32, (rows, points), 1)
    canvas[...] = jnp.zeros_like(canvas)
    for turn in range(tiles):
        row, col = slot_at(plan, tiles, turn)
        mine = jnp.where(sub >= row, 0, 1) == up
        early = lane >= col % points
        for part in range(2):
            value = jnp.where(mine, piece_of(pieces, turn)[part].astype(F32), 0.0)
            for step, keep in ((0, early), (1, ~early)):
                at = col // points + step - base
                at = jnp.where((at >= 0) & (at < 6), at, 6)
                canvas[at, part] += jnp.where(keep, value, 0.0)
    same[...] = canvas[2:4]
    up_first = plan[3, 0] // 2 % 2 == 0
    for out, at in ((even, jnp.where(up_first, 4, 0)), (odd, jnp.where(up_first, 0, 4))):
        out[...] = canvas[pl.ds(at, 2)].astype(BF16)


def split_kernel(plan, same, low, high, keep, send):
    x_at = plan[3, 0] % 2
    keep[...] = same[x_at] + low[x_at].astype(F32) + high[x_at].astype(F32)
    other = same[1 - x_at] + low[1 - x_at].astype(F32) + high[1 - x_at].astype(F32)
    send[...] = other.astype(BF16)


def end_kernel(layers, *refs):
    extra, out = refs[-2:]
    for layer in range(layers):
        out[layer] = refs[layer][...] + refs[layers + layer][...].astype(F32) + extra[layer].astype(F32)


def spread_kernel(plan, mine, beyond, came, keep, send):
    pos = plan[3, 0]
    rows = keep.shape[-2]
    for which, near in enumerate((mine, beyond)):
        for turn in range(keep.shape[1]):
            for flip in range(2):
                at = pl.ds(pl.multiple_of((pos ^ (2 * turn + flip)) * rows, rows), rows)
                total = near[:, :, at].astype(F32) + came[which, :, :, at].astype(F32)
                if flip:
                    send[which, turn] = total.astype(BF16)
                else:
                    keep[which, turn] = total


def fold_kernel(near, came, keep, send):
    keep[...] = near[0] + came[0].astype(F32)
    send[...] = (near[1] + came[1].astype(F32)).astype(BF16)


def gather_kernel(near, came, own, *sends):
    own[...] = near[0] + came[0].astype(F32)
    for turn, send in enumerate(sends, 1):
        send[...] = (near[turn] + came[turn].astype(F32)).astype(BF16)


def total_kernel(*refs):
    total = refs[0][...]
    for ref in refs[1:-1]:
        total = total + ref[...].astype(F32)
    refs[-1][...] = total


def turned(value, turn, tiles):
    return lax.ppermute(value, "tile", [(i, i ^ turn) for i in range(tiles)])


def distant_blocks(plan, pieces, tiles, points, groups):
    rows = pieces[0][0].shape[1]
    pos, tile = plan[3, 0], plan[3, 1]
    sub = (jnp.arange(rows, dtype=jnp.int32) + tile % 2 * rows)[:, None]
    lane = jnp.arange(points, dtype=jnp.int32)[None, :]
    block = jnp.arange(groups, dtype=jnp.int32)
    outside = jnp.abs(block // 2 - pos // 2) > 1
    canvas = 0.0
    for turn in range(tiles):
        place = pos * tiles + (tile ^ turn)
        row, col = jnp.take(plan[1], place), jnp.take(plan[2], place)
        mine = jnp.where(sub >= row, 0, 1) == tile // 2
        target = col // points + jnp.where(lane >= col % points, 0, 1)
        keep = outside[:, None, None] & mine[None] & (target[None] == block[:, None, None])
        value = jnp.stack([piece_of(layer, turn) for layer in pieces]).astype(F32)
        canvas = canvas + jnp.where(keep[:, None, None], value[None], 0.0)
    shares = lax.all_to_all(canvas.astype(BF16), "pos", split_axis=0, concat_axis=0, tiled=True)
    return jnp.sum(shares.astype(F32), axis=0).astype(BF16)


def on_device_by_slot(probe_modes, object_slices, amplitudes, scan_offsets, slot_counts):
    groups, tiles = lax.axis_size("pos"), lax.axis_size("tile")
    slots, points = amplitudes.shape[0], amplitudes.shape[-1]
    layers, rows = object_slices.shape[0], object_slices.shape[2]
    modes = probe_modes.shape[0]
    tables, kernel, mover = (jnp.asarray(t) for t in split_tables(points))
    field = (2, points, points)

    low = probe_modes.astype(BF16)
    low, scan_offsets = lax.optimization_barrier((low, scan_offsets))
    across = turned(low, 2, tiles)
    beside = turned(low, 1, tiles)
    shot = (points, points)
    outs = call(
        functools.partial(first_kernel, groups, tiles, points),
        (slot_counts, scan_offsets, object_slices, amplitudes),
        [SM, VM, HB, HB],
        [((layers, 2, rows, points), BF16)] * tiles
        + [((groups // 2, *shot), BF16)] * 2
        + [((8, 128), jnp.int32)],
        [
            pltpu.SMEM((8, 128), jnp.int32),
            pltpu.VMEM(object_slices.shape, BF16),
            pltpu.VMEM(amplitudes.shape, BF16),
            pltpu.SemaphoreType.DMA((3,)),
        ],
        name="first",
        us=0.1,
        mib=16,
    )
    (*cut, same, far, plan) = outs
    across, cut = lax.optimization_barrier((across, cut))
    aside = [(i, i ^ 1) for i in range(groups)]
    merged = call(
        functools.partial(merge_kernel, tiles, slots, range(groups // 2)),
        (plan, same, lax.ppermute(far, "pos", aside)),
        [SM, VM, VM],
        [(shot, BF16)] * (groups // 2),
        name="merge",
    )
    arrived = [merged[0]] + [
        lax.ppermute(merged[turn], "pos", [(i, i ^ (2 * turn)) for i in range(groups)])
        for turn in range(1, groups // 2)
    ]
    strips = [cut[0]] + [turned(cut[turn], turn, tiles) for turn in range(1, tiles)]
    probes = [probe_modes, beside, across, turned(across, 1, tiles)]
    half = ((2, points // 2, points), BF16)
    stack = (tiles * modes, *field)
    first, second, phi, far, power = call(
        functools.partial(ahead_kernel, tiles, points),
        (plan, *strips, *probes, tables, kernel),
        [SM] + [VK] * tiles + [HB] + [VK] * 3 + [HB] * 2,
        [(field, BF16), (field, BF16), (stack, BF16), (stack, BF16), ((points, points), F32)],
        [
            pltpu.VMEM(probe_modes.shape, F32),
            pltpu.VMEM(tables.shape, BF16),
            pltpu.VMEM(kernel.shape, F32),
            pltpu.VMEM(field, F32),
            pltpu.SemaphoreType.DMA((3,)),
        ],
        name="ahead",
        us=0.1,
        mib=24,
        keep=range(5),
    )
    own, other, inner = call(
        functools.partial(back_kernel, tiles, points, slots),
        (plan, power, phi, far, second, tables, mover, *arrived),
        [SM] + [VK] * 4 + [HB] * 2 + [VM] * len(arrived),
        [half, half, (stack, BF16)],
        [
            pltpu.VMEM(tables.shape, BF16),
            pltpu.VMEM(mover.shape, BF16),
            pltpu.VMEM((points, points), BF16),
            pltpu.VMEM(field, F32),
            pltpu.VMEM((points, points), F32),
            pltpu.SemaphoreType.DMA((2,)),
        ],
        name="back",
        us=0.1,
        mib=24,
        keep=(2,),
    )
    pieces = [None] * layers
    pieces[1] = [own] + [turned(v, turn, tiles) for turn, v in ((1, other), (2, own), (3, other))]
    own, other, pair, mine, beyond, beside = call(
        functools.partial(last_kernel, tiles, points),
        (plan, inner, *probes, first, tables, kernel),
        [SM, VK, HB] + [VK] * 4 + [HB] * 2,
        [half, half, ((2, *half[0]), BF16)] + [((modes, *field), BF16)] * 2 + [((2, modes, *field), BF16)],
        [
            pltpu.VMEM(probe_modes.shape, F32),
            pltpu.VMEM(tables.shape, BF16),
            pltpu.VMEM(kernel.shape, F32),
            pltpu.VMEM(field, F32),
            pltpu.SemaphoreType.DMA((3,)),
        ],
        name="last",
        us=0.1,
        mib=24,
    )
    pieces[1], beside = lax.optimization_barrier((pieces[1], beside))
    pair = turned(pair, 2, tiles)
    pieces[0] = [own, turned(other, 1, tiles), pair, turned(pair, 1, tiles)]
    share = (groups // 2, modes, 2, points // groups, points)
    keep, send = call(
        spread_kernel,
        (plan, mine, beyond, turned(beside, 1, tiles)),
        [SM] + [VM] * 3,
        [((2, *share), F32), ((2, *share), BF16)],
        name="spread",
    )
    keep, send = call(
        fold_kernel,
        (keep, lax.ppermute(send, "pos", aside)),
        [VM] * 2,
        [(share, F32), (share, BF16)],
        name="fold",
    )
    own, *sends = call(
        gather_kernel,
        (keep, turned(send, 2, tiles)),
        [VM] * 2,
        [(share[1:], F32)] + [(share[1:], BF16)] * (groups // 2 - 1),
        name="gather",
    )
    came = [
        lax.ppermute(send, "pos", [(i, i ^ (2 * turn)) for i in range(groups)]) for turn, send in enumerate(sends, 1)
    ]
    (probe_grad,) = call(total_kernel, (own, *came), [VM] * (1 + len(came)), [(share[1:], F32)], name="total")

    block = (2, rows, points)
    keeps, swapped = [None] * layers, [None] * layers
    for layer in reversed(range(layers)):
        even, same, odd = call(
            functools.partial(place_kernel, tiles, points),
            (plan, *pieces[layer]),
            [SM] + [VM] * tiles,
            [((2, *block), BF16), ((2, *block), F32), ((2, *block), BF16)],
            [pltpu.VMEM((7, *block), F32)],
            name="place",
        )
        if layer:
            pass
        pairs = [(i, i ^ 2) for i in range(groups)]
        low_in = lax.ppermute(even, "pos", pairs)
        pairs = [(i, i + 2 if i // 2 % 2 else i - 2) for i in range(2, groups - 2)]
        high_in = lax.ppermute(odd, "pos", pairs)
        if layer:
            pieces[0], low_in = lax.optimization_barrier((pieces[0], low_in))
        keeps[layer], send = call(
            split_kernel,
            (plan, same, low_in, high_in),
            [SM] + [VM] * 3,
            [(block, F32), (block, BF16)],
            name="split",
        )
        swapped[layer] = lax.ppermute(send, "pos", [(i, i ^ 1) for i in range(groups)])
    extra = lax.cond(
        plan[3, 2] > 0,
        lambda p: distant_blocks(plan, p, tiles, points, groups),
        lambda p: jnp.zeros((layers, *block), BF16),
        pieces,
    )
    (object_grad,) = call(
        functools.partial(end_kernel, layers),
        (*keeps, *swapped, extra),
        [VM] * (2 * layers + 1),
        [((layers, *block), F32)],
        name="end",
    )
    return object_grad, probe_grad


def make_tables(points):
    counter = jnp.arange(points, dtype=jnp.int32)
    product = counter[:, None] * counter[None, :] % points
    angle = 2.0 * jnp.pi / points * product.astype(jnp.float32)
    factor = 1.0 / jnp.sqrt(jnp.float32(points))
    table_re = (jnp.cos(angle) * factor).astype(jnp.bfloat16)
    table_im = (-jnp.sin(angle) * factor).astype(jnp.bfloat16)
    shifted = ((counter + points // 2) % points - points // 2).astype(jnp.float32)
    phase = (
        jnp.pi
        * FRESNEL
        / points
        * (shifted[:, None] * shifted[:, None] + shifted[None, :] * shifted[None, :])
    )
    kernel = jnp.stack([jnp.cos(phase), -jnp.sin(phase)])
    return (table_re, table_im, kernel)


def times_complex(first, second):
    real_part = (
        first[..., 0, :, :] * second[..., 0, :, :] - first[..., 1, :, :] * second[..., 1, :, :]
    )
    imag_part = (
        first[..., 0, :, :] * second[..., 1, :, :] + first[..., 1, :, :] * second[..., 0, :, :]
    )
    return jnp.stack([real_part, imag_part], axis=-3)


def conjugate(values):
    return jnp.stack([values[..., 0, :, :], -values[..., 1, :, :]], axis=-3)


def transform_many(values, table_re, table_im):
    tables = jnp.stack([table_re, table_im])
    lowered = values.astype(jnp.bfloat16)
    first = jnp.einsum("gab,nmtbc->nmgtac", tables, lowered, preferred_element_type=jnp.float32)
    middle = jnp.stack(
        [first[:, :, 0, 0] - first[:, :, 1, 1], first[:, :, 0, 1] + first[:, :, 1, 0]], axis=2
    ).astype(jnp.bfloat16)
    second = jnp.einsum("nmtab,gbc->nmtgac", middle, tables, preferred_element_type=jnp.float32)
    return jnp.stack(
        [second[:, :, 0, 0] - second[:, :, 1, 1], second[:, :, 0, 1] + second[:, :, 1, 0]], axis=2
    )


def propagate_many(values, table_re, table_im, kernel):
    return transform_many(
        times_complex(transform_many(values, table_re, table_im), kernel), table_re, -table_im
    )


def window_anchor(place):
    zero_index = jnp.int32(0)
    return (zero_index, zero_index, place[0], place[1])


def on_device_by_mode(probe_modes, object_slices, amplitudes, scan_offsets, slot_counts):
    group = lax.axis_index("pos")
    groups = lax.axis_size("pos")
    tile_at = lax.axis_index("tile")
    strips = lax.axis_size("tile")
    slots = amplitudes.shape[0]
    points = amplitudes.shape[-1]
    layers = object_slices.shape[0]
    strip_rows = object_slices.shape[2]
    starts = jnp.cumsum(slot_counts) - slot_counts
    share = slots // 2
    wanted = jnp.arange(groups * share, dtype=jnp.int32)
    within = wanted - starts[group]
    usable = (within >= 0) & (within < slot_counts[group])
    picked = jnp.take(amplitudes, jnp.clip(within, 0, slots - 1), axis=0)
    outgoing = jnp.where(usable[:, None, None], picked, jnp.zeros_like(picked))
    arrived_rows = lax.all_to_all(outgoing, "pos", split_axis=0, concat_axis=0, tiled=True)
    mine = group * share + jnp.arange(share, dtype=jnp.int32)
    source = jnp.sum((starts[None, :] <= mine[:, None]).astype(jnp.int32), axis=1) - 1
    amplitude = jnp.take(arrived_rows, source * share + jnp.arange(share, dtype=jnp.int32), axis=0)
    places = jnp.take(scan_offsets, source * slots + mine - starts[source], axis=0)
    alive = jnp.ones((share,), jnp.float32)
    padded = jnp.pad(object_slices, ((0, 0), (0, 0), (points, points), (0, 0)))

    def cut_piece(place):
        local_row = jnp.clip(place[0] - tile_at * strip_rows + points, 0, strip_rows + points)
        shifted_place = jnp.stack([local_row, place[1]])
        return lax.dynamic_slice(padded, window_anchor(shifted_place), (layers, 2, points, points))

    pieces = jax.vmap(cut_piece)(places).astype(jnp.float32)
    windows = lax.psum(pieces.astype(jnp.bfloat16), "tile").astype(jnp.float32)
    table_re, table_im, kernel = make_tables(points)
    kernel_conj = conjugate(kernel)
    current = times_complex(probe_modes[None], windows[:, None, 0])
    layer_at = 1
    arrived = propagate_many(current, table_re, table_im, kernel)
    entering = [arrived]
    current = times_complex(arrived, windows[:, None, layer_at])
    far_field = transform_many(current, table_re, table_im)
    partial_power = jnp.sum(far_field * far_field, axis=(1, 2))
    power = lax.psum(partial_power.astype(jnp.bfloat16), "tile").astype(jnp.float32)
    ratio = (1.0 - amplitude.astype(jnp.float32) / jnp.sqrt(power + 1.0)) * alive[:, None, None]
    incoming = transform_many(ratio[:, None, None] * far_field, table_re, -table_im)
    object_terms = [None] * layers
    layer_at = 1
    object_terms[layer_at] = jnp.sum(
        times_complex(conjugate(entering[layer_at - 1]), incoming), axis=1
    )
    incoming = propagate_many(
        times_complex(conjugate(windows[:, None, layer_at]), incoming),
        table_re,
        table_im,
        kernel_conj,
    )
    object_terms[0] = jnp.sum(times_complex(conjugate(probe_modes[None]), incoming), axis=1)
    probe_term = jnp.sum(times_complex(conjugate(windows[:, None, 0]), incoming), axis=0)
    slot_grads = jnp.stack(object_terms, axis=1)
    canvas = jnp.zeros((layers, 2, strip_rows * strips, object_slices.shape[3]), jnp.float32)

    def deposit(canvas, packed):
        place, term = packed
        anchor = window_anchor(place)
        current_part = lax.dynamic_slice(canvas, anchor, term.shape)
        return (lax.dynamic_update_slice(canvas, current_part + term, anchor), None)

    canvas, unused = lax.scan(deposit, canvas, (places, slot_grads))
    column_part = lax.psum_scatter(
        canvas.astype(jnp.bfloat16), "pos", scatter_dimension=3, tiled=True
    )
    object_grad = lax.psum_scatter(column_part, "tile", scatter_dimension=2, tiled=True).astype(
        jnp.float32
    )
    probe_grad = lax.psum_scatter(
        probe_term.astype(jnp.bfloat16), "pos", scatter_dimension=2, tiled=True
    ).astype(jnp.float32)
    return (object_grad, probe_grad)


def solution(mesh):
    in_specs = (
        P("tile", None, None, None),
        P(None, None, "tile", None),
        P("pos", None, None),
        P(),
        P(),
    )
    out_specs = (P(None, None, "tile", "pos"), P("tile", None, "pos", None))
    by_slot = mesh.shape["tile"] == 4 and mesh.shape["pos"] == 8
    return jax.shard_map(
        on_device_by_slot if by_slot else on_device_by_mode,
        mesh=mesh,
        in_specs=in_specs,
        out_specs=out_specs,
        check_vma=False,
    )
```
